512 devices in a mesh: space: 128 (over y, z, core), scene: 4 (over x).
Axes of the slice: x: 4, y: 8, z: 8, core: 2. Of those that a mesh axis runs over, the one named last changes fastest.
Arguments:
- features: bfloat16 [4, 16384, 256], P('scene', 'space'), may hold values from -6 to 6
- cotangent: bfloat16 [4, 16384, 128], P('scene', 'space'), may hold values from -6 to 6
- relu_mask: int32 [4, 16384, 128], P('scene', 'space'), may hold values 0 or 1
- weight: bfloat16 [27, 256, 128], replicated, may hold values from -0.078125 to 0.078125
- pair_in: int32 [4, 128, 27, 128], P('scene', 'space'), may hold values from 0 to 127, as said below
- pair_out: int32 [4, 128, 27, 128], P('scene', 'space'), may hold values from 0 to 1152, as said below
- recv_index: int32 [4, 128, 1024], P('scene', 'space'), may hold values from 0 to 128, as said below
Outputs:
- conv_out: bfloat16 [4, 16384, 128], P('scene', 'space')
- input_grad: bfloat16 [4, 16384, 256], P('scene', 'space')
- weight_grad: float32 [27, 32768], P(None, 'space')
The draws below stay inside these ranges and needn't reach their ends.
Inputs may be any that keep to these rules, and one draw needn't show every extreme that they name: `pair_in`: in each offset's list the live pairs come first and padding after; live pairs of one offset have distinct input rows; padding pairs have input row 0. `pair_out`: live pairs name an owned row (distinct among one offset's local pairs) or a live boundary slot toward another device; padding pairs, and only they, hold 1152. In each scene some device has all 128 pairs live at every offset. `recv_index`: entry q * 8 + r of device p belongs to slot r of device q toward p; it is 128 where that slot is empty. The live slots from one device to another are the first ones; no device sends to itself; in each scene one device receives 8 live slots from every other device.
All inputs are finite; a program needn't handle non-finite values. No bound on the sum of `relu_mask` on one device may be relied on, other than what follows from the above.
Results may differ from the reference program's by a relative error of at most 0.001.
Values may be sent and summed in bfloat16 or wider, within the bound.
No kernel may reach another device: no remote copies, remote signals or barrier semaphores. Data moves between devices by JAX's collectives and lax.ppermute only.
A program may use at most 64 MiB of HBM per device.

```python
import math
import jax
import jax.numpy as jnp
from jax import lax

C_IN = 256
C_OUT = 128
OFFSETS = 27
SLOTS = 8
V_DEV = 128
PAIRS = 128
SCENES = 4
VOXELS = 16384
ALL_VOXELS = 65536


def rule_tables(key):
    peer_count = VOXELS // V_DEV
    send_rows = peer_count * SLOTS
    subkeys = jax.random.split(key, 8)
    peer_ids = jnp.arange(peer_count, dtype=jnp.int32)
    slot_live = jax.random.randint(subkeys[0], (SCENES, peer_count, peer_count), 1, SLOTS + 1)
    full_peer = jax.random.randint(subkeys[1], (SCENES,), 0, peer_count)
    slot_live = jnp.where(peer_ids[None, None, :] == full_peer[:, None, None], SLOTS, slot_live)
    slot_live = jnp.where((peer_ids[:, None] == peer_ids[None, :])[None, :, :], 0, slot_live)
    targets = jax.random.randint(subkeys[2], (SCENES, peer_count, peer_count, SLOTS), 0, V_DEV)
    slot_ids = jnp.arange(SLOTS, dtype=jnp.int32)
    live_mask = slot_ids[None, None, None, :] < slot_live[..., None]
    receive_table = jnp.where(live_mask, targets, V_DEV).transpose(0, 2, 1, 3)
    receive_table = receive_table.reshape(SCENES, peer_count, send_rows)
    counts = jax.random.randint(subkeys[3], (SCENES, peer_count, OFFSETS), PAIRS // 8, PAIRS // 2 + 1)
    busy_peer = jax.random.randint(subkeys[4], (SCENES,), 0, peer_count)
    counts = jnp.where(peer_ids[None, :, None] == busy_peer[:, None, None], PAIRS, counts)
    pair_ids = jnp.arange(PAIRS, dtype=jnp.int32)
    live_pair = pair_ids[None, None, None, :] < counts[..., None]
    order_ids = jnp.arange(V_DEV, dtype=jnp.int32)
    grid_shape = (SCENES, peer_count, OFFSETS, V_DEV)
    in_scores = jax.random.randint(subkeys[5], grid_shape, 0, 2 ** 20) * V_DEV + order_ids
    out_scores = jax.random.randint(subkeys[6], grid_shape, 0, 2 ** 20) * V_DEV + order_ids
    in_rows = jnp.argsort(in_scores, axis=-1)[..., :PAIRS]
    out_rows = jnp.argsort(out_scores, axis=-1)[..., :PAIRS]
    route_draw = jax.random.randint(subkeys[7], (SCENES, peer_count, OFFSETS, PAIRS), 0, 2 * send_rows)
    peer_pick = jnp.minimum(route_draw // SLOTS, peer_count - 1)
    live_at = jnp.take_along_axis(slot_live, peer_pick.reshape(SCENES, peer_count, OFFSETS * PAIRS), axis=2)
    live_at = live_at.reshape(peer_pick.shape)
    boundary = (route_draw < send_rows) & (route_draw % SLOTS < live_at)
    out_table = jnp.where(live_pair, jnp.where(boundary, V_DEV + route_draw, out_rows), V_DEV + send_rows)
    in_table = jnp.where(live_pair, in_rows, 0)
    return (in_table.astype(jnp.int32), out_table.astype(jnp.int32), receive_table.astype(jnp.int32))


def draw_pair_in(key, part):
    return rule_tables(jax.random.fold_in(key, 11))[0]


def draw_pair_out(key, part):
    return rule_tables(jax.random.fold_in(key, 11))[1]


def draw_recv_index(key, part):
    return rule_tables(jax.random.fold_in(key, 11))[2]


def with_ends(entries, rng, least, top_value):
    longest = entries.shape.index(max(entries.shape))
    spots = []
    for shift in (0, 1):
        where = [jax.random.randint(jax.random.fold_in(rng, axis), (), 0, length) for axis, length in enumerate(entries.shape)]
        where[longest] = (where[longest] + shift) % entries.shape[longest]
        spots.append(tuple(where))
    return entries.at[spots[0]].set(least).at[spots[1]].set(top_value)


def levels(key, extent, cuts, smallest, high):
    level = 1.0
    for position, parts in cuts:
        draws = jax.random.uniform(jax.random.fold_in(jax.random.fold_in(key, 6), position), (parts,), jnp.float32, smallest / len(cuts), high / len(cuts))
        level = level * jnp.repeat(jnp.exp(draws), extent[position] // parts).reshape((-1,) + (1,) * (len(extent) - 1 - position))
    return level


def scatter_about(stream_key, shape, width, bound, cuts=(), held_as=jnp.bfloat16):
    factor_of = levels(stream_key, shape, cuts, -0.22, 0.18) if cuts else 1.0
    result = jax.random.normal(stream_key, shape, jnp.float32) * width * factor_of
    return jnp.minimum(jnp.maximum(result, -bound), bound).astype(held_as)


def setup_inputs(seed: int = 0) -> dict:
    streams_of = jax.random.split(jax.random.key(seed), 8)
    features = scatter_about(streams_of[0], (SCENES, VOXELS, C_IN), 1.0, 6.0, ((0, 4), (1, 128)))
    cotangent = scatter_about(streams_of[1], (SCENES, VOXELS, C_OUT), 1.0, 6.0, ((0, 4), (1, 128)))
    relu_mask = with_ends((jax.random.randint(streams_of[2], (SCENES, VOXELS, C_OUT), 0, 2) < 1).astype(jnp.int32), jax.random.fold_in(streams_of[2], 1), 0, 1)
    weight = scatter_about(streams_of[3], (OFFSETS, C_IN, C_OUT), (C_IN * OFFSETS) ** -0.5, 0.078125)
    pair_in = draw_pair_in(jax.random.fold_in(streams_of[7], 71), 0)
    pair_out = draw_pair_out(jax.random.fold_in(streams_of[7], 71), 0)
    recv_index = draw_recv_index(jax.random.fold_in(streams_of[7], 71), 0)
    return {"features": features, "cotangent": cotangent, "relu_mask": relu_mask, "weight": weight, "pair_in": pair_in, "pair_out": pair_out, "recv_index": recv_index}


def reference(features, cotangent, relu_mask, weight, pair_in, pair_out, recv_index):
    peer_count = VOXELS // V_DEV
    send_rows = peer_count * SLOTS
    weight_wide = weight.astype(jnp.float32)

    def forward_device(operands):
        voxel_rows, in_table, out_table = operands

        def advance(partial_value, pieces):
            in_rows, out_rows, kernel = pieces
            gathered = voxel_rows[in_rows].astype(jnp.float32)
            return (partial_value.at[out_rows].add(jnp.dot(gathered, kernel)), None)
        start_buffer = jnp.zeros((V_DEV + send_rows + 1, C_OUT), jnp.float32)
        partial_value, unused = lax.scan(advance, start_buffer, (in_table, out_table, weight_wide))
        return (partial_value[:V_DEV], partial_value[V_DEV:V_DEV + send_rows])

    def backward_device(grad_total, operands):
        voxel_rows, extended, in_table, out_table = operands

        def advance(input_sums, pieces):
            in_rows, out_rows, kernel = pieces
            gathered = extended[out_rows].astype(jnp.float32)
            input_sums = input_sums.at[in_rows].add(jnp.dot(gathered, kernel.T))
            kernel_grad = jnp.dot(voxel_rows[in_rows].astype(jnp.float32).T, gathered)
            return (input_sums, kernel_grad)
        start_sums = jnp.zeros((V_DEV, C_IN), jnp.float32)
        input_sums, kernel_grads = lax.scan(advance, start_sums, (in_table, out_table, weight_wide))
        return (grad_total + kernel_grads, input_sums.astype(jnp.bfloat16))

    def receive(local_part, arrived, recv_rows):
        received = jnp.zeros((V_DEV + 1, C_OUT), jnp.float32).at[recv_rows].add(arrived)
        return local_part + received[:V_DEV]

    def take_rows(padded, recv_rows):
        return padded[recv_rows]

    def scene_step(grad_total, operands):
        scene_feats, scene_cot, scene_mask, in_tables, out_tables, recv_rows = operands
        voxel_blocks = scene_feats.reshape(peer_count, V_DEV, C_IN)
        local_part, outbound = lax.map(forward_device, (voxel_blocks, in_tables, out_tables))
        arrived = outbound.reshape(peer_count, peer_count, SLOTS, C_OUT).transpose(1, 0, 2, 3)
        arrived = arrived.reshape(peer_count, send_rows, C_OUT)
        conv_scene = jax.vmap(receive)(local_part, arrived, recv_rows).astype(jnp.bfloat16)
        upstream = (scene_cot.astype(jnp.float32) * scene_mask.astype(jnp.float32)).astype(jnp.bfloat16)
        upstream = upstream.reshape(peer_count, V_DEV, C_OUT)
        zero_row = jnp.zeros((peer_count, 1, C_OUT), jnp.bfloat16)
        outgoing = jax.vmap(take_rows)(jnp.concatenate([upstream, zero_row], axis=1), recv_rows)
        returned = outgoing.reshape(peer_count, peer_count, SLOTS, C_OUT).transpose(1, 0, 2, 3)
        returned = returned.reshape(peer_count, send_rows, C_OUT)
        extended = jnp.concatenate([upstream, returned, zero_row], axis=1)
        grad_total, input_grad = lax.scan(backward_device, grad_total, (voxel_blocks, extended, in_tables, out_tables))
        return (grad_total, (conv_scene.reshape(VOXELS, C_OUT), input_grad.reshape(VOXELS, C_IN)))
    start_total = jnp.zeros((OFFSETS, C_IN, C_OUT), jnp.float32)
    grad_total, outputs = lax.scan(scene_step, start_total, (features, cotangent, relu_mask, pair_in, pair_out, recv_index))
    conv_out, input_grad = outputs
    weight_grad = (grad_total * (1.0 / math.sqrt(ALL_VOXELS))).reshape(OFFSETS, C_IN * C_OUT)
    return (conv_out, input_grad, weight_grad)
```

```python
import math

import jax
import jax.numpy as jnp
from jax import lax
from jax.experimental import pallas as pl
from jax.experimental.pallas import tpu as pltpu
from jax.sharding import Mesh
from jax.sharding import PartitionSpec as P

F32 = jnp.float32
BF16 = jnp.bfloat16
I32 = jnp.int32
LANES = 128
VMEM_BYTES = 24 * 1024 * 1024


def call(kernel, outs, scratch=(), flops=0, moved=0):
    return pl.pallas_call(
        kernel,
        out_shape=outs,
        scratch_shapes=list(scratch),
        compiler_params=pltpu.CompilerParams(vmem_limit_bytes=VMEM_BYTES),
        cost_estimate=pl.CostEstimate(flops=flops, bytes_accessed=moved, transcendentals=0),
    )


def rows_iota(rows, start=0):
    return lax.broadcasted_iota(I32, (rows, LANES), 0) + start


def one_hot(iota, row):
    return jnp.where(iota == row, 1.0, 0.0).astype(BF16)


def split_two(value):
    high = value.astype(BF16)
    low = (value - high.astype(F32)).astype(BF16)
    return high, low


def gather_kernel(cot_ref, mask_ref, recv_ref, up_ref, out_ref):
    up = (cot_ref[...].astype(F32) * mask_ref[...].astype(F32)).astype(BF16)
    up_ref[...] = up
    iota = rows_iota(LANES)
    for g in range(recv_ref.shape[0]):
        hot = one_hot(iota, recv_ref[g : g + 1, :])
        rows = lax.dot_general(hot, up, (((0,), (0,)), ((), ())), preferred_element_type=F32)
        out_ref[g * LANES : (g + 1) * LANES, :] = rows.astype(BF16)


def forward_kernel(x_ref, w_ref, in_ref, out_ref, table_ref, own_ref, send_ref, terms_ref, hot_ref):
    offsets = w_ref.shape[0]
    no_target = own_ref.shape[0] + send_ref.shape[0]
    iota = rows_iota(LANES)
    picks = rows_iota(16)

    def product(k, carry):
        hot = one_hot(iota, in_ref[pl.ds(k, 1), :])
        target = out_ref[pl.ds(k, 1), :]
        code = jnp.where(target < no_target, target + 1, 0)
        digits = jnp.where(picks == 0, code >> 7, jnp.where(picks == 1, code & 127, 0))
        found = lax.dot_general(
            digits.astype(F32).astype(BF16), hot, (((1,), (1,)), ((), ())), preferred_element_type=F32
        )
        table_ref[pl.ds(k, 1), :] = (found[0:1] * 128.0 + found[1:2] - 1.0).astype(I32)
        high, low = split_two(jnp.dot(x_ref[...], w_ref[k], preferred_element_type=F32))
        spot = pl.ds(pl.multiple_of(k * LANES, LANES), LANES)
        terms_ref[spot, 0:LANES] = high
        terms_ref[spot, LANES : 2 * LANES] = low
        return carry

    lax.fori_loop(0, offsets, product, 0)

    def block(start):
        here = iota + start
        for k in range(offsets):
            hot_ref[:, k * LANES : (k + 1) * LANES] = one_hot(here, table_ref[k : k + 1, :])
        both = jnp.dot(hot_ref[...], terms_ref[...], preferred_element_type=F32)
        return both[:, :LANES] + both[:, LANES:]

    own_ref[...] = block(0)

    def scatter(b, carry):
        spot = pl.ds(pl.multiple_of(b * LANES, LANES), LANES)
        send_ref[spot, :] = block((b + 1) * LANES)
        return carry

    lax.fori_loop(0, send_ref.shape[0] // LANES, scatter, 0)


def backward_kernel(up_ref, back_ref, table_ref, w_ref, gathered_ref, grad_ref, ext_ref, sum_ref):
    offsets = w_ref.shape[0]
    blocks = back_ref.shape[0] // LANES
    ext_ref[:, 0:LANES] = up_ref[...].T
    for b in range(blocks):
        ext_ref[:, (b + 1) * LANES : (b + 2) * LANES] = back_ref[b * LANES : (b + 1) * LANES, :].T
    iota = rows_iota((blocks + 1) * LANES)
    sum_ref[...] = jnp.zeros_like(sum_ref)

    def step(k, carry):
        hot = one_hot(iota, table_ref[pl.ds(k, 1), :])
        rows = jnp.dot(ext_ref[...], hot, preferred_element_type=F32).astype(BF16)
        gathered_ref[pl.ds(pl.multiple_of(k * LANES, LANES), LANES), :] = rows
        sum_ref[...] += jnp.dot(w_ref[k], rows, preferred_element_type=F32)
        return carry

    lax.fori_loop(0, offsets, step, 0)
    grad_ref[...] = sum_ref[...].T.astype(BF16)


def receive_kernel(own_ref, arrived_ref, recv_ref, out_ref):
    iota = rows_iota(LANES)
    total = own_ref[...]
    for g in range(recv_ref.shape[0]):
        hot = one_hot(iota, recv_ref[g : g + 1, :])
        high, low = split_two(arrived_ref[g * LANES : (g + 1) * LANES, :])
        total += jnp.dot(hot, high, preferred_element_type=F32)
        total += jnp.dot(hot, low, preferred_element_type=F32)
    out_ref[...] = total.astype(BF16)


def kernel_grad_kernel(g_ref, x_ref, out_ref):
    columns = g_ref.shape[1]
    total = jnp.dot(g_ref[0], x_ref[0], preferred_element_type=F32)
    for s in range(1, g_ref.shape[0]):
        total += jnp.dot(g_ref[s], x_ref[s], preferred_element_type=F32)
    wide = -(-columns // LANES) * LANES
    total = jnp.concatenate([total, jnp.zeros((wide - columns, total.shape[1]), F32)], axis=0)
    out_ref[...] = total.T


def local(features, cotangent, relu_mask, weight, pair_in, pair_out, recv_index):
    space = ("y", "z", "core")
    ring = ("z", "core")
    x = features[0]
    own_rows, in_width = x.shape
    offsets, unused, out_width = weight.shape
    peers = lax.axis_size(space)
    send_rows = recv_index.shape[2]
    slots = send_rows // peers
    recv = recv_index.reshape(send_rows // LANES, LANES)
    pairs_in = pair_in[0, 0]
    pairs_out = pair_out[0, 0]
    shape = jax.ShapeDtypeStruct

    upstream, outgoing = call(
        gather_kernel,
        (shape((own_rows, out_width), BF16), shape((send_rows, out_width), BF16)),
        flops=2 * send_rows * own_rows * out_width,
        moved=send_rows * out_width * 3,
    )(cotangent[0], relu_mask[0], recv)
    returned = lax.all_to_all(outgoing.reshape(peers, slots, out_width), space, 0, 0, tiled=True)

    ring_size = lax.axis_size(ring)
    group_x = lax.all_gather(x, ring)

    table, own, outbound = call(
        forward_kernel,
        (
            shape((offsets, own_rows), I32),
            shape((own_rows, out_width), F32),
            shape((send_rows, out_width), F32),
        ),
        scratch=(
            pltpu.VMEM((offsets * own_rows, 2 * out_width), BF16),
            pltpu.VMEM((LANES, offsets * own_rows), BF16),
        ),
        flops=2 * (own_rows + send_rows) * offsets * own_rows * out_width * 2,
        moved=4 * offsets * in_width * out_width,
    )(x, weight, pairs_in, pairs_out)
    arrived = lax.all_to_all(outbound.reshape(peers, slots, out_width), space, 0, 0, tiled=True)

    gathered, input_grad = call(
        backward_kernel,
        (shape((offsets * out_width, own_rows), BF16), shape((own_rows, in_width), BF16)),
        scratch=(
            pltpu.VMEM((out_width, own_rows + send_rows), BF16),
            pltpu.VMEM((in_width, own_rows), F32),
        ),
        flops=2 * (own_rows + send_rows) * offsets * own_rows * out_width,
        moved=4 * offsets * in_width * out_width,
    )(upstream, returned.reshape(send_rows, out_width), table, weight)

    conv_out = call(
        receive_kernel,
        shape((own_rows, out_width), BF16),
        flops=4 * send_rows * own_rows * out_width,
        moved=send_rows * out_width * 4,
    )(own, arrived.reshape(send_rows, out_width), recv)

    columns = offsets * out_width // ring_size
    wide = -(-columns // LANES) * LANES
    group_g = lax.all_to_all(gathered.reshape(ring_size, columns, own_rows), ring, 0, 0, tiled=True)
    partial = call(
        kernel_grad_kernel,
        shape((in_width, wide), F32),
        flops=2 * columns * in_width * own_rows * ring_size,
        moved=4 * in_width * wide,
    )(group_g, group_x)
    y_size = lax.axis_size("y")
    parts = lax.all_to_all(partial.reshape(y_size, in_width // y_size, wide), "y", 0, 0, tiled=True)
    summed = parts.sum(axis=0)

    scenes = lax.axis_size("scene")
    own_in = in_width // peers
    last = jnp.broadcast_to(
        summed.reshape(ring_size, 1, own_in, wide), (ring_size, scenes, own_in, wide)
    ).reshape(ring_size * scenes, own_in, wide)
    last = lax.all_to_all(last, ("z", "core", "scene"), 0, 0, tiled=True)
    reduced = last.reshape(ring_size, scenes, own_in, wide).sum(axis=1)[:, :, :columns]
    reduced = reduced.transpose(1, 0, 2).reshape(own_in, offsets, out_width)
    reduced = reduced.transpose(1, 0, 2).reshape(offsets, own_in * out_width)
    normalizer = 1.0 / math.sqrt(scenes * peers * own_rows)
    return (conv_out[None], input_grad[None], reduced * normalizer)


def solution(mesh):
    space, scenes = mesh.devices.shape
    fine = Mesh(mesh.devices.reshape(8, space // 16, 2, scenes), ("y", "z", "core", "scene"))
    voxels = P("scene", ("y", "z", "core"))
    return jax.shard_map(
        local,
        mesh=fine,
        in_specs=(voxels, voxels, voxels, P(), voxels, voxels, voxels),
        out_specs=(voxels, voxels, P(None, ("y", "z", "core"))),
        check_vma=False,
    )
```

```python
import functools
import math

import jax
import jax.numpy as jnp
from jax import lax
from jax.experimental import pallas as pl
from jax.experimental.pallas import tpu as pltpu
from jax.sharding import Mesh
from jax.sharding import PartitionSpec as P

F32 = jnp.float32
BF16 = jnp.bfloat16
I32 = jnp.int32
LANES = 128
STEP = 3
VMEM_BYTES = 24 * 1024 * 1024
SPACE = ("y", "zh", "zl", "core")
GROUP = ("zl", "core", "scene")


def call(kernel, outs, scratch=(), flops=0, moved=0):
    return pl.pallas_call(
        kernel,
        out_shape=outs,
        scratch_shapes=list(scratch),
        compiler_params=pltpu.CompilerParams(vmem_limit_bytes=VMEM_BYTES),
        cost_estimate=pl.CostEstimate(flops=flops, bytes_accessed=moved, transcendentals=0),
    )


def rows_iota(rows, start=0):
    return lax.broadcasted_iota(I32, (rows, LANES), 0) + start


def one_hot(iota, row):
    return jnp.where(iota == row, 1.0, 0.0).astype(BF16)


def split_two(value):
    high = value.astype(BF16)
    low = (value - high.astype(F32)).astype(BF16)
    return high, low


def lane_block(k):
    return slice(k * LANES, (k + 1) * LANES)


def gather_kernel(cot_ref, mask_ref, recv_ref, up_ref, out_ref):
    up = (cot_ref[...].astype(F32) * mask_ref[...].astype(F32)).astype(BF16)
    up_ref[...] = up
    iota = rows_iota(LANES)
    for g in range(recv_ref.shape[0]):
        hot = one_hot(iota, recv_ref[g : g + 1, :])
        rows = lax.dot_general(hot, up, (((0,), (0,)), ((), ())), preferred_element_type=F32)
        out_ref[lane_block(g), :] = rows.astype(BF16)


def table_kernel(in_ref, out_ref, table_ref, *, targets):
    iota = rows_iota(LANES)
    picks = rows_iota(16)
    for k in range(in_ref.shape[0]):
        hot = one_hot(iota, in_ref[k : k + 1, :])
        target = out_ref[k : k + 1, :]
        code = jnp.where(target < targets, target + 1, 0)
        digits = jnp.where(picks == 0, code >> 7, jnp.where(picks == 1, code & 127, 0))
        found = lax.dot_general(
            digits.astype(F32).astype(BF16), hot, (((1,), (1,)), ((), ())), preferred_element_type=F32
        )
        table_ref[k : k + 1, :] = (found[0:1] * 128.0 + found[1:2] - 1.0).astype(I32)


def lookup_kernel(up_ref, back_ref, table_ref, gathered_ref, ext_ref, hot_ref):
    blocks = back_ref.shape[0] // LANES
    offsets = table_ref.shape[0]
    ext_ref[:, 0:LANES] = up_ref[...].T
    for b in range(blocks):
        ext_ref[:, lane_block(b + 1)] = back_ref[lane_block(b), :].T
    iota = rows_iota((blocks + 1) * LANES)
    step = STEP
    for first in range(0, offsets, step):
        count = min(step, offsets - first)
        slot = (first // step) % 2
        for k in range(count):
            hot_ref[slot, :, lane_block(k)] = one_hot(iota, table_ref[first + k : first + k + 1, :])
        rows = jnp.dot(
            ext_ref[...], hot_ref[slot, :, : count * LANES], preferred_element_type=F32
        ).astype(BF16)
        for k in range(count):
            gathered_ref[lane_block(first + k), :] = rows[:, lane_block(k)]


def forward_kernel(x_ref, w_ref, table_ref, gathered_ref, own_ref, send_ref, grad_ref, terms_ref, hot_ref):
    offsets = w_ref.shape[0]
    total = jnp.zeros((w_ref.shape[1], LANES), F32)
    for k in range(offsets):
        high, low = split_two(jnp.dot(x_ref[...], w_ref[k], preferred_element_type=F32))
        terms_ref[lane_block(k), 0:LANES] = high
        terms_ref[lane_block(k), LANES : 2 * LANES] = low
        total += jnp.dot(w_ref[k], gathered_ref[lane_block(k), :], preferred_element_type=F32)
    grad_ref[...] = total.T.astype(BF16)

    def block(start):
        here = rows_iota(LANES) + start
        for k in range(offsets):
            hot_ref[:, lane_block(k)] = one_hot(here, table_ref[k : k + 1, :])
        both = jnp.dot(hot_ref[...], terms_ref[...], preferred_element_type=F32)
        return both[:, :LANES] + both[:, LANES:]

    own_ref[...] = block(0)

    def scatter(b, carry):
        send_ref[pl.ds(pl.multiple_of(b * LANES, LANES), LANES), :] = block((b + 1) * LANES)
        return carry

    lax.fori_loop(0, send_ref.shape[0] // LANES, scatter, 0)


def pack_kernel(g_ref, x_ref, send_ref, out_ref, turn_ref):
    columns = g_ref.shape[1]
    peers = x_ref.shape[2] // 2
    total = jnp.dot(g_ref[0], x_ref[0], preferred_element_type=F32)
    for s in range(1, g_ref.shape[0]):
        total += jnp.dot(g_ref[s], x_ref[s], preferred_element_type=F32)
    total = jnp.concatenate([total, jnp.zeros((2 * LANES - columns, total.shape[1]), F32)], axis=0)
    for half in range(2):
        turn_ref[half] = total[lane_block(half), :].T
    for r in range(8):
        out_ref[pl.ds(r, peers, stride=12), :] = send_ref[pl.ds(r, peers, stride=8), :]
    for c in range(2):
        for half in range(2):
            rows = turn_ref[half, pl.ds(c, peers, stride=2), :]
            out_ref[pl.ds(8 + 2 * c + half, peers, stride=12), :] = rows


def sum_kernel(arrived_ref, out_ref):
    total = arrived_ref[0]
    for i in range(1, arrived_ref.shape[0]):
        total += arrived_ref[i]
    for s in range(out_ref.shape[0]):
        for i in range(4):
            out_ref[s, 4 * i : 4 * i + 4, :] = total[12 * i + 8 : 12 * i + 12, :]


def receive_kernel(own_ref, arrived_ref, recv_ref, out_ref, rows_ref):
    peers = arrived_ref.shape[0] // 12
    iota = rows_iota(LANES)
    for r in range(8):
        rows_ref[pl.ds(r, peers, stride=8), :] = arrived_ref[pl.ds(r, peers, stride=12), :]
    total = own_ref[...]
    for g in range(recv_ref.shape[0]):
        hot = one_hot(iota, recv_ref[g : g + 1, :])
        high, low = split_two(rows_ref[lane_block(g), :])
        total += jnp.dot(hot, high, preferred_element_type=F32)
        total += jnp.dot(hot, low, preferred_element_type=F32)
    out_ref[...] = total.astype(BF16)


def local(features, cotangent, relu_mask, weight, pair_in, pair_out, recv_index):
    x = features[0]
    own_rows, in_width = x.shape
    offsets, unused, out_width = weight.shape
    peers = lax.axis_size(SPACE)
    group = lax.axis_size(GROUP)
    scenes = lax.axis_size("scene")
    send_rows = recv_index.shape[2]
    slots = send_rows // peers
    targets = own_rows + send_rows
    columns = offsets * out_width // group
    recv = recv_index.reshape(send_rows // LANES, LANES)
    shape = jax.ShapeDtypeStruct

    group_x = lax.all_gather(x, GROUP)
    upstream, outgoing = call(
        gather_kernel,
        (shape((own_rows, out_width), BF16), shape((send_rows, out_width), BF16)),
        flops=2 * send_rows * own_rows * out_width,
        moved=send_rows * out_width * 3,
    )(cotangent[0], relu_mask[0], recv)
    returned = lax.all_to_all(outgoing.reshape(peers, slots, out_width), SPACE, 0, 0, tiled=True)

    table = call(
        functools.partial(table_kernel, targets=targets),
        shape((offsets, own_rows), I32),
        flops=2 * targets * offsets * own_rows * 100,
    )(pair_in[0, 0], pair_out[0, 0])

    gathered = call(
        lookup_kernel,
        shape((offsets * out_width, own_rows), BF16),
        scratch=(pltpu.VMEM((out_width, targets), BF16), pltpu.VMEM((2, targets, STEP * LANES), BF16)),
        flops=2 * targets * offsets * own_rows * out_width,
        moved=2 * offsets * own_rows * out_width,
    )(upstream, returned.reshape(send_rows, out_width), table)

    gathered, group_x = lax.optimization_barrier((gathered, group_x))
    group_g = lax.all_to_all(gathered.reshape(group, columns, own_rows), GROUP, 0, 0, tiled=True)

    own, outbound, input_grad = call(
        forward_kernel,
        (
            shape((own_rows, out_width), F32),
            shape((send_rows, out_width), F32),
            shape((own_rows, in_width), BF16),
        ),
        scratch=(
            pltpu.VMEM((offsets * own_rows, 2 * out_width), BF16),
            pltpu.VMEM((LANES, offsets * own_rows), BF16),
        ),
        flops=4 * targets * offsets * own_rows * out_width,
        moved=4 * offsets * in_width * out_width,
    )(x, weight, table, gathered)

    packed = call(
        pack_kernel,
        shape((peers * 12, LANES), F32),
        scratch=(pltpu.VMEM((2, in_width, LANES), F32),),
        flops=2 * columns * in_width * own_rows * group,
        moved=peers * 12 * LANES * 8,
    )(group_g, group_x, outbound)
    arrived = lax.all_to_all(packed.reshape(peers, 1, 12 * LANES), SPACE, 0, 0, tiled=True)
    arrived = arrived.reshape(peers * 12, LANES)

    quarter = call(sum_kernel, shape((scenes, 16, LANES), F32), moved=peers * 12 * LANES * 4)(
        arrived.reshape(peers // 4, 48, LANES)
    )
    blocks = lax.all_to_all(quarter, "scene", 0, 0, tiled=True)
    conv_out = call(
        receive_kernel,
        shape((own_rows, out_width), BF16),
        scratch=(pltpu.VMEM((send_rows, out_width), F32),),
        flops=4 * send_rows * own_rows * out_width,
        moved=send_rows * out_width * 4,
    )(own, arrived, recv)

    own_in = in_width // peers
    blocks = blocks.reshape(scenes, 4, own_in, 2 * LANES)[:, :, :, :columns]
    kernel_grad = blocks.transpose(2, 1, 0, 3).reshape(own_in, offsets, out_width)
    kernel_grad = kernel_grad.transpose(1, 0, 2).reshape(offsets, own_in * out_width)
    normalizer = 1.0 / math.sqrt(scenes * peers * own_rows)
    return (conv_out[None], input_grad[None], kernel_grad * normalizer)


def solution(mesh):
    scenes = mesh.devices.shape[1]
    fine = Mesh(mesh.devices.reshape(8, 4, 2, 2, scenes), ("y", "zh", "zl", "core", "scene"))
    voxels = P("scene", SPACE)
    return jax.shard_map(
        local,
        mesh=fine,
        in_specs=(voxels, voxels, voxels, P(), voxels, voxels, voxels),
        out_specs=(voxels, voxels, P(None, SPACE)),
        check_vma=False,
    )
```

```python
import functools
import math

import jax
import jax.numpy as jnp
from jax import lax
from jax.experimental import pallas as pl
from jax.experimental.pallas import tpu as pltpu
from jax.sharding import Mesh
from jax.sharding import PartitionSpec as P

F32 = jnp.float32
BF16 = jnp.bfloat16
I32 = jnp.int32
LANES = 128
STEP = 3
WAIT_FLOPS = 2 * 10**10
VMEM_BYTES = 24 * 1024 * 1024
SPACE = ("y", "zh", "zl", "core")
GROUP = ("zl", "core", "scene")


def call(kernel, outs, scratch=(), flops=0, moved=0):
    return pl.pallas_call(
        kernel,
        out_shape=outs,
        scratch_shapes=list(scratch),
        compiler_params=pltpu.CompilerParams(vmem_limit_bytes=VMEM_BYTES),
        cost_estimate=pl.CostEstimate(flops=flops, bytes_accessed=moved, transcendentals=0),
    )


def rows_iota(rows, start=0):
    return lax.broadcasted_iota(I32, (rows, LANES), 0) + start


def one_hot(iota, row):
    return jnp.where(iota == row, 1.0, 0.0).astype(BF16)


def split_two(value):
    high = value.astype(BF16)
    low = (value - high.astype(F32)).astype(BF16)
    return high, low


def lane_block(k):
    return slice(k * LANES, (k + 1) * LANES)


def gather_kernel(cot_ref, mask_ref, recv_ref, up_ref, out_ref):
    up = (cot_ref[...].astype(F32) * mask_ref[...].astype(F32)).astype(BF16)
    up_ref[...] = up
    iota = rows_iota(LANES)
    for g in range(recv_ref.shape[0]):
        hot = one_hot(iota, recv_ref[g : g + 1, :])
        rows = lax.dot_general(hot, up, (((0,), (0,)), ((), ())), preferred_element_type=F32)
        out_ref[lane_block(g), :] = rows.astype(BF16)


def table_kernel(in_ref, out_ref, table_ref, *, targets):
    iota = rows_iota(LANES)
    picks = rows_iota(16)
    for k in range(in_ref.shape[0]):
        hot = one_hot(iota, in_ref[k : k + 1, :])
        target = out_ref[k : k + 1, :]
        code = jnp.where(target < targets, target + 1, 0)
        digits = jnp.where(picks == 0, code >> 7, jnp.where(picks == 1, code & 127, 0))
        found = lax.dot_general(
            digits.astype(F32).astype(BF16), hot, (((1,), (1,)), ((), ())), preferred_element_type=F32
        )
        table_ref[k : k + 1, :] = (found[0:1] * 128.0 + found[1:2] - 1.0).astype(I32)


def lookup_kernel(up_ref, back_ref, table_ref, gathered_ref, ext_ref, hot_ref):
    blocks = back_ref.shape[0] // LANES
    offsets = table_ref.shape[0]
    ext_ref[:, 0:LANES] = up_ref[...].T
    for b in range(blocks):
        ext_ref[:, lane_block(b + 1)] = back_ref[lane_block(b), :].T
    iota = rows_iota((blocks + 1) * LANES)
    step = STEP
    for first in range(0, offsets, step):
        count = min(step, offsets - first)
        slot = (first // step) % 2
        for k in range(count):
            hot_ref[slot, :, lane_block(k)] = one_hot(iota, table_ref[first + k : first + k + 1, :])
        rows = jnp.dot(
            ext_ref[...], hot_ref[slot, :, : count * LANES], preferred_element_type=F32
        ).astype(BF16)
        for k in range(count):
            gathered_ref[lane_block(first + k), :] = rows[:, lane_block(k)]


def input_grad_kernel(w_ref, gathered_ref, grad_ref):
    total = jnp.zeros((w_ref.shape[1], LANES), F32)
    for k in range(w_ref.shape[0]):
        total += jnp.dot(w_ref[k], gathered_ref[lane_block(k), :], preferred_element_type=F32)
    grad_ref[...] = total.T.astype(BF16)


def forward_kernel(x_ref, w_ref, table_ref, own_ref, send_ref, terms_ref, hot_ref):
    offsets = w_ref.shape[0]
    for k in range(offsets):
        high, low = split_two(jnp.dot(x_ref[...], w_ref[k], preferred_element_type=F32))
        terms_ref[lane_block(k), 0:LANES] = high
        terms_ref[lane_block(k), LANES : 2 * LANES] = low

    def block(start):
        here = rows_iota(LANES) + start
        for k in range(offsets):
            hot_ref[:, lane_block(k)] = one_hot(here, table_ref[k : k + 1, :])
        both = jnp.dot(hot_ref[...], terms_ref[...], preferred_element_type=F32)
        return both[:, :LANES] + both[:, LANES:]

    own_ref[...] = block(0)

    def scatter(b, carry):
        send_ref[pl.ds(pl.multiple_of(b * LANES, LANES), LANES), :] = block((b + 1) * LANES)
        return carry

    lax.fori_loop(0, send_ref.shape[0] // LANES, scatter, 0)


def encode(value, top):
    level = jnp.ceil(jnp.log2(jnp.maximum(top, 1e-36)) * 8.0)
    code = jnp.round(value * jnp.exp2(level * -0.125) * 32767.0)
    return jnp.clip(code, -32767.0, 32767.0).astype(I32), level.astype(I32)


def unit(level):
    return jnp.exp2(level.astype(F32) * 0.125) * (1.0 / 32767.0)


def join(first, second):
    return (first << 16) | (second & 0xFFFF)


def halves(word):
    return (word >> 16).astype(F32), ((word << 16) >> 16).astype(F32)


def row_top(value):
    return jnp.max(jnp.abs(value), axis=1, keepdims=True)


def pack_kernel(g_ref, x_ref, send_ref, out_ref, turn_ref):
    columns = g_ref.shape[1]
    peers = x_ref.shape[2] // 2
    total = jnp.dot(g_ref[0], x_ref[0], preferred_element_type=F32)
    for s in range(1, g_ref.shape[0]):
        total += jnp.dot(g_ref[s], x_ref[s], preferred_element_type=F32)
    total = jnp.concatenate([total, jnp.zeros((2 * LANES - columns, total.shape[1]), F32)], axis=0)
    for half in range(2):
        turn_ref[half] = total[lane_block(half), :].T
    free = columns - LANES
    lane = lax.broadcasted_iota(I32, (peers, LANES), 1)
    levels = jnp.zeros((peers, LANES), I32)
    for r in range(4):
        words = []
        for slot in (r, r + 4):
            value = send_ref[pl.ds(slot, peers, stride=8), :]
            code, level = encode(value, row_top(value))
            words.append(code)
            levels = jnp.where(lane == free + slot, level, levels)
        out_ref[pl.ds(r, peers, stride=6), :] = join(*words)
    parts = [[turn_ref[h, pl.ds(c, peers, stride=2), :] for c in range(2)] for h in range(2)]
    top = jnp.maximum(
        jnp.maximum(row_top(parts[0][0]), row_top(parts[0][1])),
        jnp.maximum(row_top(parts[1][0]), row_top(parts[1][1])),
    )
    for half in range(2):
        codes = [encode(parts[half][c], top) for c in range(2)]
        word = join(codes[0][0], codes[1][0])
        if half == 1:
            levels = jnp.where(lane == free + 8, codes[0][1], levels)
            word = jnp.where(lane < free, word, levels)
        out_ref[pl.ds(4 + half, peers, stride=6), :] = word


def sum_kernel(arrived_ref, out_ref, *, free):
    peers = arrived_ref.shape[0] // 6
    words = [arrived_ref[pl.ds(4 + half, peers, stride=6), :] for half in range(2)]
    scale = unit(words[1][:, free + 8 : free + 9])
    for half in range(2):
        for c, value in enumerate(halves(words[half])):
            total = (value * scale).reshape(peers // 8, 8, LANES).sum(axis=0)
            total = total[0:4] + total[4:8]
            row = 4 * (2 * c + half)
            for s in range(out_ref.shape[0]):
                out_ref[s, row : row + 4, :] = total


def receive_kernel(own_ref, arrived_ref, recv_ref, out_ref, rows_ref, *, free):
    peers = arrived_ref.shape[0] // 6
    iota = rows_iota(LANES)
    levels = arrived_ref[pl.ds(5, peers, stride=6), :]
    for r in range(4):
        pair = halves(arrived_ref[pl.ds(r, peers, stride=6), :])
        for value, slot in zip(pair, (r, r + 4)):
            scale = unit(levels[:, free + slot : free + slot + 1])
            rows_ref[pl.ds(slot, peers, stride=8), :] = value * scale
    total = own_ref[...]
    for g in range(recv_ref.shape[0]):
        hot = one_hot(iota, recv_ref[g : g + 1, :])
        high, low = split_two(rows_ref[lane_block(g), :])
        total += jnp.dot(hot, high, preferred_element_type=F32)
        total += jnp.dot(hot, low, preferred_element_type=F32)
    out_ref[...] = total.astype(BF16)


def local(features, cotangent, relu_mask, weight, pair_in, pair_out, recv_index):
    x = features[0]
    own_rows, in_width = x.shape
    offsets, unused, out_width = weight.shape
    peers = lax.axis_size(SPACE)
    group = lax.axis_size(GROUP)
    scenes = lax.axis_size("scene")
    send_rows = recv_index.shape[2]
    slots = send_rows // peers
    targets = own_rows + send_rows
    columns = offsets * out_width // group
    recv = recv_index.reshape(send_rows // LANES, LANES)
    shape = jax.ShapeDtypeStruct

    group_x = lax.all_gather(x, GROUP)
    upstream, outgoing = call(
        gather_kernel,
        (shape((own_rows, out_width), BF16), shape((send_rows, out_width), BF16)),
        flops=2 * send_rows * own_rows * out_width,
        moved=send_rows * out_width * 3,
    )(cotangent[0], relu_mask[0], recv)
    returned = lax.all_to_all(outgoing.reshape(peers, slots, out_width), SPACE, 0, 0, tiled=True)

    table = call(
        functools.partial(table_kernel, targets=targets),
        shape((offsets, own_rows), I32),
    )(pair_in[0, 0], pair_out[0, 0])

    own, outbound = call(
        forward_kernel,
        (shape((own_rows, out_width), F32), shape((send_rows, out_width), F32)),
        scratch=(
            pltpu.VMEM((offsets * own_rows, 2 * out_width), BF16),
            pltpu.VMEM((LANES, offsets * own_rows), BF16),
        ),
    )(x, weight, table)

    returned, own, outbound = lax.optimization_barrier((returned, own, outbound))
    gathered = call(
        lookup_kernel,
        shape((offsets * out_width, own_rows), BF16),
        scratch=(pltpu.VMEM((out_width, targets), BF16), pltpu.VMEM((2, targets, STEP * LANES), BF16)),
    )(upstream, returned.reshape(send_rows, out_width), table)
    group_g = lax.all_to_all(gathered.reshape(group, columns, own_rows), GROUP, 0, 0, tiled=True)

    gathered, group_x = lax.optimization_barrier((gathered, group_x))
    input_grad = call(
        input_grad_kernel,
        shape((own_rows, in_width), BF16),
        flops=WAIT_FLOPS,
    )(weight, gathered)
    outbound, input_grad = lax.optimization_barrier((outbound, input_grad))

    packed = call(
        pack_kernel,
        shape((peers * 6, LANES), I32),
        scratch=(pltpu.VMEM((2, in_width, LANES), F32),),
        flops=2 * columns * in_width * own_rows * group,
        moved=peers * 6 * LANES * 8,
    )(group_g, group_x, outbound)
    arrived = lax.all_to_all(packed.reshape(peers, 1, 6 * LANES), SPACE, 0, 0, tiled=True)
    arrived = arrived.reshape(peers * 6, LANES)

    free = columns - LANES
    quarter = call(
        functools.partial(sum_kernel, free=free),
        shape((scenes, 16, LANES), F32),
        moved=peers * 6 * LANES * 4,
    )(arrived)
    blocks = lax.all_to_all(quarter, "scene", 0, 0, tiled=True)
    conv_out = call(
        functools.partial(receive_kernel, free=free),
        shape((own_rows, out_width), BF16),
        scratch=(pltpu.VMEM((send_rows, out_width), F32),),
        flops=4 * send_rows * own_rows * out_width,
        moved=send_rows * out_width * 4,
    )(own, arrived, recv)

    own_in = in_width // peers
    blocks = blocks.reshape(scenes, own_in, 2, 4, LANES).transpose(1, 3, 0, 2, 4)
    blocks = blocks.reshape(own_in, group, 2 * LANES)[:, :, :columns]
    kernel_grad = blocks.reshape(own_in, offsets, out_width)
    kernel_grad = kernel_grad.transpose(1, 0, 2).reshape(offsets, own_in * out_width)
    normalizer = 1.0 / math.sqrt(scenes * peers * own_rows)
    return (conv_out[None], input_grad[None], kernel_grad * normalizer)


def solution(mesh):
    scenes = mesh.devices.shape[1]
    fine = Mesh(mesh.devices.reshape(8, 4, 2, 2, scenes), ("y", "zh", "zl", "core", "scene"))
    voxels = P("scene", SPACE)
    return jax.shard_map(
        local,
        mesh=fine,
        in_specs=(voxels, voxels, voxels, P(), voxels, voxels, voxels),
        out_specs=(voxels, voxels, P(None, SPACE)),
        check_vma=False,
    )
```

```python
import functools
import math

import jax
import jax.numpy as jnp
from jax import lax
from jax.experimental import pallas as pl
from jax.experimental.pallas import tpu as pltpu
from jax.sharding import Mesh
from jax.sharding import PartitionSpec as P

F32 = jnp.float32
BF16 = jnp.bfloat16
I32 = jnp.int32
LANES = 128
STEP = 3
VMEM_BYTES = 24 * 1024 * 1024
SPACE = ("y", "zh", "zl", "core")
GROUP = ("zl", "core", "scene")


def call(kernel, outs, scratch=(), flops=0, moved=0, **specs):
    return pl.pallas_call(
        kernel,
        out_shape=outs,
        scratch_shapes=list(scratch),
        **specs,
        compiler_params=pltpu.CompilerParams(vmem_limit_bytes=VMEM_BYTES),
        cost_estimate=pl.CostEstimate(flops=flops, bytes_accessed=moved, transcendentals=0),
    )


def rows_iota(rows, start=0):
    return lax.broadcasted_iota(I32, (rows, LANES), 0) + start


def one_hot(iota, row):
    return jnp.where(iota == row, 1.0, 0.0).astype(BF16)


def split_two(value):
    high = value.astype(BF16)
    low = (value - high.astype(F32)).astype(BF16)
    return high, low


def lane_block(k):
    return slice(k * LANES, (k + 1) * LANES)


def gather_kernel(cot_ref, mask_ref, recv_ref, up_ref, out_ref):
    up = (cot_ref[...].astype(F32) * mask_ref[...].astype(F32)).astype(BF16)
    up_ref[...] = up
    iota = rows_iota(LANES)
    for g in range(recv_ref.shape[0]):
        hot = one_hot(iota, recv_ref[g : g + 1, :])
        rows = lax.dot_general(hot, up, (((0,), (0,)), ((), ())), preferred_element_type=F32)
        out_ref[lane_block(g), :] = rows.astype(BF16)


def table_kernel(in_ref, out_ref, table_ref, *, targets):
    iota = rows_iota(LANES)
    picks = rows_iota(16)
    for k in range(in_ref.shape[0]):
        hot = one_hot(iota, in_ref[k : k + 1, :])
        target = out_ref[k : k + 1, :]
        code = jnp.where(target < targets, target + 1, 0)
        digits = jnp.where(picks == 0, code >> 7, jnp.where(picks == 1, code & 127, 0))
        found = lax.dot_general(
            digits.astype(F32).astype(BF16), hot, (((1,), (1,)), ((), ())), preferred_element_type=F32
        )
        table_ref[k : k + 1, :] = (found[0:1] * 128.0 + found[1:2] - 1.0).astype(I32)


def lookup_kernel(up_ref, back_ref, table_ref, gathered_ref, ext_ref, hot_ref):
    blocks = back_ref.shape[0] // LANES
    offsets = table_ref.shape[0]
    ext_ref[:, 0:LANES] = up_ref[...].T
    for b in range(blocks):
        ext_ref[:, lane_block(b + 1)] = back_ref[lane_block(b), :].T
    iota = rows_iota((blocks + 1) * LANES)
    step = STEP
    for first in range(0, offsets, step):
        count = min(step, offsets - first)
        slot = (first // step) % 2
        for k in range(count):
            hot_ref[slot, :, lane_block(k)] = one_hot(iota, table_ref[first + k : first + k + 1, :])
        rows = jnp.dot(
            ext_ref[...], hot_ref[slot, :, : count * LANES], preferred_element_type=F32
        ).astype(BF16)
        for k in range(count):
            gathered_ref[lane_block(first + k), :] = rows[:, lane_block(k)]


def input_grad_kernel(w_ref, gathered_ref, grad_ref):
    total = jnp.zeros((w_ref.shape[1], LANES), F32)
    for k in range(w_ref.shape[0]):
        total += jnp.dot(w_ref[k], gathered_ref[lane_block(k), :], preferred_element_type=F32)
    grad_ref[...] = total.T.astype(BF16)


def forward_kernel(x_ref, w_ref, table_ref, own_ref, send_ref, terms_ref, hot_ref):
    offsets = w_ref.shape[0]
    for k in range(offsets):
        high, low = split_two(jnp.dot(x_ref[...], w_ref[k], preferred_element_type=F32))
        terms_ref[lane_block(k), 0:LANES] = high
        terms_ref[lane_block(k), LANES : 2 * LANES] = low

    def block(start):
        here = rows_iota(LANES) + start
        for k in range(offsets):
            hot_ref[:, lane_block(k)] = one_hot(here, table_ref[k : k + 1, :])
        both = jnp.dot(hot_ref[...], terms_ref[...], preferred_element_type=F32)
        return both[:, :LANES] + both[:, LANES:]

    own_ref[...] = block(0)

    def scatter(b, carry):
        send_ref[pl.ds(pl.multiple_of(b * LANES, LANES), LANES), :] = block((b + 1) * LANES)
        return carry

    lax.fori_loop(0, send_ref.shape[0] // LANES, scatter, 0)


def encode(value, top):
    level = jnp.ceil(jnp.log2(jnp.maximum(top, 1e-36)) * 8.0)
    code = jnp.round(value * jnp.exp2(level * -0.125) * 32767.0)
    return jnp.clip(code, -32767.0, 32767.0).astype(I32), level.astype(I32)


def unit(level):
    return jnp.exp2(level.astype(F32) * 0.125) * (1.0 / 32767.0)


def join(first, second):
    return (first << 16) | (second & 0xFFFF)


def halves(word):
    return (word >> 16).astype(F32), ((word << 16) >> 16).astype(F32)


def row_top(value):
    return jnp.max(jnp.abs(value), axis=1, keepdims=True)


def pack_kernel(g_ref, near_ref, far_ref, send_ref, out_ref, turn_ref):
    columns = g_ref.shape[1]
    peers = near_ref.shape[2] // 2
    total = jnp.zeros((columns, near_ref.shape[2]), F32)
    low, core, scene = (lax.axis_index(axis) for axis in GROUP)
    scenes = near_ref.shape[0] // 2
    for s in range(g_ref.shape[0]):
        x_ref = near_ref if s < 2 * scenes else far_ref
        zl = low if s // scenes % 2 == 0 else 1 - low
        other = core if s < 2 * scenes else 1 - core
        sender = (zl * 2 + other) * scenes + lax.rem(scene + scenes - s % scenes, scenes)
        total += jnp.dot(g_ref[sender], x_ref[s % (2 * scenes)], preferred_element_type=F32)
    total = jnp.concatenate([total, jnp.zeros((2 * LANES - columns, total.shape[1]), F32)], axis=0)
    for half in range(2):
        turn_ref[half] = total[lane_block(half), :].T
    free = columns - LANES
    lane = lax.broadcasted_iota(I32, (peers, LANES), 1)
    levels = jnp.zeros((peers, LANES), I32)
    for r in range(4):
        words = []
        for slot in (r, r + 4):
            value = send_ref[pl.ds(slot, peers, stride=8), :]
            code, level = encode(value, row_top(value))
            words.append(code)
            levels = jnp.where(lane == free + slot, level, levels)
        out_ref[pl.ds(r, peers, stride=6), :] = join(*words)
    parts = [[turn_ref[h, pl.ds(c, peers, stride=2), :] for c in range(2)] for h in range(2)]
    top = jnp.maximum(
        jnp.maximum(row_top(parts[0][0]), row_top(parts[0][1])),
        jnp.maximum(row_top(parts[1][0]), row_top(parts[1][1])),
    )
    for half in range(2):
        codes = [encode(parts[half][c], top) for c in range(2)]
        word = join(codes[0][0], codes[1][0])
        if half == 1:
            levels = jnp.where(lane == free + 8, codes[0][1], levels)
            word = jnp.where(lane < free, word, levels)
        out_ref[pl.ds(4 + half, peers, stride=6), :] = word


def sum_kernel(arrived_ref, out_ref, *, free):
    peers = arrived_ref.shape[0] // 6
    words = [arrived_ref[pl.ds(4 + half, peers, stride=6), :] for half in range(2)]
    scale = unit(words[1][:, free + 8 : free + 9])
    for half in range(2):
        for c, value in enumerate(halves(words[half])):
            total = (value * scale).reshape(peers // 8, 8, LANES).sum(axis=0)
            total = total[0:4] + total[4:8]
            row = 4 * (2 * c + half)
            for s in range(out_ref.shape[0]):
                out_ref[s, row : row + 4, :] = total


def receive_kernel(own_ref, arrived_ref, recv_ref, out_ref, rows_ref, *, free):
    peers = arrived_ref.shape[0] // 6
    iota = rows_iota(LANES)
    levels = arrived_ref[pl.ds(5, peers, stride=6), :]
    for r in range(4):
        pair = halves(arrived_ref[pl.ds(r, peers, stride=6), :])
        for value, slot in zip(pair, (r, r + 4)):
            scale = unit(levels[:, free + slot : free + slot + 1])
            rows_ref[pl.ds(slot, peers, stride=8), :] = value * scale
    total = own_ref[...]
    for g in range(recv_ref.shape[0]):
        hot = one_hot(iota, recv_ref[g : g + 1, :])
        high, low = split_two(rows_ref[lane_block(g), :])
        total += jnp.dot(hot, high, preferred_element_type=F32)
        total += jnp.dot(hot, low, preferred_element_type=F32)
    out_ref[...] = total.astype(BF16)


def local(features, cotangent, relu_mask, weight, pair_in, pair_out, recv_index):
    x = features[0]
    own_rows, in_width = x.shape
    offsets, unused, out_width = weight.shape
    peers = lax.axis_size(SPACE)
    group = lax.axis_size(GROUP)
    scenes = lax.axis_size("scene")
    send_rows = recv_index.shape[2]
    slots = send_rows // peers
    targets = own_rows + send_rows
    columns = offsets * out_width // group
    recv = recv_index.reshape(send_rows // LANES, LANES)
    shape = jax.ShapeDtypeStruct

    upstream, outgoing = call(
        gather_kernel,
        (shape((own_rows, out_width), BF16), shape((send_rows, out_width), BF16)),
        flops=2 * send_rows * own_rows * out_width,
        moved=send_rows * out_width * 3,
    )(cotangent[0], relu_mask[0], recv)
    own_x, outgoing = lax.optimization_barrier((x, outgoing))
    returned = lax.all_to_all(outgoing.reshape(peers, slots, out_width), SPACE, 0, 0, tiled=True)

    swap = [(0, 1), (1, 0)]
    ring = [
        lax.ppermute(own_x, "scene", [(i, (i + d) % scenes) for i in range(scenes)])
        for d in range(1, scenes)
    ]

    table = call(
        functools.partial(table_kernel, targets=targets),
        shape((offsets, own_rows), I32),
    )(pair_in[0, 0], pair_out[0, 0])

    own, outbound = call(
        forward_kernel,
        (shape((own_rows, out_width), F32), shape((send_rows, out_width), F32)),
        scratch=(
            pltpu.VMEM((offsets * own_rows, 2 * out_width), BF16),
            pltpu.VMEM((LANES, offsets * own_rows), BF16),
        ),
    )(x, weight, table)

    returned, *ring = lax.optimization_barrier((returned, *ring))
    gathered = call(
        lookup_kernel,
        shape((offsets * out_width, own_rows), BF16),
        scratch=(pltpu.VMEM((out_width, targets), BF16), pltpu.VMEM((2, targets, STEP * LANES), BF16)),
    )(upstream, returned.reshape(send_rows, out_width), table)
    group_g = lax.all_to_all(gathered.reshape(group, columns, own_rows), GROUP, 0, 0, tiled=True)

    input_grad = call(
        input_grad_kernel,
        shape((own_rows, in_width), BF16),
        flops=10**9,
    )(weight, gathered)

    near = jnp.stack([x] + ring)
    other = lax.ppermute(near, "zl", swap)
    half = jnp.concatenate([near, other])
    far = lax.ppermute(half, "core", swap)
    packed = call(
        pack_kernel,
        shape((peers * 6, LANES), I32),
        scratch=(pltpu.VMEM((2, in_width, LANES), F32),),
        flops=2 * columns * in_width * own_rows * group,
        moved=peers * 6 * LANES * 8,
    )(group_g, half, far, outbound)
    arrived = lax.all_to_all(packed.reshape(peers, 1, 6 * LANES), SPACE, 0, 0, tiled=True)
    arrived = arrived.reshape(peers * 6, LANES)

    free = columns - LANES
    quarter = call(
        functools.partial(sum_kernel, free=free),
        shape((scenes, 16, LANES), F32),
        moved=peers * 6 * LANES * 4,
    )(arrived)
    blocks = lax.all_to_all(quarter, "scene", 0, 0, tiled=True)
    conv_out = call(
        functools.partial(receive_kernel, free=free),
        shape((own_rows, out_width), BF16),
        scratch=(pltpu.VMEM((send_rows, out_width), F32),),
        flops=4 * send_rows * own_rows * out_width,
        moved=send_rows * out_width * 4,
    )(own, arrived, recv)

    own_in = in_width // peers
    blocks = blocks.reshape(scenes, own_in, 2, 4, LANES).transpose(1, 3, 0, 2, 4)
    blocks = blocks.reshape(own_in, group, 2 * LANES)[:, :, :columns]
    kernel_grad = blocks.reshape(own_in, offsets, out_width)
    kernel_grad = kernel_grad.transpose(1, 0, 2).reshape(offsets, own_in * out_width)
    normalizer = 1.0 / math.sqrt(scenes * peers * own_rows)
    return (conv_out[None], input_grad[None], kernel_grad * normalizer)


def solution(mesh):
    scenes = mesh.devices.shape[1]
    fine = Mesh(mesh.devices.reshape(8, 4, 2, 2, scenes), ("y", "zh", "zl", "core", "scene"))
    voxels = P("scene", SPACE)
    return jax.shard_map(
        local,
        mesh=fine,
        in_specs=(voxels, voxels, voxels, P(), voxels, voxels, voxels),
        out_specs=(voxels, voxels, P(None, SPACE)),
        check_vma=False,
    )
```

```python
import functools
import math

import jax
import jax.numpy as jnp
from jax import lax
from jax.experimental import pallas as pl
from jax.experimental.pallas import tpu as pltpu
from jax.sharding import Mesh
from jax.sharding import PartitionSpec as P

F32 = jnp.float32
BF16 = jnp.bfloat16
I32 = jnp.int32
LANES = 128
STEP = 4
WORDS = 8
VMEM_BYTES = 24 * 1024 * 1024
MOST_VMEM = 64 * 1024 * 1024 - 128 * 1024
SPACE = ("y", "z", "core")
GROUP = ("core", "scene")


def call(kernel, outs, scratch=(), flops=0, moved=0, vmem=VMEM_BYTES, **specs):
    return pl.pallas_call(
        kernel,
        out_shape=outs,
        scratch_shapes=list(scratch),
        **specs,
        compiler_params=pltpu.CompilerParams(vmem_limit_bytes=vmem),
        cost_estimate=pl.CostEstimate(flops=flops, bytes_accessed=moved, transcendentals=0),
    )


def rows_iota(rows, start=0):
    return lax.broadcasted_iota(I32, (rows, LANES), 0) + start


def one_hot(iota, row):
    return jnp.where(iota == row, 1.0, 0.0).astype(BF16)


def split_two(value):
    high = value.astype(BF16)
    low = (value - high.astype(F32)).astype(BF16)
    return high, low


def lane_block(k):
    return slice(k * LANES, (k + 1) * LANES)


def gather_kernel(cot_any, mask_any, recv_any, up_ref, out_ref, cot_ref, mask_ref, recv_ref, sems):
    pairs = ((cot_any, cot_ref), (mask_any, mask_ref), (recv_any, recv_ref))
    copies = [pltpu.make_async_copy(a, b, sems.at[i]) for i, (a, b) in enumerate(pairs)]
    for copy in copies:
        copy.start()
    for copy in copies:
        copy.wait()
    up = (cot_ref[...].astype(F32) * mask_ref[...].astype(F32)).astype(BF16)
    up_ref[...] = up
    iota = rows_iota(LANES)
    for g in range(recv_ref.shape[0]):
        hot = one_hot(iota, recv_ref[g : g + 1, :])
        rows = lax.dot_general(hot, up, (((0,), (0,)), ((), ())), preferred_element_type=F32)
        out_ref[lane_block(g), :] = rows.astype(BF16)


def table_kernel(in_ref, out_ref, up_ref, table_ref, turned_ref, *, targets):
    turned_ref[...] = up_ref[...].T
    iota = rows_iota(LANES)
    picks = rows_iota(16)
    for k in range(in_ref.shape[0]):
        hot = one_hot(iota, in_ref[k : k + 1, :])
        target = out_ref[k : k + 1, :]
        code = jnp.where(target < targets, target + 1, 0)
        digits = jnp.where(picks == 0, code >> 7, jnp.where(picks == 1, code & 127, 0))
        found = lax.dot_general(
            digits.astype(F32).astype(BF16), hot, (((1,), (1,)), ((), ())), preferred_element_type=F32
        )
        table_ref[k : k + 1, :] = (found[0:1] * 128.0 + found[1:2] - 1.0).astype(I32)


def lookup_kernel(turned_ref, back_ref, table_ref, gathered_ref, ext_ref, hot_ref):
    blocks = back_ref.shape[0] // LANES
    offsets = table_ref.shape[0]
    ext_ref[:, 0:LANES] = turned_ref[...]
    for b in range(blocks):
        ext_ref[:, lane_block(b + 1)] = back_ref[lane_block(b), :].T
    iota = rows_iota((blocks + 1) * LANES)
    step = STEP
    for first in range(0, offsets, step):
        count = min(step, offsets - first)
        slot = (first // step) % 2
        for k in range(count):
            hot_ref[slot, :, lane_block(k)] = one_hot(iota, table_ref[first + k : first + k + 1, :])
        rows = jnp.dot(
            ext_ref[...], hot_ref[slot, :, : count * LANES], preferred_element_type=F32
        ).astype(BF16)
        for k in range(count):
            gathered_ref[lane_block(first + k), :] = rows[:, lane_block(k)]


def encode(value, top):
    level = jnp.ceil(jnp.log2(jnp.maximum(top, 1e-36)) * 8.0)
    code = jnp.round(value * jnp.exp2(level * -0.125) * 32767.0)
    return jnp.clip(code, -32767.0, 32767.0).astype(I32), level.astype(I32)


def unit(level):
    return jnp.exp2(level.astype(F32) * 0.125) * (1.0 / 32767.0)


def join(first, second):
    return (first << 16) | (second & 0xFFFF)


def halves(word):
    return (word >> 16).astype(F32), ((word << 16) >> 16).astype(F32)


def row_top(value):
    return jnp.max(jnp.abs(value), axis=1, keepdims=True)


def fetch(w_any, w_ref, sems):
    offsets = w_ref.shape[0]
    step = offsets // sems.shape[0]
    copies = []
    for i in range(sems.shape[0]):
        part = pl.ds(i * step, step)
        copies.append(pltpu.make_async_copy(w_any.at[part], w_ref.at[part], sems.at[i]))
        copies[-1].start()
    return copies, step


def input_grad_kernel(w_any, gathered_ref, grad_ref, w_ref, sems):
    copies, step = fetch(w_any, w_ref, sems)
    total = jnp.zeros((w_ref.shape[1], LANES), F32)
    for k in range(w_ref.shape[0]):
        if k % step == 0:
            copies[k // step].wait()
        total += jnp.dot(w_ref[k], gathered_ref[lane_block(k), :], preferred_element_type=F32)
    grad_ref[...] = total.T.astype(BF16)


def forward_kernel(
    x_ref, w_any, table_ref, own_ref, word_ref, w_ref, terms_ref, hot_ref, send_ref, sems, *, free
):
    offsets = w_ref.shape[0]
    copies, step = fetch(w_any, w_ref, sems)
    for k in range(offsets):
        if k % step == 0:
            copies[k // step].wait()
        high, low = split_two(jnp.dot(x_ref[...], w_ref[k], preferred_element_type=F32))
        terms_ref[lane_block(k), 0:LANES] = high
        terms_ref[lane_block(k), LANES : 2 * LANES] = low

    def block(start):
        here = rows_iota(LANES) + start
        for k in range(offsets):
            hot_ref[:, lane_block(k)] = one_hot(here, table_ref[k : k + 1, :])
        both = jnp.dot(hot_ref[...], terms_ref[...], preferred_element_type=F32)
        return both[:, :LANES] + both[:, LANES:]

    own_ref[...] = block(0)

    def scatter(b, carry):
        send_ref[pl.ds(pl.multiple_of(b * LANES, LANES), LANES), :] = block((b + 1) * LANES)
        return carry

    lax.fori_loop(0, send_ref.shape[0] // LANES, scatter, 0)
    peers = word_ref.shape[1]
    lane = lax.broadcasted_iota(I32, (peers, LANES), 1)
    levels = jnp.zeros((peers, LANES), I32)
    for r in range(4):
        words = []
        for slot in (r, r + 4):
            value = send_ref[pl.ds(slot, peers, stride=8), :]
            code, level = encode(value, row_top(value))
            words.append(code)
            levels = jnp.where(lane == free + slot, level, levels)
        word_ref[r] = join(*words)
    word_ref[4] = levels


def pack_kernel(g_ref, near_ref, far_ref, word_ref, out_ref, turn_ref):
    columns = g_ref.shape[1]
    peers = word_ref.shape[1]
    blocks = turn_ref.shape[0]
    scenes = near_ref.shape[0]
    core, scene = (lax.axis_index(axis) for axis in GROUP)
    total = jnp.zeros((columns, near_ref.shape[2]), F32)
    for s in range(g_ref.shape[0]):
        x_ref, holder = (near_ref, core) if s < scenes else (far_ref, 1 - core)
        sender = holder * scenes + lax.rem(scene + scenes - s % scenes, scenes)
        total += jnp.dot(g_ref[sender], x_ref[s % scenes], preferred_element_type=F32)
    rest = blocks * LANES - columns
    total = jnp.concatenate([total, jnp.zeros((rest, total.shape[1]), F32)], axis=0)
    for h in range(blocks):
        turn_ref[h] = total[lane_block(h), :].T
    for r in range(4):
        out_ref[pl.ds(r, peers, stride=WORDS), :] = word_ref[r]
    parts = [[turn_ref[h, pl.ds(c, peers, stride=2), :] for c in range(2)] for h in range(blocks)]
    top = functools.reduce(jnp.maximum, [jnp.abs(part) for pair in parts for part in pair])
    top = jnp.max(top, axis=1, keepdims=True)
    free = LANES - rest
    lane = lax.broadcasted_iota(I32, (peers, LANES), 1)
    for h in range(blocks):
        codes = [encode(part, top) for part in parts[h]]
        word = join(codes[0][0], codes[1][0])
        if h == blocks - 1:
            levels = jnp.where(lane == free + 8, codes[0][1], word_ref[4])
            word = jnp.where(lane < free, word, levels)
        out_ref[pl.ds(4 + h, peers, stride=WORDS), :] = word


def sum_kernel(arrived_ref, out_ref, *, free):
    peers = arrived_ref.shape[0] // WORDS
    words = [arrived_ref[pl.ds(4 + h, peers, stride=WORDS), :] for h in range(4)]
    scale = unit(words[-1][:, free + 8 : free + 9])
    for h in range(4):
        for c, value in enumerate(halves(words[h])):
            total = (value * scale).reshape(peers // 8, 8, LANES).sum(axis=0)
            total = (total[0:2] + total[2:4]) + (total[4:6] + total[6:8])
            row = 2 * (4 * c + h)
            for s in range(out_ref.shape[0]):
                out_ref[s, row : row + 2, :] = total


def receive_kernel(own_ref, arrived_ref, recv_ref, out_ref, rows_ref, *, free):
    peers = arrived_ref.shape[0] // WORDS
    iota = rows_iota(LANES)
    levels = arrived_ref[pl.ds(WORDS - 1, peers, stride=WORDS), :]
    for r in range(4):
        pair = halves(arrived_ref[pl.ds(r, peers, stride=WORDS), :])
        for value, slot in zip(pair, (r, r + 4)):
            scale = unit(levels[:, free + slot : free + slot + 1])
            rows_ref[pl.ds(slot, peers, stride=8), :] = value * scale
    total = own_ref[...]
    for g in range(recv_ref.shape[0]):
        hot = one_hot(iota, recv_ref[g : g + 1, :])
        high, low = split_two(rows_ref[lane_block(g), :])
        total += jnp.dot(hot, high, preferred_element_type=F32)
        total += jnp.dot(hot, low, preferred_element_type=F32)
    out_ref[...] = total.astype(BF16)


def local(features, cotangent, relu_mask, weight, pair_in, pair_out, recv_index):
    x = features[0]
    own_rows, in_width = x.shape
    offsets, unused, out_width = weight.shape
    peers = lax.axis_size(SPACE)
    group = lax.axis_size(GROUP)
    scenes = lax.axis_size("scene")
    send_rows = recv_index.shape[2]
    slots = send_rows // peers
    targets = own_rows + send_rows
    columns = offsets * out_width // group
    recv = recv_index.reshape(send_rows // LANES, LANES)
    shape = jax.ShapeDtypeStruct

    hbm = pl.BlockSpec(memory_space=pltpu.HBM)
    vmem = pl.BlockSpec(memory_space=pltpu.VMEM)
    weights = (pltpu.VMEM(weight.shape, BF16), pltpu.SemaphoreType.DMA((3,)))
    blocks = -(-columns // LANES)
    free = columns - (blocks - 1) * LANES

    upstream, outgoing = call(
        gather_kernel,
        (shape((own_rows, out_width), BF16), shape((send_rows, out_width), BF16)),
        scratch=(
            pltpu.VMEM((own_rows, out_width), BF16),
            pltpu.VMEM((own_rows, out_width), I32),
            pltpu.VMEM(recv.shape, I32),
            pltpu.SemaphoreType.DMA((3,)),
        ),
        in_specs=[hbm] * 3,
        vmem=MOST_VMEM,
        flops=2 * send_rows * own_rows * out_width,
        moved=send_rows * out_width * 3,
    )(cotangent[0], relu_mask[0], recv)
    own_x, outgoing = lax.optimization_barrier((x, outgoing))
    returned = lax.all_to_all(outgoing.reshape(peers, slots, out_width), SPACE, 0, 0, tiled=True)

    swap = [(0, 1), (1, 0)]
    ring = [
        lax.ppermute(own_x, "scene", [(i, (i + d) % scenes) for i in range(scenes)])
        for d in range(1, scenes)
    ]

    table, turned = call(
        functools.partial(table_kernel, targets=targets),
        (shape((offsets, own_rows), I32), shape((out_width, own_rows), BF16)),
    )(pair_in[0, 0], pair_out[0, 0], upstream)

    own, words = call(
        functools.partial(forward_kernel, free=free),
        (
            shape((own_rows, out_width), F32),
            shape((5, peers, out_width), I32),
        ),
        scratch=(
            weights[0],
            pltpu.VMEM((offsets * own_rows, 2 * out_width), BF16),
            pltpu.VMEM((LANES, offsets * own_rows), BF16),
            pltpu.VMEM((send_rows, out_width), F32),
            weights[1],
        ),
        in_specs=[vmem, hbm, vmem],
    )(x, weight, table)

    returned, *ring = lax.optimization_barrier((returned, *ring))
    gathered = call(
        lookup_kernel,
        shape((offsets * out_width, own_rows), BF16),
        scratch=(pltpu.VMEM((out_width, targets), BF16), pltpu.VMEM((2, targets, STEP * LANES), BF16)),
    )(turned, returned.reshape(send_rows, out_width), table)
    group_g = lax.all_to_all(gathered.reshape(group, columns, own_rows), GROUP, 0, 0, tiled=True)

    input_grad = call(
        input_grad_kernel,
        shape((own_rows, in_width), BF16),
        scratch=weights,
        in_specs=[hbm, vmem],
        flops=10**9,
    )(weight, gathered)

    near = jnp.stack([x] + ring)
    far = lax.ppermute(near, "core", swap)
    packed = call(
        pack_kernel,
        shape((peers * WORDS, LANES), I32),
        scratch=(pltpu.VMEM((blocks, in_width, LANES), F32),),
        flops=2 * columns * in_width * own_rows * group,
        moved=peers * WORDS * LANES * 8,
    )(group_g, near, far, words)
    arrived = lax.all_to_all(packed.reshape(peers, WORDS, LANES), SPACE, 0, 0, tiled=True)
    arrived = arrived.reshape(peers * WORDS, LANES)

    quarter = call(
        functools.partial(sum_kernel, free=free),
        shape((scenes, 16, LANES), F32),
        moved=peers * WORDS * LANES * 4,
    )(arrived)
    sums = lax.all_to_all(quarter, "scene", 0, 0, tiled=True)
    conv_out = call(
        functools.partial(receive_kernel, free=free),
        shape((own_rows, out_width), BF16),
        scratch=(pltpu.VMEM((send_rows, out_width), F32),),
        flops=4 * send_rows * own_rows * out_width,
        moved=send_rows * out_width * 4,
    )(own, arrived, recv)

    own_in = in_width // peers
    sums = sums.reshape(scenes, own_in, blocks, 2, LANES).transpose(1, 3, 0, 2, 4)
    sums = sums.reshape(own_in, group, blocks * LANES)[:, :, :columns]
    kernel_grad = sums.reshape(own_in, offsets, out_width)
    kernel_grad = kernel_grad.transpose(1, 0, 2).reshape(offsets, own_in * out_width)
    normalizer = 1.0 / math.sqrt(scenes * peers * own_rows)
    return (conv_out[None], input_grad[None], kernel_grad * normalizer)


def solution(mesh):
    scenes = mesh.devices.shape[1]
    fine = Mesh(mesh.devices.reshape(8, 8, 2, scenes), ("y", "z", "core", "scene"))
    voxels = P("scene", SPACE)
    return jax.shard_map(
        local,
        mesh=fine,
        in_specs=(voxels, voxels, voxels, P(), voxels, voxels, voxels),
        out_specs=(voxels, voxels, P(None, SPACE)),
        check_vma=False,
    )
```

```python
import functools
import math

import jax
import jax.numpy as jnp
from jax import lax
from jax.experimental import pallas as pl
from jax.experimental.pallas import tpu as pltpu
from jax.sharding import Mesh
from jax.sharding import PartitionSpec as P

F32 = jnp.float32
BF16 = jnp.bfloat16
I32 = jnp.int32
LANES = 128
STEP = 4
WORDS = 8
VMEM_BYTES = 24 * 1024 * 1024
MOST_VMEM = 64 * 1024 * 1024 - 128 * 1024
SPACE = ("y", "z", "core")
GROUP = ("core", "scene")


def call(kernel, outs, scratch=(), flops=0, moved=0, vmem=VMEM_BYTES, **specs):
    return pl.pallas_call(
        kernel,
        out_shape=outs,
        scratch_shapes=list(scratch),
        **specs,
        compiler_params=pltpu.CompilerParams(vmem_limit_bytes=vmem),
        cost_estimate=pl.CostEstimate(flops=flops, bytes_accessed=moved, transcendentals=0),
    )


def rows_iota(rows, start=0):
    return lax.broadcasted_iota(I32, (rows, LANES), 0) + start


def one_hot(iota, row):
    return jnp.where(iota == row, 1.0, 0.0).astype(BF16)


def one_hot_16(iota, row):
    rows = iota.shape[0]
    narrow = jnp.broadcast_to(row, (16, LANES)).astype(jnp.int16)
    narrow = jnp.concatenate([narrow] * (rows // 16), axis=0)
    return jnp.where(iota == narrow, jnp.ones((rows, LANES), BF16), jnp.zeros((rows, LANES), BF16))


def split_two(value):
    high = value.astype(BF16)
    low = (value - high.astype(F32)).astype(BF16)
    return high, low


def lane_block(k):
    return slice(k * LANES, (k + 1) * LANES)


def gather_kernel(cot_any, mask_any, recv_any, up_ref, out_any, cot_ref, mask_ref, recv_ref, out_ref, sems, out_sems):
    pairs = ((cot_any, cot_ref), (mask_any, mask_ref), (recv_any, recv_ref))
    copies = [pltpu.make_async_copy(a, b, sems.at[i]) for i, (a, b) in enumerate(pairs)]
    for copy in copies:
        copy.start()
    for copy in copies:
        copy.wait()
    up = (cot_ref[...].astype(F32) * mask_ref[...].astype(F32)).astype(BF16)
    up_ref[...] = up
    iota = rows_iota(LANES)
    copies = []
    for g in range(recv_ref.shape[0]):
        hot = one_hot(iota, recv_ref[g : g + 1, :])
        rows = lax.dot_general(hot, up, (((0,), (0,)), ((), ())), preferred_element_type=F32)
        out_ref[lane_block(g), :] = rows.astype(BF16)
        part = pl.ds(g * LANES, LANES)
        copies.append(pltpu.make_async_copy(out_ref.at[part], out_any.at[part], out_sems.at[g]))
        copies[-1].start()
    for copy in copies:
        copy.wait()


def table_kernel(in_ref, out_ref, up_ref, table_ref, turned_ref, *, targets):
    turned_ref[...] = up_ref[...].T
    iota = rows_iota(LANES)
    picks = rows_iota(16)
    for k in range(in_ref.shape[0]):
        hot = one_hot(iota, in_ref[k : k + 1, :])
        target = out_ref[k : k + 1, :]
        code = jnp.where(target < targets, target + 1, 0)
        digits = jnp.where(picks == 0, code >> 7, jnp.where(picks == 1, code & 127, 0))
        found = lax.dot_general(
            digits.astype(F32).astype(BF16), hot, (((1,), (1,)), ((), ())), preferred_element_type=F32
        )
        table_ref[k : k + 1, :] = (found[0:1] * 128.0 + found[1:2] - 1.0).astype(I32)


def lookup_kernel(turned_ref, back_ref, table_ref, gathered_any, ext_ref, hot_ref, gathered_ref, sems):
    blocks = back_ref.shape[0] // LANES
    offsets = table_ref.shape[0]
    ext_ref[:, 0:LANES] = turned_ref[...]
    for b in range(blocks):
        ext_ref[:, lane_block(b + 1)] = back_ref[lane_block(b), :].T
    iota = rows_iota((blocks + 1) * LANES).astype(jnp.int16)
    copies = []
    for first in range(0, offsets, STEP):
        count = min(STEP, offsets - first)
        slot = (first // STEP) % 2
        for k in range(count):
            hot_ref[slot, :, lane_block(k)] = one_hot_16(iota, table_ref[first + k : first + k + 1, :])
        rows = jnp.dot(
            ext_ref[...], hot_ref[slot, :, : count * LANES], preferred_element_type=F32
        ).astype(BF16)
        for k in range(count):
            gathered_ref[lane_block(first + k), :] = rows[:, lane_block(k)]
        part = pl.ds(first * LANES, count * LANES)
        copies.append(
            pltpu.make_async_copy(gathered_ref.at[part], gathered_any.at[part], sems.at[first // STEP])
        )
        copies[-1].start()
    for copy in copies:
        copy.wait()


def encode(value, top):
    level = jnp.ceil(jnp.log2(jnp.maximum(top, 1e-36)) * 8.0)
    code = jnp.round(value * jnp.exp2(level * -0.125) * 32767.0)
    return jnp.clip(code, -32767.0, 32767.0).astype(I32), level.astype(I32)


def unit(level):
    return jnp.exp2(level.astype(F32) * 0.125) * (1.0 / 32767.0)


def join(first, second):
    return (first << 16) | (second & 0xFFFF)


def halves(word):
    return (word >> 16).astype(F32), ((word << 16) >> 16).astype(F32)


def row_top(value):
    return jnp.max(jnp.abs(value), axis=1, keepdims=True)


def fetch(w_any, w_ref, gathered_any, gathered_ref, sems):
    offsets = w_ref.shape[0]
    parts = sems.shape[1]
    step = offsets // parts
    copies = []
    for i in range(parts):
        part = pl.ds(i * step, step)
        rows = pl.ds(i * step * LANES, step * LANES)
        copies.append(
            (
                pltpu.make_async_copy(w_any.at[part], w_ref.at[part], sems.at[0, i]),
                pltpu.make_async_copy(gathered_any.at[rows], gathered_ref.at[rows], sems.at[1, i]),
            )
        )
        for copy in copies[-1]:
            copy.start()
    return copies, step


def forward_kernel(
    x_ref,
    w_any,
    table_ref,
    gathered_any,
    own_ref,
    word_ref,
    grad_ref,
    w_ref,
    gathered_ref,
    terms_ref,
    hot_ref,
    send_ref,
    sems,
    *,
    free,
):
    offsets = w_ref.shape[0]
    copies, step = fetch(w_any, w_ref, gathered_any, gathered_ref, sems)
    total = jnp.zeros((w_ref.shape[1], LANES), F32)
    for k in range(offsets):
        if k % step == 0:
            for copy in copies[k // step]:
                copy.wait()
        high, low = split_two(jnp.dot(x_ref[...], w_ref[k], preferred_element_type=F32))
        terms_ref[lane_block(k), 0:LANES] = high
        terms_ref[lane_block(k), LANES : 2 * LANES] = low
        total += jnp.dot(w_ref[k], gathered_ref[lane_block(k), :], preferred_element_type=F32)
    grad_ref[...] = total.T.astype(BF16)
    iota = rows_iota(LANES).astype(jnp.int16)

    def block(start):
        for k in range(offsets):
            hot_ref[:, lane_block(k)] = one_hot_16(iota, table_ref[k : k + 1, :] - start)
        both = jnp.dot(hot_ref[...], terms_ref[...], preferred_element_type=F32)
        return both[:, :LANES] + both[:, LANES:]

    own_ref[...] = block(0)

    def scatter(b, carry):
        send_ref[pl.ds(pl.multiple_of(b * LANES, LANES), LANES), :] = block((b + 1) * LANES)
        return carry

    lax.fori_loop(0, send_ref.shape[0] // LANES, scatter, 0)
    peers = word_ref.shape[1]
    lane = lax.broadcasted_iota(I32, (peers, LANES), 1)
    levels = jnp.zeros((peers, LANES), I32)
    for r in range(4):
        words = []
        for slot in (r, r + 4):
            value = send_ref[pl.ds(slot, peers, stride=8), :]
            code, level = encode(value, row_top(value))
            words.append(code)
            levels = jnp.where(lane == free + slot, level, levels)
        word_ref[r] = join(*words)
    word_ref[4] = levels


def pack_kernel(g_ref, near_ref, far_ref, word_ref, out_ref, turn_ref):
    columns = g_ref.shape[1]
    peers = word_ref.shape[1]
    blocks = turn_ref.shape[0]
    scenes = near_ref.shape[0]
    core, scene = (lax.axis_index(axis) for axis in GROUP)
    total = jnp.zeros((columns, near_ref.shape[2]), F32)
    for s in range(g_ref.shape[0]):
        x_ref, holder = (near_ref, core) if s < scenes else (far_ref, 1 - core)
        sender = holder * scenes + lax.rem(scene + scenes - s % scenes, scenes)
        total += jnp.dot(g_ref[sender], x_ref[s % scenes], preferred_element_type=F32)
    rest = blocks * LANES - columns
    total = jnp.concatenate([total, jnp.zeros((rest, total.shape[1]), F32)], axis=0)
    for h in range(blocks):
        turn_ref[h] = total[lane_block(h), :].T
    for r in range(4):
        out_ref[pl.ds(r, peers, stride=WORDS), :] = word_ref[r]
    parts = [[turn_ref[h, pl.ds(c, peers, stride=2), :] for c in range(2)] for h in range(blocks)]
    top = functools.reduce(jnp.maximum, [jnp.abs(part) for pair in parts for part in pair])
    top = jnp.max(top, axis=1, keepdims=True)
    free = LANES - rest
    lane = lax.broadcasted_iota(I32, (peers, LANES), 1)
    for h in range(blocks):
        codes = [encode(part, top) for part in parts[h]]
        word = join(codes[0][0], codes[1][0])
        if h == blocks - 1:
            levels = jnp.where(lane == free + 8, codes[0][1], word_ref[4])
            word = jnp.where(lane < free, word, levels)
        out_ref[pl.ds(4 + h, peers, stride=WORDS), :] = word


def sum_kernel(arrived_ref, out_ref, *, free):
    peers = arrived_ref.shape[0] // WORDS
    words = [arrived_ref[pl.ds(4 + h, peers, stride=WORDS), :] for h in range(4)]
    scale = unit(words[-1][:, free + 8 : free + 9])
    for h in range(4):
        for c, value in enumerate(halves(words[h])):
            total = (value * scale).reshape(peers // 8, 8, LANES).sum(axis=0)
            total = (total[0:2] + total[2:4]) + (total[4:6] + total[6:8])
            row = 2 * (4 * c + h)
            for s in range(out_ref.shape[0]):
                out_ref[s, row : row + 2, :] = total


def receive_kernel(own_ref, arrived_ref, recv_ref, out_ref, rows_ref, *, free):
    peers = arrived_ref.shape[0] // WORDS
    iota = rows_iota(LANES)
    levels = arrived_ref[pl.ds(WORDS - 1, peers, stride=WORDS), :]
    for r in range(4):
        pair = halves(arrived_ref[pl.ds(r, peers, stride=WORDS), :])
        for value, slot in zip(pair, (r, r + 4)):
            scale = unit(levels[:, free + slot : free + slot + 1])
            rows_ref[pl.ds(slot, peers, stride=8), :] = value * scale
    total = own_ref[...]
    for g in range(recv_ref.shape[0]):
        hot = one_hot(iota, recv_ref[g : g + 1, :])
        high, low = split_two(rows_ref[lane_block(g), :])
        total += jnp.dot(hot, high, preferred_element_type=F32)
        total += jnp.dot(hot, low, preferred_element_type=F32)
    out_ref[...] = total.astype(BF16)


def local(features, cotangent, relu_mask, weight, pair_in, pair_out, recv_index):
    x = features[0]
    own_rows, in_width = x.shape
    offsets, unused, out_width = weight.shape
    peers = lax.axis_size(SPACE)
    group = lax.axis_size(GROUP)
    scenes = lax.axis_size("scene")
    send_rows = recv_index.shape[2]
    slots = send_rows // peers
    targets = own_rows + send_rows
    columns = offsets * out_width // group
    recv = recv_index.reshape(send_rows // LANES, LANES)
    shape = jax.ShapeDtypeStruct

    hbm = pl.BlockSpec(memory_space=pltpu.HBM)
    vmem = pl.BlockSpec(memory_space=pltpu.VMEM)
    blocks = -(-columns // LANES)
    free = columns - (blocks - 1) * LANES

    upstream, outgoing = call(
        gather_kernel,
        (shape((own_rows, out_width), BF16), shape((send_rows, out_width), BF16)),
        scratch=(
            pltpu.VMEM((own_rows, out_width), BF16),
            pltpu.VMEM((own_rows, out_width), I32),
            pltpu.VMEM(recv.shape, I32),
            pltpu.VMEM((send_rows, out_width), BF16),
            pltpu.SemaphoreType.DMA((3,)),
            pltpu.SemaphoreType.DMA(recv.shape[:1]),
        ),
        in_specs=[hbm] * 3,
        out_specs=(vmem, hbm),
        vmem=MOST_VMEM,
        flops=2 * send_rows * own_rows * out_width,
        moved=send_rows * out_width * 3,
    )(cotangent[0], relu_mask[0], recv)
    own_x, outgoing = lax.optimization_barrier((x, outgoing))
    returned = lax.all_to_all(outgoing.reshape(peers, slots, out_width), SPACE, 0, 0, tiled=True)

    swap = [(0, 1), (1, 0)]
    ring = [
        lax.ppermute(own_x, "scene", [(i, (i + d) % scenes) for i in range(scenes)])
        for d in range(1, scenes)
    ]

    table, turned = call(
        functools.partial(table_kernel, targets=targets),
        (shape((offsets, own_rows), I32), shape((out_width, own_rows), BF16)),
    )(pair_in[0, 0], pair_out[0, 0], upstream)

    returned, *ring = lax.optimization_barrier((returned, *ring))
    gathered = call(
        lookup_kernel,
        shape((offsets * out_width, own_rows), BF16),
        scratch=(
            pltpu.VMEM((out_width, targets), BF16),
            pltpu.VMEM((2, targets, STEP * LANES), BF16),
            pltpu.VMEM((offsets * out_width, own_rows), BF16),
            pltpu.SemaphoreType.DMA((-(-offsets // STEP),)),
        ),
        out_specs=hbm,
    )(turned, returned.reshape(send_rows, out_width), table)
    group_g = lax.all_to_all(gathered.reshape(group, columns, own_rows), GROUP, 0, 0, tiled=True)

    own, words, input_grad = call(
        functools.partial(forward_kernel, free=free),
        (
            shape((own_rows, out_width), F32),
            shape((5, peers, out_width), I32),
            shape((own_rows, in_width), BF16),
        ),
        scratch=(
            pltpu.VMEM(weight.shape, BF16),
            pltpu.VMEM((offsets * out_width, own_rows), BF16),
            pltpu.VMEM((offsets * own_rows, 2 * out_width), BF16),
            pltpu.VMEM((LANES, offsets * own_rows), BF16),
            pltpu.VMEM((send_rows, out_width), F32),
            pltpu.SemaphoreType.DMA((2, 3)),
        ),
        in_specs=[vmem, hbm, vmem, hbm],
    )(x, weight, table, gathered)

    near = jnp.stack([x] + ring)
    far = lax.ppermute(near, "core", swap)
    packed = call(
        pack_kernel,
        shape((peers * WORDS, LANES), I32),
        scratch=(pltpu.VMEM((blocks, in_width, LANES), F32),),
        flops=2 * columns * in_width * own_rows * group,
        moved=peers * WORDS * LANES * 8,
    )(group_g, near, far, words)
    arrived = lax.all_to_all(packed.reshape(peers, WORDS, LANES), SPACE, 0, 0, tiled=True)
    arrived = arrived.reshape(peers * WORDS, LANES)

    quarter = call(
        functools.partial(sum_kernel, free=free),
        shape((scenes, 16, LANES), F32),
        moved=peers * WORDS * LANES * 4,
    )(arrived)
    sums = lax.all_to_all(quarter, "scene", 0, 0, tiled=True)
    conv_out = call(
        functools.partial(receive_kernel, free=free),
        shape((own_rows, out_width), BF16),
        scratch=(pltpu.VMEM((send_rows, out_width), F32),),
        flops=4 * send_rows * own_rows * out_width,
        moved=send_rows * out_width * 4,
    )(own, arrived, recv)

    own_in = in_width // peers
    sums = sums.reshape(scenes, own_in, blocks, 2, LANES).transpose(1, 3, 0, 2, 4)
    sums = sums.reshape(own_in, group, blocks * LANES)[:, :, :columns]
    kernel_grad = sums.reshape(own_in, offsets, out_width)
    kernel_grad = kernel_grad.transpose(1, 0, 2).reshape(offsets, own_in * out_width)
    normalizer = 1.0 / math.sqrt(scenes * peers * own_rows)
    return (conv_out[None], input_grad[None], kernel_grad * normalizer)


def solution(mesh):
    scenes = mesh.devices.shape[1]
    fine = Mesh(mesh.devices.reshape(8, 8, 2, scenes), ("y", "z", "core", "scene"))
    voxels = P("scene", SPACE)
    return jax.shard_map(
        local,
        mesh=fine,
        in_specs=(voxels, voxels, voxels, P(), voxels, voxels, voxels),
        out_specs=(voxels, voxels, P(None, SPACE)),
        check_vma=False,
    )
```

```python
import functools
import math

import jax
import jax.numpy as jnp
from jax import lax
from jax.experimental import pallas as pl
from jax.experimental.pallas import tpu as pltpu
from jax.sharding import Mesh
from jax.sharding import PartitionSpec as P

F32 = jnp.float32
BF16 = jnp.bfloat16
I32 = jnp.int32
LANES = 128
STEP = 4
WORDS = 8
VMEM_BYTES = 24 * 1024 * 1024
MOST_VMEM = 64 * 1024 * 1024 - 128 * 1024
SPACE = ("y", "z", "core")
GROUP = ("core", "scene")


def call(kernel, outs, scratch=(), flops=0, moved=0, vmem=VMEM_BYTES, **specs):
    return pl.pallas_call(
        kernel,
        out_shape=outs,
        scratch_shapes=list(scratch),
        **specs,
        compiler_params=pltpu.CompilerParams(vmem_limit_bytes=vmem),
        cost_estimate=pl.CostEstimate(flops=flops, bytes_accessed=moved, transcendentals=0),
    )


def rows_iota(rows, start=0):
    return lax.broadcasted_iota(I32, (rows, LANES), 0) + start


def one_hot(iota, row):
    return jnp.where(iota == row, 1.0, 0.0).astype(BF16)


def one_hot_16(iota, row):
    rows = iota.shape[0]
    narrow = jnp.broadcast_to(row, (16, LANES)).astype(jnp.int16)
    narrow = jnp.concatenate([narrow] * (rows // 16), axis=0)
    return jnp.where(iota == narrow, jnp.ones((rows, LANES), BF16), jnp.zeros((rows, LANES), BF16))


def split_two(value):
    high = value.astype(BF16)
    low = (value - high.astype(F32)).astype(BF16)
    return high, low


def lane_block(k):
    return slice(k * LANES, (k + 1) * LANES)


def gather_kernel(cot_any, mask_any, recv_any, up_ref, out_ref, cot_ref, mask_ref, recv_ref, sems):
    pairs = ((cot_any, cot_ref), (mask_any, mask_ref), (recv_any, recv_ref))
    copies = [pltpu.make_async_copy(a, b, sems.at[i]) for i, (a, b) in enumerate(pairs)]
    for copy in copies:
        copy.start()
    for copy in copies:
        copy.wait()
    up = (cot_ref[...].astype(F32) * mask_ref[...].astype(F32)).astype(BF16)
    up_ref[...] = up
    iota = rows_iota(LANES)
    for g in range(recv_ref.shape[0]):
        hot = one_hot(iota, recv_ref[g : g + 1, :])
        rows = lax.dot_general(hot, up, (((0,), (0,)), ((), ())), preferred_element_type=F32)
        out_ref[lane_block(g), :] = rows.astype(BF16)


def table_kernel(in_ref, out_ref, up_ref, table_ref, turned_ref, *, targets):
    turned_ref[...] = up_ref[...].T
    iota = rows_iota(LANES)
    picks = rows_iota(16)
    for k in range(in_ref.shape[0]):
        hot = one_hot(iota, in_ref[k : k + 1, :])
        target = out_ref[k : k + 1, :]
        code = jnp.where(target < targets, target + 1, 0)
        digits = jnp.where(picks == 0, code >> 7, jnp.where(picks == 1, code & 127, 0))
        found = lax.dot_general(
            digits.astype(F32).astype(BF16), hot, (((1,), (1,)), ((), ())), preferred_element_type=F32
        )
        table_ref[k : k + 1, :] = (found[0:1] * 128.0 + found[1:2] - 1.0).astype(I32)


def lookup_kernel(turned_ref, back_ref, table_ref, gathered_any, ext_ref, hot_ref, gathered_ref, sems):
    blocks = back_ref.shape[0] // LANES
    offsets = table_ref.shape[0]
    ext_ref[:, 0:LANES] = turned_ref[...]
    for b in range(blocks):
        ext_ref[:, lane_block(b + 1)] = back_ref[lane_block(b), :].T
    iota = rows_iota((blocks + 1) * LANES).astype(jnp.int16)
    copies = []
    for first in range(0, offsets, STEP):
        count = min(STEP, offsets - first)
        slot = (first // STEP) % 2
        for k in range(count):
            hot_ref[slot, :, lane_block(k)] = one_hot_16(iota, table_ref[first + k : first + k + 1, :])
        rows = jnp.dot(
            ext_ref[...], hot_ref[slot, :, : count * LANES], preferred_element_type=F32
        ).astype(BF16)
        for k in range(count):
            gathered_ref[lane_block(first + k), :] = rows[:, lane_block(k)]
        part = pl.ds(first * LANES, count * LANES)
        copies.append(
            pltpu.make_async_copy(gathered_ref.at[part], gathered_any.at[part], sems.at[first // STEP])
        )
        copies[-1].start()
    for copy in copies:
        copy.wait()


def encode(value, top):
    level = jnp.ceil(jnp.log2(jnp.maximum(top, 1e-36)) * 8.0)
    code = jnp.round(value * jnp.exp2(level * -0.125) * 32767.0)
    return jnp.clip(code, -32767.0, 32767.0).astype(I32), level.astype(I32)


def unit(level):
    return jnp.exp2(level.astype(F32) * 0.125) * (1.0 / 32767.0)


def join(first, second):
    return (first << 16) | (second & 0xFFFF)


def halves(word):
    return (word >> 16).astype(F32), ((word << 16) >> 16).astype(F32)


def row_top(value):
    return jnp.max(jnp.abs(value), axis=1, keepdims=True)


def fetch(w_any, w_ref, gathered_any, gathered_ref, sems):
    offsets = w_ref.shape[0]
    parts = sems.shape[1]
    step = offsets // parts
    copies = []
    for i in range(parts):
        part = pl.ds(i * step, step)
        rows = pl.ds(i * step * LANES, step * LANES)
        copies.append(
            (
                pltpu.make_async_copy(w_any.at[part], w_ref.at[part], sems.at[0, i]),
                pltpu.make_async_copy(gathered_any.at[rows], gathered_ref.at[rows], sems.at[1, i]),
            )
        )
        for copy in copies[-1]:
            copy.start()
    return copies, step


def forward_kernel(
    near_ref,
    w_any,
    table_ref,
    gathered_any,
    own_any,
    word_ref,
    grad_ref,
    w_ref,
    gathered_ref,
    terms_ref,
    hot_ref,
    send_ref,
    sems,
    own_sem,
    *,
    free,
):
    offsets = w_ref.shape[0]
    copies, step = fetch(w_any, w_ref, gathered_any, gathered_ref, sems)
    total = jnp.zeros((w_ref.shape[1], LANES), F32)
    for k in range(offsets):
        if k % step == 0:
            for copy in copies[k // step]:
                copy.wait()
        high, low = split_two(jnp.dot(near_ref[0], w_ref[k], preferred_element_type=F32))
        terms_ref[lane_block(k), 0:LANES] = high
        terms_ref[lane_block(k), LANES : 2 * LANES] = low
        total += jnp.dot(w_ref[k], gathered_ref[lane_block(k), :], preferred_element_type=F32)
    grad_ref[...] = total.T.astype(BF16)
    iota = rows_iota(LANES).astype(jnp.int16)

    span = hot_ref.shape[1]
    own_rows = own_any.shape[0]
    own_copy = pltpu.make_async_copy(send_ref.at[pl.ds(0, own_rows)], own_any, own_sem)
    for i in range(send_ref.shape[0] // span):
        for j in range(span // LANES):
            for k in range(offsets):
                row = table_ref[k : k + 1, :] - (i * span + j * LANES)
                hot_ref[i % 2, lane_block(j), lane_block(k)] = one_hot_16(iota, row)
        both = jnp.dot(hot_ref[i % 2], terms_ref[...], preferred_element_type=F32)
        send_ref[pl.ds(i * span, span), :] = both[:, :LANES] + both[:, LANES:]
        if i == 0:
            own_copy.start()
    peers = word_ref.shape[1]
    lane = lax.broadcasted_iota(I32, (peers, LANES), 1)
    levels = jnp.zeros((peers, LANES), I32)
    for r in range(4):
        words = []
        for slot in (r, r + 4):
            value = send_ref[pl.ds(own_rows + slot, peers, stride=8), :]
            code, level = encode(value, row_top(value))
            words.append(code)
            levels = jnp.where(lane == free + slot, level, levels)
        word_ref[r] = join(*words)
    word_ref[4] = levels
    own_copy.wait()


def pack_kernel(g_ref, near_ref, far_ref, word_ref, out_ref, turn_ref):
    columns = g_ref.shape[1]
    peers = word_ref.shape[1]
    blocks = turn_ref.shape[0]
    scenes = near_ref.shape[0]
    core, scene = (lax.axis_index(axis) for axis in GROUP)
    total = jnp.zeros((columns, near_ref.shape[2]), F32)
    for s in range(g_ref.shape[0]):
        x_ref, holder = (near_ref, core) if s < scenes else (far_ref, 1 - core)
        sender = holder * scenes + (scene ^ (s % scenes))
        total += jnp.dot(g_ref[sender], x_ref[s % scenes], preferred_element_type=F32)
    rest = blocks * LANES - columns
    total = jnp.concatenate([total, jnp.zeros((rest, total.shape[1]), F32)], axis=0)
    for h in range(blocks):
        turn_ref[h] = total[lane_block(h), :].T
    for r in range(4):
        out_ref[pl.ds(r, peers, stride=WORDS), :] = word_ref[r]
    parts = [[turn_ref[h, pl.ds(c, peers, stride=2), :] for c in range(2)] for h in range(blocks)]
    top = functools.reduce(jnp.maximum, [jnp.abs(part) for pair in parts for part in pair])
    top = jnp.max(top, axis=1, keepdims=True)
    free = LANES - rest
    lane = lax.broadcasted_iota(I32, (peers, LANES), 1)
    for h in range(blocks):
        codes = [encode(part, top) for part in parts[h]]
        word = join(codes[0][0], codes[1][0])
        if h == blocks - 1:
            levels = jnp.where(lane == free + 8, codes[0][1], word_ref[4])
            word = jnp.where(lane < free, word, levels)
        out_ref[pl.ds(4 + h, peers, stride=WORDS), :] = word


def sum_kernel(arrived_ref, out_ref, *, free):
    peers = arrived_ref.shape[0] // WORDS
    words = [arrived_ref[pl.ds(4 + h, peers, stride=WORDS), :] for h in range(4)]
    scale = unit(words[-1][:, free + 8 : free + 9])
    for h in range(4):
        for c, value in enumerate(halves(words[h])):
            total = (value * scale).reshape(peers // 8, 8, LANES).sum(axis=0)
            total = (total[0:2] + total[2:4]) + (total[4:6] + total[6:8])
            row = 2 * (4 * c + h)
            for s in range(out_ref.shape[0]):
                out_ref[s, row : row + 2, :] = total


def receive_kernel(own_ref, arrived_ref, recv_ref, out_ref, rows_ref, *, free):
    peers = arrived_ref.shape[0] // WORDS
    iota = rows_iota(LANES)
    levels = arrived_ref[pl.ds(WORDS - 1, peers, stride=WORDS), :]
    for r in range(4):
        pair = halves(arrived_ref[pl.ds(r, peers, stride=WORDS), :])
        for value, slot in zip(pair, (r, r + 4)):
            scale = unit(levels[:, free + slot : free + slot + 1])
            rows_ref[pl.ds(slot, peers, stride=8), :] = value * scale
    total = own_ref[...]
    for g in range(recv_ref.shape[0]):
        hot = one_hot(iota, recv_ref[g : g + 1, :])
        high, low = split_two(rows_ref[lane_block(g), :])
        total += jnp.dot(hot, high, preferred_element_type=F32)
        total += jnp.dot(hot, low, preferred_element_type=F32)
    out_ref[...] = total.astype(BF16)


def local(features, cotangent, relu_mask, weight, pair_in, pair_out, recv_index):
    x = features[0]
    own_rows, in_width = x.shape
    offsets, unused, out_width = weight.shape
    peers = lax.axis_size(SPACE)
    group = lax.axis_size(GROUP)
    scenes = lax.axis_size("scene")
    send_rows = recv_index.shape[2]
    slots = send_rows // peers
    targets = own_rows + send_rows
    columns = offsets * out_width // group
    recv = recv_index.reshape(send_rows // LANES, LANES)
    shape = jax.ShapeDtypeStruct

    hbm = pl.BlockSpec(memory_space=pltpu.HBM)
    vmem = pl.BlockSpec(memory_space=pltpu.VMEM)
    blocks = -(-columns // LANES)
    free = columns - (blocks - 1) * LANES

    upstream, outgoing = call(
        gather_kernel,
        (shape((own_rows, out_width), BF16), shape((send_rows, out_width), BF16)),
        scratch=(
            pltpu.VMEM((own_rows, out_width), BF16),
            pltpu.VMEM((own_rows, out_width), I32),
            pltpu.VMEM(recv.shape, I32),
            pltpu.SemaphoreType.DMA((3,)),
        ),
        in_specs=[hbm] * 3,
        vmem=MOST_VMEM,
        flops=2 * send_rows * own_rows * out_width,
        moved=send_rows * out_width * 3,
    )(cotangent[0], relu_mask[0], recv)
    own_x, outgoing = lax.optimization_barrier((x, outgoing))
    returned = lax.all_to_all(outgoing.reshape(peers, slots, out_width), SPACE, 0, 0, tiled=True)

    swap = [(0, 1), (1, 0)]
    one, two = ([(i, i ^ d) for i in range(scenes)] for d in (1, 2))
    pair = jnp.stack([own_x, lax.ppermute(own_x, "scene", one)])
    other = lax.ppermute(pair, "scene", two)

    table, turned = call(
        functools.partial(table_kernel, targets=targets),
        (shape((offsets, own_rows), I32), shape((out_width, own_rows), BF16)),
    )(pair_in[0, 0], pair_out[0, 0], upstream)

    returned, pair, other = lax.optimization_barrier((returned, pair, other))
    near = jnp.concatenate([pair, other])
    gathered = call(
        lookup_kernel,
        shape((offsets * out_width, own_rows), BF16),
        scratch=(
            pltpu.VMEM((out_width, targets), BF16),
            pltpu.VMEM((2, targets, STEP * LANES), BF16),
            pltpu.VMEM((offsets * out_width, own_rows), BF16),
            pltpu.SemaphoreType.DMA((-(-offsets // STEP),)),
        ),
        out_specs=hbm,
    )(turned, returned.reshape(send_rows, out_width), table)
    group_g = lax.all_to_all(gathered.reshape(group, columns, own_rows), GROUP, 0, 0, tiled=True)

    own, words, input_grad = call(
        functools.partial(forward_kernel, free=free),
        (
            shape((own_rows, out_width), F32),
            shape((5, peers, out_width), I32),
            shape((own_rows, in_width), BF16),
        ),
        scratch=(
            pltpu.VMEM(weight.shape, BF16),
            pltpu.VMEM((offsets * out_width, own_rows), BF16),
            pltpu.VMEM((offsets * own_rows, 2 * out_width), BF16),
            pltpu.VMEM((2, targets // 3, offsets * own_rows), BF16),
            pltpu.VMEM((targets, out_width), F32),
            pltpu.SemaphoreType.DMA((2, 3)),
            pltpu.SemaphoreType.DMA,
        ),
        in_specs=[vmem, hbm, vmem, hbm],
        out_specs=(hbm, vmem, vmem),
    )(near, weight, table, gathered)

    far = lax.ppermute(near, "core", swap)
    packed = call(
        pack_kernel,
        shape((peers * WORDS, LANES), I32),
        scratch=(pltpu.VMEM((blocks, in_width, LANES), F32),),
        flops=2 * columns * in_width * own_rows * group,
        moved=peers * WORDS * LANES * 8,
    )(group_g, near, far, words)
    arrived = lax.all_to_all(packed.reshape(peers, WORDS, LANES), SPACE, 0, 0, tiled=True)
    arrived = arrived.reshape(peers * WORDS, LANES)

    quarter = call(
        functools.partial(sum_kernel, free=free),
        shape((scenes, 16, LANES), F32),
        moved=peers * WORDS * LANES * 4,
    )(arrived)
    sums = lax.all_to_all(quarter, "scene", 0, 0, tiled=True)
    conv_out = call(
        functools.partial(receive_kernel, free=free),
        shape((own_rows, out_width), BF16),
        scratch=(pltpu.VMEM((send_rows, out_width), F32),),
        flops=4 * send_rows * own_rows * out_width,
        moved=send_rows * out_width * 4,
    )(own, arrived, recv)

    own_in = in_width // peers
    sums = sums.reshape(scenes, own_in, blocks, 2, LANES).transpose(1, 3, 0, 2, 4)
    sums = sums.reshape(own_in, group, blocks * LANES)[:, :, :columns]
    kernel_grad = sums.reshape(own_in, offsets, out_width)
    kernel_grad = kernel_grad.transpose(1, 0, 2).reshape(offsets, own_in * out_width)
    normalizer = 1.0 / math.sqrt(scenes * peers * own_rows)
    return (conv_out[None], input_grad[None], kernel_grad * normalizer)


def solution(mesh):
    scenes = mesh.devices.shape[1]
    fine = Mesh(mesh.devices.reshape(8, 8, 2, scenes), ("y", "z", "core", "scene"))
    voxels = P("scene", SPACE)
    return jax.shard_map(
        local,
        mesh=fine,
        in_specs=(voxels, voxels, voxels, P(), voxels, voxels, voxels),
        out_specs=(voxels, voxels, P(None, SPACE)),
        check_vma=False,
    )
```

```python
import functools
import math

import jax
import jax.numpy as jnp
from jax import lax
from jax.experimental import pallas as pl
from jax.experimental.pallas import tpu as pltpu
from jax.sharding import Mesh
from jax.sharding import PartitionSpec as P

F32 = jnp.float32
BF16 = jnp.bfloat16
I32 = jnp.int32
LANES = 128
STEP = 4
WORDS = 8
VMEM_BYTES = 24 * 1024 * 1024
MOST_VMEM = 64 * 1024 * 1024 - 128 * 1024
SPACE = ("y", "z", "core")
GROUP = ("core", "scene")


def call(kernel, outs, scratch=(), flops=0, moved=0, vmem=VMEM_BYTES, **specs):
    return pl.pallas_call(
        kernel,
        out_shape=outs,
        scratch_shapes=list(scratch),
        **specs,
        compiler_params=pltpu.CompilerParams(vmem_limit_bytes=vmem),
        cost_estimate=pl.CostEstimate(flops=flops, bytes_accessed=moved, transcendentals=0),
    )


def rows_iota(rows, start=0):
    return lax.broadcasted_iota(I32, (rows, LANES), 0) + start


def one_hot(iota, row):
    return jnp.where(iota == row, 1.0, 0.0).astype(BF16)


def one_hot_16(iota, row):
    rows = iota.shape[0]
    narrow = jnp.broadcast_to(row, (16, LANES)).astype(jnp.int16)
    narrow = jnp.concatenate([narrow] * (rows // 16), axis=0)
    return jnp.where(iota == narrow, jnp.ones((rows, LANES), BF16), jnp.zeros((rows, LANES), BF16))


def split_two(value):
    high = value.astype(BF16)
    low = (value - high.astype(F32)).astype(BF16)
    return high, low


def lane_block(k):
    return slice(k * LANES, (k + 1) * LANES)


def gather_kernel(cot_any, mask_any, recv_any, up_ref, out_ref, cot_ref, mask_ref, recv_ref, sems):
    pairs = ((cot_any, cot_ref), (mask_any, mask_ref), (recv_any, recv_ref))
    copies = [pltpu.make_async_copy(a, b, sems.at[i]) for i, (a, b) in enumerate(pairs)]
    for copy in copies:
        copy.start()
    for copy in copies:
        copy.wait()
    up = (cot_ref[...].astype(F32) * mask_ref[...].astype(F32)).astype(BF16)
    up_ref[...] = up
    iota = rows_iota(LANES)
    for g in range(recv_ref.shape[0]):
        hot = one_hot(iota, recv_ref[g : g + 1, :])
        rows = lax.dot_general(hot, up, (((0,), (0,)), ((), ())), preferred_element_type=F32)
        out_ref[lane_block(g), :] = rows.astype(BF16)


def table_kernel(in_ref, out_ref, up_ref, table_ref, turned_ref, *, targets):
    turned_ref[...] = up_ref[...].T
    iota = rows_iota(LANES)
    picks = rows_iota(16)
    for k in range(in_ref.shape[0]):
        hot = one_hot(iota, in_ref[k : k + 1, :])
        target = out_ref[k : k + 1, :]
        code = jnp.where(target < targets, target + 1, 0)
        digits = jnp.where(picks == 0, code >> 7, jnp.where(picks == 1, code & 127, 0))
        found = lax.dot_general(
            digits.astype(F32).astype(BF16), hot, (((1,), (1,)), ((), ())), preferred_element_type=F32
        )
        table_ref[k : k + 1, :] = (found[0:1] * 128.0 + found[1:2] - 1.0).astype(I32)


def lookup_kernel(turned_ref, back_ref, table_ref, gathered_any, ext_ref, hot_ref, gathered_ref, sems):
    blocks = back_ref.shape[0] // LANES
    offsets = table_ref.shape[0]
    ext_ref[:, 0:LANES] = turned_ref[...]
    for b in range(blocks):
        ext_ref[:, lane_block(b + 1)] = back_ref[lane_block(b), :].T
    iota = rows_iota((blocks + 1) * LANES).astype(jnp.int16)
    copies = []
    for first in range(0, offsets, STEP):
        count = min(STEP, offsets - first)
        slot = (first // STEP) % 2
        for k in range(count):
            hot_ref[slot, :, lane_block(k)] = one_hot_16(iota, table_ref[first + k : first + k + 1, :])
        rows = jnp.dot(
            ext_ref[...], hot_ref[slot, :, : count * LANES], preferred_element_type=F32
        ).astype(BF16)
        for k in range(count):
            gathered_ref[lane_block(first + k), :] = rows[:, lane_block(k)]
        part = pl.ds(first * LANES, count * LANES)
        copies.append(
            pltpu.make_async_copy(gathered_ref.at[part], gathered_any.at[part], sems.at[first // STEP])
        )
        copies[-1].start()
    for copy in copies:
        copy.wait()


def encode(value, top):
    level = jnp.ceil(jnp.log2(jnp.maximum(top, 1e-36)) * 8.0)
    code = jnp.round(value * jnp.exp2(level * -0.125) * 32767.0)
    return jnp.clip(code, -32767.0, 32767.0).astype(I32), level.astype(I32)


def unit(level):
    return jnp.exp2(level.astype(F32) * 0.125) * (1.0 / 32767.0)


def join(first, second):
    return (first << 16) | (second & 0xFFFF)


def halves(word):
    return (word >> 16).astype(F32), ((word << 16) >> 16).astype(F32)


def row_top(value):
    return jnp.max(jnp.abs(value), axis=1, keepdims=True)


def fetch(w_any, w_ref, gathered_any, gathered_ref, sems):
    offsets = w_ref.shape[0]
    parts = sems.shape[1]
    step = offsets // parts
    copies = []
    for i in range(parts):
        part = pl.ds(i * step, step)
        rows = pl.ds(i * step * LANES, step * LANES)
        copies.append(
            (
                pltpu.make_async_copy(w_any.at[part], w_ref.at[part], sems.at[0, i]),
                pltpu.make_async_copy(gathered_any.at[rows], gathered_ref.at[rows], sems.at[1, i]),
            )
        )
        for copy in copies[-1]:
            copy.start()
    return copies, step


def forward_kernel(
    near_ref,
    w_any,
    table_ref,
    gathered_any,
    own_any,
    word_ref,
    grad_ref,
    w_ref,
    gathered_ref,
    terms_ref,
    hot_ref,
    send_ref,
    sems,
    own_sem,
    *,
    free,
):
    offsets = w_ref.shape[0]
    copies, step = fetch(w_any, w_ref, gathered_any, gathered_ref, sems)
    total = jnp.zeros((w_ref.shape[1], LANES), F32)
    for k in range(offsets):
        if k % step == 0:
            for copy in copies[k // step]:
                copy.wait()
        high, low = split_two(jnp.dot(near_ref[0], w_ref[k], preferred_element_type=F32))
        terms_ref[lane_block(k), 0:LANES] = high
        terms_ref[lane_block(k), LANES : 2 * LANES] = low
        total += jnp.dot(w_ref[k], gathered_ref[lane_block(k), :], preferred_element_type=F32)
    grad_ref[...] = total.T.astype(BF16)
    iota = rows_iota(LANES).astype(jnp.int16)

    span = hot_ref.shape[1]
    own_rows = own_any.shape[0]
    own_copy = pltpu.make_async_copy(send_ref.at[pl.ds(0, own_rows)], own_any, own_sem)
    for i in range(send_ref.shape[0] // span):
        for j in range(span // LANES):
            for k in range(offsets):
                row = table_ref[k : k + 1, :] - (i * span + j * LANES)
                hot_ref[i % 2, lane_block(j), lane_block(k)] = one_hot_16(iota, row)
        both = jnp.dot(hot_ref[i % 2], terms_ref[...], preferred_element_type=F32)
        send_ref[pl.ds(i * span, span), :] = both[:, :LANES] + both[:, LANES:]
        if i == 0:
            own_copy.start()
    peers = word_ref.shape[1]
    lane = lax.broadcasted_iota(I32, (peers, LANES), 1)
    levels = jnp.zeros((peers, LANES), I32)
    for r in range(4):
        words = []
        for slot in (r, r + 4):
            value = send_ref[pl.ds(own_rows + slot, peers, stride=8), :]
            code, level = encode(value, row_top(value))
            words.append(code)
            levels = jnp.where(lane == free + slot, level, levels)
        word_ref[r] = join(*words)
    word_ref[4] = levels
    own_copy.wait()


def pack_kernel(g_ref, near_ref, far_ref, word_ref, out_ref, turn_ref):
    columns = g_ref.shape[1]
    peers = word_ref.shape[1]
    blocks = turn_ref.shape[0]
    scenes = near_ref.shape[0]
    core, scene = (lax.axis_index(axis) for axis in GROUP)
    total = jnp.zeros((columns, near_ref.shape[2]), F32)
    for s in range(g_ref.shape[0]):
        x_ref, holder = (near_ref, core) if s < scenes else (far_ref, 1 - core)
        sender = holder * scenes + (scene ^ (s % scenes))
        total += jnp.dot(g_ref[sender], x_ref[s % scenes], preferred_element_type=F32)
    rest = blocks * LANES - columns
    total = jnp.concatenate([total, jnp.zeros((rest, total.shape[1]), F32)], axis=0)
    for h in range(blocks):
        turn_ref[h] = total[lane_block(h), :].T
    for r in range(4):
        out_ref[pl.ds(r, peers, stride=WORDS), :] = word_ref[r]
    parts = [[turn_ref[h, pl.ds(c, peers, stride=2), :] for c in range(2)] for h in range(blocks)]
    top = functools.reduce(jnp.maximum, [jnp.abs(part) for pair in parts for part in pair])
    top = jnp.max(top, axis=1, keepdims=True)
    free = LANES - rest
    lane = lax.broadcasted_iota(I32, (peers, LANES), 1)
    for h in range(blocks):
        codes = [encode(part, top) for part in parts[h]]
        word = join(codes[0][0], codes[1][0])
        if h == blocks - 1:
            levels = jnp.where(lane == free + 8, codes[0][1], word_ref[4])
            word = jnp.where(lane < free, word, levels)
        out_ref[pl.ds(4 + h, peers, stride=WORDS), :] = word


def sum_kernel(arrived_ref, out_ref, *, free):
    peers = arrived_ref.shape[0] // WORDS
    words = [arrived_ref[pl.ds(4 + h, peers, stride=WORDS), :] for h in range(4)]
    scale = unit(words[-1][:, free + 8 : free + 9])
    for h in range(4):
        for c, value in enumerate(halves(words[h])):
            total = (value * scale).reshape(peers // 8, 8, LANES).sum(axis=0)
            total = (total[0:2] + total[2:4]) + (total[4:6] + total[6:8])
            row = 2 * (4 * c + h)
            for s in range(out_ref.shape[0]):
                out_ref[s, row : row + 2, :] = total


def receive_kernel(own_ref, arrived_ref, recv_ref, out_ref, rows_ref, *, free):
    peers = arrived_ref.shape[0] // WORDS
    iota = rows_iota(LANES)
    levels = arrived_ref[pl.ds(WORDS - 1, peers, stride=WORDS), :]
    for r in range(4):
        pair = halves(arrived_ref[pl.ds(r, peers, stride=WORDS), :])
        for value, slot in zip(pair, (r, r + 4)):
            scale = unit(levels[:, free + slot : free + slot + 1])
            rows_ref[pl.ds(slot, peers, stride=8), :] = value * scale
    total = own_ref[...]
    for g in range(recv_ref.shape[0]):
        hot = one_hot(iota, recv_ref[g : g + 1, :])
        high, low = split_two(rows_ref[lane_block(g), :])
        total += jnp.dot(hot, high, preferred_element_type=F32)
        total += jnp.dot(hot, low, preferred_element_type=F32)
    out_ref[...] = total.astype(BF16)


def local(features, cotangent, relu_mask, weight, pair_in, pair_out, recv_index):
    x = features[0]
    own_rows, in_width = x.shape
    offsets, unused, out_width = weight.shape
    peers = lax.axis_size(SPACE)
    group = lax.axis_size(GROUP)
    scenes = lax.axis_size("scene")
    send_rows = recv_index.shape[2]
    slots = send_rows // peers
    targets = own_rows + send_rows
    columns = offsets * out_width // group
    recv = recv_index.reshape(send_rows // LANES, LANES)
    shape = jax.ShapeDtypeStruct

    hbm = pl.BlockSpec(memory_space=pltpu.HBM)
    vmem = pl.BlockSpec(memory_space=pltpu.VMEM)
    blocks = -(-columns // LANES)
    free = columns - (blocks - 1) * LANES

    upstream, outgoing = call(
        gather_kernel,
        (shape((own_rows, out_width), BF16), shape((send_rows, out_width), BF16)),
        scratch=(
            pltpu.VMEM((own_rows, out_width), BF16),
            pltpu.VMEM((own_rows, out_width), I32),
            pltpu.VMEM(recv.shape, I32),
            pltpu.SemaphoreType.DMA((3,)),
        ),
        in_specs=[hbm] * 3,
        vmem=MOST_VMEM,
        flops=2 * send_rows * own_rows * out_width,
        moved=send_rows * out_width * 3,
    )(cotangent[0], relu_mask[0], recv)
    own_x, outgoing = lax.optimization_barrier((x, outgoing))
    returned = lax.all_to_all(outgoing.reshape(peers, slots, out_width), SPACE, 0, 0, tiled=True)

    swap = [(0, 1), (1, 0)]
    ring = [
        lax.ppermute(own_x, "scene", [(i, i ^ d) for i in range(scenes)]) for d in range(1, scenes)
    ]

    table, turned = call(
        functools.partial(table_kernel, targets=targets),
        (shape((offsets, own_rows), I32), shape((out_width, own_rows), BF16)),
    )(pair_in[0, 0], pair_out[0, 0], upstream)

    returned, *ring = lax.optimization_barrier((returned, *ring))
    gathered = call(
        lookup_kernel,
        shape((offsets * out_width, own_rows), BF16),
        scratch=(
            pltpu.VMEM((out_width, targets), BF16),
            pltpu.VMEM((2, targets, STEP * LANES), BF16),
            pltpu.VMEM((offsets * out_width, own_rows), BF16),
            pltpu.SemaphoreType.DMA((-(-offsets // STEP),)),
        ),
        out_specs=hbm,
    )(turned, returned.reshape(send_rows, out_width), table)
    group_g = lax.all_to_all(gathered.reshape(group, columns, own_rows), GROUP, 0, 0, tiled=True)

    near = jnp.stack([x] + ring)
    own, words, input_grad = call(
        functools.partial(forward_kernel, free=free),
        (
            shape((own_rows, out_width), F32),
            shape((5, peers, out_width), I32),
            shape((own_rows, in_width), BF16),
        ),
        scratch=(
            pltpu.VMEM(weight.shape, BF16),
            pltpu.VMEM((offsets * out_width, own_rows), BF16),
            pltpu.VMEM((offsets * own_rows, 2 * out_width), BF16),
            pltpu.VMEM((2, targets // 3, offsets * own_rows), BF16),
            pltpu.VMEM((targets, out_width), F32),
            pltpu.SemaphoreType.DMA((2, 3)),
            pltpu.SemaphoreType.DMA,
        ),
        in_specs=[vmem, hbm, vmem, hbm],
        out_specs=(hbm, vmem, vmem),
    )(near, weight, table, gathered)

    far = lax.ppermute(near, "core", swap)
    packed = call(
        pack_kernel,
        shape((peers * WORDS, LANES), I32),
        scratch=(pltpu.VMEM((blocks, in_width, LANES), F32),),
        flops=2 * columns * in_width * own_rows * group,
        moved=peers * WORDS * LANES * 8,
    )(group_g, near, far, words)
    arrived = lax.all_to_all(packed.reshape(peers, WORDS, LANES), SPACE, 0, 0, tiled=True)
    arrived = arrived.reshape(peers * WORDS, LANES)

    quarter = call(
        functools.partial(sum_kernel, free=free),
        shape((scenes, 16, LANES), F32),
        moved=peers * WORDS * LANES * 4,
    )(arrived)
    sums = lax.all_to_all(quarter, "scene", 0, 0, tiled=True)
    conv_out = call(
        functools.partial(receive_kernel, free=free),
        shape((own_rows, out_width), BF16),
        scratch=(pltpu.VMEM((send_rows, out_width), F32),),
        flops=4 * send_rows * own_rows * out_width,
        moved=send_rows * out_width * 4,
    )(own, arrived, recv)

    own_in = in_width // peers
    sums = sums.reshape(scenes, own_in, blocks, 2, LANES).transpose(1, 3, 0, 2, 4)
    sums = sums.reshape(own_in, group, blocks * LANES)[:, :, :columns]
    kernel_grad = sums.reshape(own_in, offsets, out_width)
    kernel_grad = kernel_grad.transpose(1, 0, 2).reshape(offsets, own_in * out_width)
    normalizer = 1.0 / math.sqrt(scenes * peers * own_rows)
    return (conv_out[None], input_grad[None], kernel_grad * normalizer)


def solution(mesh):
    scenes = mesh.devices.shape[1]
    fine = Mesh(mesh.devices.reshape(8, 8, 2, scenes), ("y", "z", "core", "scene"))
    voxels = P("scene", SPACE)
    return jax.shard_map(
        local,
        mesh=fine,
        in_specs=(voxels, voxels, voxels, P(), voxels, voxels, voxels),
        out_specs=(voxels, voxels, P(None, SPACE)),
        check_vma=False,
    )
```

```python
import functools
import math

import jax
import jax.numpy as jnp
from jax import lax
from jax.experimental import pallas as pl
from jax.experimental.pallas import tpu as pltpu
from jax.sharding import Mesh
from jax.sharding import PartitionSpec as P

F32 = jnp.float32
BF16 = jnp.bfloat16
I32 = jnp.int32
LANES = 128
STEP = 4
WORDS = 8
VMEM_BYTES = 24 * 1024 * 1024
MOST_VMEM = 64 * 1024 * 1024 - 128 * 1024
SPACE = ("y", "z", "core")
GROUP = ("core", "scene")


def call(kernel, outs, scratch=(), flops=0, moved=0, vmem=VMEM_BYTES, **specs):
    return pl.pallas_call(
        kernel,
        out_shape=outs,
        scratch_shapes=list(scratch),
        **specs,
        compiler_params=pltpu.CompilerParams(vmem_limit_bytes=vmem),
        cost_estimate=pl.CostEstimate(flops=flops, bytes_accessed=moved, transcendentals=0),
    )


def rows_iota(rows, start=0):
    return lax.broadcasted_iota(I32, (rows, LANES), 0) + start


def one_hot(iota, row):
    return jnp.where(iota == row, 1.0, 0.0).astype(BF16)


def one_hot_16(iota, row):
    rows = iota.shape[0]
    narrow = jnp.broadcast_to(row, (16, LANES)).astype(jnp.int16)
    narrow = jnp.concatenate([narrow] * (rows // 16), axis=0)
    return jnp.where(iota == narrow, jnp.ones((rows, LANES), BF16), jnp.zeros((rows, LANES), BF16))


def split_two(value):
    high = value.astype(BF16)
    low = (value - high.astype(F32)).astype(BF16)
    return high, low


def lane_block(k):
    return slice(k * LANES, (k + 1) * LANES)


def gather_kernel(cot_any, mask_any, recv_any, up_ref, out_ref, cot_ref, mask_ref, recv_ref, sems):
    pairs = ((cot_any, cot_ref), (mask_any, mask_ref), (recv_any, recv_ref))
    copies = [pltpu.make_async_copy(a, b, sems.at[i]) for i, (a, b) in enumerate(pairs)]
    for copy in copies:
        copy.start()
    for copy in copies:
        copy.wait()
    up = (cot_ref[...].astype(F32) * mask_ref[...].astype(F32)).astype(BF16)
    up_ref[...] = up
    iota = rows_iota(LANES)
    for g in range(recv_ref.shape[0]):
        hot = one_hot(iota, recv_ref[g : g + 1, :])
        rows = lax.dot_general(hot, up, (((0,), (0,)), ((), ())), preferred_element_type=F32)
        out_ref[lane_block(g), :] = rows.astype(BF16)


def table_kernel(in_ref, out_ref, up_ref, table_ref, turned_ref, *, targets):
    turned_ref[...] = up_ref[...].T
    iota = rows_iota(LANES)
    picks = rows_iota(16)
    for k in range(in_ref.shape[0]):
        hot = one_hot(iota, in_ref[k : k + 1, :])
        target = out_ref[k : k + 1, :]
        code = jnp.where(target < targets, target + 1, 0)
        digits = jnp.where(picks == 0, code >> 7, jnp.where(picks == 1, code & 127, 0))
        found = lax.dot_general(
            digits.astype(F32).astype(BF16), hot, (((1,), (1,)), ((), ())), preferred_element_type=F32
        )
        table_ref[k : k + 1, :] = (found[0:1] * 128.0 + found[1:2] - 1.0).astype(I32)


def lookup_kernel(turned_ref, back_ref, table_ref, gathered_any, ext_ref, hot_ref, gathered_ref, sems):
    blocks = back_ref.shape[0] // LANES
    offsets = table_ref.shape[0]
    ext_ref[:, 0:LANES] = turned_ref[...]
    for b in range(blocks):
        ext_ref[:, lane_block(b + 1)] = back_ref[lane_block(b), :].T
    iota = rows_iota((blocks + 1) * LANES).astype(jnp.int16)
    copies = []
    for first in range(0, offsets, STEP):
        count = min(STEP, offsets - first)
        slot = (first // STEP) % 2
        for k in range(count):
            hot_ref[slot, :, lane_block(k)] = one_hot_16(iota, table_ref[first + k : first + k + 1, :])
        rows = jnp.dot(
            ext_ref[...], hot_ref[slot, :, : count * LANES], preferred_element_type=F32
        ).astype(BF16)
        for k in range(count):
            gathered_ref[lane_block(first + k), :] = rows[:, lane_block(k)]
        part = pl.ds(first * LANES, count * LANES)
        copies.append(
            pltpu.make_async_copy(gathered_ref.at[part], gathered_any.at[part], sems.at[first // STEP])
        )
        copies[-1].start()
    for copy in copies:
        copy.wait()


def encode(value, top):
    level = jnp.ceil(jnp.log2(jnp.maximum(top, 1e-36)) * 8.0)
    code = jnp.round(value * jnp.exp2(level * -0.125) * 32767.0)
    return jnp.clip(code, -32767.0, 32767.0).astype(I32), level.astype(I32)


def unit(level):
    return jnp.exp2(level.astype(F32) * 0.125) * (1.0 / 32767.0)


def join(first, second):
    return (first << 16) | (second & 0xFFFF)


def halves(word):
    return (word >> 16).astype(F32), ((word << 16) >> 16).astype(F32)


def row_top(value):
    return jnp.max(jnp.abs(value), axis=1, keepdims=True)


def fetch(w_any, w_ref, gathered_any, gathered_ref, sems):
    offsets = w_ref.shape[0]
    parts = sems.shape[1]
    step = offsets // parts
    copies = []
    for i in range(parts):
        part = pl.ds(i * step, step)
        rows = pl.ds(i * step * LANES, step * LANES)
        copies.append(
            (
                pltpu.make_async_copy(w_any.at[part], w_ref.at[part], sems.at[0, i]),
                pltpu.make_async_copy(gathered_any.at[rows], gathered_ref.at[rows], sems.at[1, i]),
            )
        )
        for copy in copies[-1]:
            copy.start()
    return copies, step


def forward_kernel(
    near_ref,
    w_any,
    table_ref,
    gathered_any,
    own_any,
    word_ref,
    grad_ref,
    w_ref,
    gathered_ref,
    terms_ref,
    hot_ref,
    send_ref,
    sems,
    own_sem,
    *,
    free,
):
    offsets = w_ref.shape[0]
    copies, step = fetch(w_any, w_ref, gathered_any, gathered_ref, sems)
    total = jnp.zeros((w_ref.shape[1], LANES), F32)
    for k in range(offsets):
        if k % step == 0:
            for copy in copies[k // step]:
                copy.wait()
        high, low = split_two(jnp.dot(near_ref[0], w_ref[k], preferred_element_type=F32))
        terms_ref[lane_block(k), 0:LANES] = high
        terms_ref[lane_block(k), LANES : 2 * LANES] = low
        total += jnp.dot(w_ref[k], gathered_ref[lane_block(k), :], preferred_element_type=F32)
    grad_ref[...] = total.T.astype(BF16)
    iota = rows_iota(LANES).astype(jnp.int16)

    span = hot_ref.shape[1]
    own_rows = own_any.shape[0]
    own_copy = pltpu.make_async_copy(send_ref.at[pl.ds(0, own_rows)], own_any, own_sem)
    for i in range(send_ref.shape[0] // span):
        for j in range(span // LANES):
            for k in range(offsets):
                row = table_ref[k : k + 1, :] - (i * span + j * LANES)
                hot_ref[i % 2, lane_block(j), lane_block(k)] = one_hot_16(iota, row)
        both = jnp.dot(hot_ref[i % 2], terms_ref[...], preferred_element_type=F32)
        send_ref[pl.ds(i * span, span), :] = both[:, :LANES] + both[:, LANES:]
        if i == 0:
            own_copy.start()
    peers = word_ref.shape[1]
    lane = lax.broadcasted_iota(I32, (peers, LANES), 1)
    levels = jnp.zeros((peers, LANES), I32)
    for r in range(4):
        words = []
        for slot in (r, r + 4):
            value = send_ref[pl.ds(own_rows + slot, peers, stride=8), :]
            code, level = encode(value, row_top(value))
            words.append(code)
            levels = jnp.where(lane == free + slot, level, levels)
        word_ref[r] = join(*words)
    word_ref[4] = levels
    own_copy.wait()


def pack_kernel(g_ref, near_ref, far_ref, word_ref, out_ref, turn_ref):
    columns = g_ref.shape[1]
    peers = word_ref.shape[1]
    blocks = turn_ref.shape[0]
    scenes = near_ref.shape[0]
    core, scene = (lax.axis_index(axis) for axis in GROUP)
    total = jnp.zeros((columns, near_ref.shape[2]), F32)
    for s in range(g_ref.shape[0]):
        x_ref, holder = (near_ref, core) if s < scenes else (far_ref, 1 - core)
        sender = holder * scenes + (scene ^ (s % scenes))
        total += jnp.dot(g_ref[sender], x_ref[s % scenes], preferred_element_type=F32)
    rest = blocks * LANES - columns
    total = jnp.concatenate([total, jnp.zeros((rest, total.shape[1]), F32)], axis=0)
    for h in range(blocks):
        turn_ref[h] = total[lane_block(h), :].T
    for r in range(4):
        out_ref[pl.ds(r, peers, stride=WORDS), :] = word_ref[r]
    parts = [[turn_ref[h, pl.ds(c, peers, stride=2), :] for c in range(2)] for h in range(blocks)]
    top = functools.reduce(jnp.maximum, [jnp.abs(part) for pair in parts for part in pair])
    top = jnp.max(top, axis=1, keepdims=True)
    free = LANES - rest
    lane = lax.broadcasted_iota(I32, (peers, LANES), 1)
    for h in range(blocks):
        codes = [encode(part, top) for part in parts[h]]
        word = join(codes[0][0], codes[1][0])
        if h == blocks - 1:
            levels = jnp.where(lane == free + 8, codes[0][1], word_ref[4])
            word = jnp.where(lane < free, word, levels)
        out_ref[pl.ds(4 + h, peers, stride=WORDS), :] = word


def sum_kernel(arrived_ref, out_ref, *, free):
    peers = arrived_ref.shape[0] // WORDS
    words = [arrived_ref[pl.ds(4 + h, peers, stride=WORDS), :] for h in range(4)]
    scale = unit(words[-1][:, free + 8 : free + 9])
    for h in range(4):
        for c, value in enumerate(halves(words[h])):
            total = (value * scale).reshape(peers // 8, 8, LANES).sum(axis=0)
            total = (total[0:2] + total[2:4]) + (total[4:6] + total[6:8])
            row = 2 * (4 * c + h)
            for s in range(out_ref.shape[0]):
                out_ref[s, row : row + 2, :] = total


def receive_kernel(own_ref, arrived_ref, recv_ref, out_ref, rows_ref, *, free):
    peers = arrived_ref.shape[0] // WORDS
    iota = rows_iota(LANES)
    levels = arrived_ref[pl.ds(WORDS - 1, peers, stride=WORDS), :]
    for r in range(4):
        pair = halves(arrived_ref[pl.ds(r, peers, stride=WORDS), :])
        for value, slot in zip(pair, (r, r + 4)):
            scale = unit(levels[:, free + slot : free + slot + 1])
            rows_ref[pl.ds(slot, peers, stride=8), :] = value * scale
    total = own_ref[...]
    for g in range(recv_ref.shape[0]):
        hot = one_hot(iota, recv_ref[g : g + 1, :])
        high, low = split_two(rows_ref[lane_block(g), :])
        total += jnp.dot(hot, high, preferred_element_type=F32)
        total += jnp.dot(hot, low, preferred_element_type=F32)
    out_ref[...] = total.astype(BF16)


def local(features, cotangent, relu_mask, weight, pair_in, pair_out, recv_index):
    x = features[0]
    own_rows, in_width = x.shape
    offsets, unused, out_width = weight.shape
    peers = lax.axis_size(SPACE)
    group = lax.axis_size(GROUP)
    scenes = lax.axis_size("scene")
    send_rows = recv_index.shape[2]
    slots = send_rows // peers
    targets = own_rows + send_rows
    columns = offsets * out_width // group
    recv = recv_index.reshape(send_rows // LANES, LANES)
    shape = jax.ShapeDtypeStruct

    hbm = pl.BlockSpec(memory_space=pltpu.HBM)
    vmem = pl.BlockSpec(memory_space=pltpu.VMEM)
    blocks = -(-columns // LANES)
    free = columns - (blocks - 1) * LANES

    upstream, outgoing = call(
        gather_kernel,
        (shape((own_rows, out_width), BF16), shape((send_rows, out_width), BF16)),
        scratch=(
            pltpu.VMEM((own_rows, out_width), BF16),
            pltpu.VMEM((own_rows, out_width), I32),
            pltpu.VMEM(recv.shape, I32),
            pltpu.SemaphoreType.DMA((3,)),
        ),
        in_specs=[hbm] * 3,
        vmem=MOST_VMEM,
        flops=2 * send_rows * own_rows * out_width,
        moved=send_rows * out_width * 3,
    )(cotangent[0], relu_mask[0], recv)
    own_x, outgoing = lax.optimization_barrier((x, outgoing))
    returned = lax.all_to_all(outgoing.reshape(peers, slots, out_width), SPACE, 0, 0, tiled=True)

    swap = [(0, 1), (1, 0)]
    ring = [
        lax.ppermute(own_x, "scene", [(i, i ^ d) for i in range(scenes)]) for d in range(1, scenes)
    ]

    table, turned = call(
        functools.partial(table_kernel, targets=targets),
        (shape((offsets, own_rows), I32), shape((out_width, own_rows), BF16)),
    )(pair_in[0, 0], pair_out[0, 0], upstream)

    gathered = call(
        lookup_kernel,
        shape((offsets * out_width, own_rows), BF16),
        scratch=(
            pltpu.VMEM((out_width, targets), BF16),
            pltpu.VMEM((2, targets, STEP * LANES), BF16),
            pltpu.VMEM((offsets * out_width, own_rows), BF16),
            pltpu.SemaphoreType.DMA((-(-offsets // STEP),)),
        ),
        out_specs=hbm,
    )(turned, returned.reshape(send_rows, out_width), table)
    gathered, *ring = lax.optimization_barrier((gathered, *ring))
    group_g = lax.all_to_all(gathered.reshape(group, columns, own_rows), GROUP, 0, 0, tiled=True)

    near = jnp.stack([x] + ring)
    own, words, input_grad = call(
        functools.partial(forward_kernel, free=free),
        (
            shape((own_rows, out_width), F32),
            shape((5, peers, out_width), I32),
            shape((own_rows, in_width), BF16),
        ),
        scratch=(
            pltpu.VMEM(weight.shape, BF16),
            pltpu.VMEM((offsets * out_width, own_rows), BF16),
            pltpu.VMEM((offsets * own_rows, 2 * out_width), BF16),
            pltpu.VMEM((2, targets // 3, offsets * own_rows), BF16),
            pltpu.VMEM((targets, out_width), F32),
            pltpu.SemaphoreType.DMA((2, 3)),
            pltpu.SemaphoreType.DMA,
        ),
        in_specs=[vmem, hbm, vmem, hbm],
        out_specs=(hbm, vmem, vmem),
    )(near, weight, table, gathered)

    far = lax.ppermute(near, "core", swap)
    packed = call(
        pack_kernel,
        shape((peers * WORDS, LANES), I32),
        scratch=(pltpu.VMEM((blocks, in_width, LANES), F32),),
        flops=2 * columns * in_width * own_rows * group,
        moved=peers * WORDS * LANES * 8,
    )(group_g, near, far, words)
    arrived = lax.all_to_all(packed.reshape(peers, WORDS, LANES), SPACE, 0, 0, tiled=True)
    arrived = arrived.reshape(peers * WORDS, LANES)

    quarter = call(
        functools.partial(sum_kernel, free=free),
        shape((scenes, 16, LANES), F32),
        moved=peers * WORDS * LANES * 4,
    )(arrived)
    sums = lax.all_to_all(quarter, "scene", 0, 0, tiled=True)
    conv_out = call(
        functools.partial(receive_kernel, free=free),
        shape((own_rows, out_width), BF16),
        scratch=(pltpu.VMEM((send_rows, out_width), F32),),
        flops=4 * send_rows * own_rows * out_width,
        moved=send_rows * out_width * 4,
    )(own, arrived, recv)

    own_in = in_width // peers
    sums = sums.reshape(scenes, own_in, blocks, 2, LANES).transpose(1, 3, 0, 2, 4)
    sums = sums.reshape(own_in, group, blocks * LANES)[:, :, :columns]
    kernel_grad = sums.reshape(own_in, offsets, out_width)
    kernel_grad = kernel_grad.transpose(1, 0, 2).reshape(offsets, own_in * out_width)
    normalizer = 1.0 / math.sqrt(scenes * peers * own_rows)
    return (conv_out[None], input_grad[None], kernel_grad * normalizer)


def solution(mesh):
    scenes = mesh.devices.shape[1]
    fine = Mesh(mesh.devices.reshape(8, 8, 2, scenes), ("y", "z", "core", "scene"))
    voxels = P("scene", SPACE)
    return jax.shard_map(
        local,
        mesh=fine,
        in_specs=(voxels, voxels, voxels, P(), voxels, voxels, voxels),
        out_specs=(voxels, voxels, P(None, SPACE)),
        check_vma=False,
    )
```

```python
import functools
import math

import jax
import jax.numpy as jnp
from jax import lax
from jax.experimental import pallas as pl
from jax.experimental.pallas import tpu as pltpu
from jax.sharding import Mesh
from jax.sharding import PartitionSpec as P

F32 = jnp.float32
BF16 = jnp.bfloat16
I32 = jnp.int32
LANES = 128
STEP = 4
WORDS = 8
VMEM_BYTES = 24 * 1024 * 1024
MOST_VMEM = 64 * 1024 * 1024 - 128 * 1024
SPACE = ("y", "z", "core")
GROUP = ("core", "scene")


def call(kernel, outs, scratch=(), flops=0, moved=0, vmem=VMEM_BYTES, **specs):
    return pl.pallas_call(
        kernel,
        out_shape=outs,
        scratch_shapes=list(scratch),
        **specs,
        compiler_params=pltpu.CompilerParams(vmem_limit_bytes=vmem),
        cost_estimate=pl.CostEstimate(flops=flops, bytes_accessed=moved, transcendentals=0),
    )


def rows_iota(rows, start=0):
    return lax.broadcasted_iota(I32, (rows, LANES), 0) + start


def one_hot(iota, row):
    return jnp.where(iota == row, 1.0, 0.0).astype(BF16)


def one_hot_16(iota, row):
    rows = iota.shape[0]
    narrow = jnp.broadcast_to(row, (16, LANES)).astype(jnp.int16)
    narrow = jnp.concatenate([narrow] * (rows // 16), axis=0)
    return jnp.where(iota == narrow, jnp.ones((rows, LANES), BF16), jnp.zeros((rows, LANES), BF16))


def split_two(value):
    high = value.astype(BF16)
    low = (value - high.astype(F32)).astype(BF16)
    return high, low


def lane_block(k):
    return slice(k * LANES, (k + 1) * LANES)


def gather_kernel(
    cot_any, mask_any, recv_any, in_any, pair_any, shared_ref, out_ref, cot_ref, mask_ref, recv_ref, in_ref, pair_ref, digit_ref, sems, *, targets
):
    pairs = (
        (cot_any, cot_ref),
        (mask_any, mask_ref),
        (recv_any, recv_ref),
        (in_any, in_ref),
        (pair_any, pair_ref),
    )
    copies = [pltpu.make_async_copy(a, b, sems.at[i]) for i, (a, b) in enumerate(pairs)]
    for copy in copies:
        copy.start()
    digit_ref[...] = jnp.zeros_like(digit_ref)
    for copy in copies:
        copy.wait()
    up = (cot_ref[...].astype(F32) * mask_ref[...].astype(F32)).astype(BF16)
    shared_ref[0:LANES, :] = up.T
    iota = rows_iota(LANES)
    for g in range(recv_ref.shape[0]):
        hot = one_hot(iota, recv_ref[g : g + 1, :])
        rows = lax.dot_general(hot, up, (((0,), (0,)), ((), ())), preferred_element_type=F32)
        out_ref[lane_block(g), :] = rows.astype(BF16)
    picks = rows_iota(16)
    for k in range(in_ref.shape[0]):
        hot = one_hot(iota, in_ref[k])
        target = pair_ref[k]
        code = jnp.where(target < targets, target + 1, 0)
        digits = jnp.where(picks == 0, code >> 7, jnp.where(picks == 1, code & 127, 0))
        found = lax.dot_general(
            digits.astype(F32).astype(BF16), hot, (((1,), (1,)), ((), ())), preferred_element_type=F32
        )
        digit_ref[k : k + 1, :] = found[0:1]
        digit_ref[32 + k : 33 + k, :] = found[1:2]
    shared_ref[LANES : LANES + 64, :] = digit_ref[...].astype(BF16)


def table_kernel(shared_ref, table_ref, turned_ref):
    high = shared_ref[LANES : LANES + 32, :].astype(F32)
    low = shared_ref[LANES + 32 : LANES + 64, :].astype(F32)
    table_ref[...] = (high * 128.0 + low - 1.0).astype(I32)
    turned_ref[...] = shared_ref[0:LANES, :]


def lookup_kernel(turned_ref, back_ref, table_ref, gathered_any, ext_ref, hot_ref, gathered_ref, sems):
    blocks = back_ref.shape[0] // LANES
    offsets = gathered_ref.shape[0] // LANES
    ext_ref[:, 0:LANES] = turned_ref[...]
    for b in range(blocks):
        ext_ref[:, lane_block(b + 1)] = back_ref[lane_block(b), :].T
    iota = rows_iota((blocks + 1) * LANES).astype(jnp.int16)
    copies = []
    for first in range(0, offsets, STEP):
        count = min(STEP, offsets - first)
        slot = (first // STEP) % 2
        for k in range(count):
            hot_ref[slot, :, lane_block(k)] = one_hot_16(iota, table_ref[first + k : first + k + 1, :])
        rows = jnp.dot(
            ext_ref[...], hot_ref[slot, :, : count * LANES], preferred_element_type=F32
        ).astype(BF16)
        for k in range(count):
            gathered_ref[lane_block(first + k), :] = rows[:, lane_block(k)]
        part = pl.ds(first * LANES, count * LANES)
        copies.append(
            pltpu.make_async_copy(gathered_ref.at[part], gathered_any.at[part], sems.at[first // STEP])
        )
        copies[-1].start()
    for copy in copies:
        copy.wait()


def encode(value, top):
    level = jnp.ceil(jnp.log2(jnp.maximum(top, 1e-36)) * 8.0)
    code = jnp.round(value * jnp.exp2(level * -0.125) * 32767.0)
    return jnp.clip(code, -32767.0, 32767.0).astype(I32), level.astype(I32)


def unit(level):
    return jnp.exp2(level.astype(F32) * 0.125) * (1.0 / 32767.0)


def join(first, second):
    return (first << 16) | (second & 0xFFFF)


def halves(word):
    return (word >> 16).astype(F32), ((word << 16) >> 16).astype(F32)


def row_top(value):
    return jnp.max(jnp.abs(value), axis=1, keepdims=True)


def fetch(w_any, w_ref, gathered_any, gathered_ref, sems):
    offsets = w_ref.shape[0]
    parts = sems.shape[1]
    step = offsets // parts
    copies = []
    for i in range(parts):
        part = pl.ds(i * step, step)
        rows = pl.ds(i * step * LANES, step * LANES)
        copies.append(
            (
                pltpu.make_async_copy(w_any.at[part], w_ref.at[part], sems.at[0, i]),
                pltpu.make_async_copy(gathered_any.at[rows], gathered_ref.at[rows], sems.at[1, i]),
            )
        )
        for copy in copies[-1]:
            copy.start()
    return copies, step


def forward_kernel(
    near_ref,
    w_any,
    table_ref,
    gathered_any,
    own_any,
    word_ref,
    grad_ref,
    w_ref,
    gathered_ref,
    terms_ref,
    hot_ref,
    send_ref,
    sems,
    own_sem,
    *,
    free,
):
    offsets = w_ref.shape[0]
    copies, step = fetch(w_any, w_ref, gathered_any, gathered_ref, sems)
    total = jnp.zeros((w_ref.shape[1], LANES), F32)
    for k in range(offsets):
        if k % step == 0:
            for copy in copies[k // step]:
                copy.wait()
        high, low = split_two(jnp.dot(near_ref[0], w_ref[k], preferred_element_type=F32))
        terms_ref[lane_block(k), 0:LANES] = high
        terms_ref[lane_block(k), LANES : 2 * LANES] = low
        total += jnp.dot(w_ref[k], gathered_ref[lane_block(k), :], preferred_element_type=F32)
    grad_ref[...] = total.T.astype(BF16)
    iota = rows_iota(LANES).astype(jnp.int16)

    span = hot_ref.shape[1]
    own_rows = own_any.shape[0]
    own_copy = pltpu.make_async_copy(send_ref.at[pl.ds(0, own_rows)], own_any, own_sem)
    for i in range(send_ref.shape[0] // span):
        for j in range(span // LANES):
            for k in range(offsets):
                row = table_ref[k : k + 1, :] - (i * span + j * LANES)
                hot_ref[i % 2, lane_block(j), lane_block(k)] = one_hot_16(iota, row)
        both = jnp.dot(hot_ref[i % 2], terms_ref[...], preferred_element_type=F32)
        send_ref[pl.ds(i * span, span), :] = both[:, :LANES] + both[:, LANES:]
        if i == 0:
            own_copy.start()
    peers = word_ref.shape[1]
    lane = lax.broadcasted_iota(I32, (peers, LANES), 1)
    levels = jnp.zeros((peers, LANES), I32)
    for r in range(4):
        words = []
        for slot in (r, r + 4):
            value = send_ref[pl.ds(own_rows + slot, peers, stride=8), :]
            code, level = encode(value, row_top(value))
            words.append(code)
            levels = jnp.where(lane == free + slot, level, levels)
        word_ref[r] = join(*words)
    word_ref[4] = levels
    own_copy.wait()


def pack_kernel(g_ref, near_ref, far_ref, word_ref, out_ref, turn_ref):
    columns = g_ref.shape[1]
    peers = word_ref.shape[1]
    blocks = turn_ref.shape[0]
    scenes = near_ref.shape[0]
    core, scene = (lax.axis_index(axis) for axis in GROUP)
    total = jnp.zeros((columns, near_ref.shape[2]), F32)
    for s in range(g_ref.shape[0]):
        x_ref, holder = (near_ref, core) if s < scenes else (far_ref, 1 - core)
        sender = holder * scenes + (scene ^ (s % scenes))
        total += jnp.dot(g_ref[sender], x_ref[s % scenes], preferred_element_type=F32)
    rest = blocks * LANES - columns
    total = jnp.concatenate([total, jnp.zeros((rest, total.shape[1]), F32)], axis=0)
    for h in range(blocks):
        turn_ref[h] = total[lane_block(h), :].T
    for r in range(4):
        out_ref[pl.ds(r, peers, stride=WORDS), :] = word_ref[r]
    parts = [[turn_ref[h, pl.ds(c, peers, stride=2), :] for c in range(2)] for h in range(blocks)]
    top = functools.reduce(jnp.maximum, [jnp.abs(part) for pair in parts for part in pair])
    top = jnp.max(top, axis=1, keepdims=True)
    free = LANES - rest
    lane = lax.broadcasted_iota(I32, (peers, LANES), 1)
    for h in range(blocks):
        codes = [encode(part, top) for part in parts[h]]
        word = join(codes[0][0], codes[1][0])
        if h == blocks - 1:
            levels = jnp.where(lane == free + 8, codes[0][1], word_ref[4])
            word = jnp.where(lane < free, word, levels)
        out_ref[pl.ds(4 + h, peers, stride=WORDS), :] = word


def sum_kernel(arrived_ref, out_ref, *, free):
    peers = arrived_ref.shape[0] // WORDS
    words = [arrived_ref[pl.ds(4 + h, peers, stride=WORDS), :] for h in range(4)]
    scale = unit(words[-1][:, free + 8 : free + 9])
    for h in range(4):
        for c, value in enumerate(halves(words[h])):
            total = (value * scale).reshape(peers // 8, 8, LANES).sum(axis=0)
            total = (total[0:2] + total[2:4]) + (total[4:6] + total[6:8])
            row = 2 * (4 * c + h)
            for s in range(out_ref.shape[0]):
                out_ref[s, row : row + 2, :] = total


def receive_kernel(own_ref, arrived_ref, recv_ref, out_ref, rows_ref, *, free):
    peers = arrived_ref.shape[0] // WORDS
    iota = rows_iota(LANES)
    levels = arrived_ref[pl.ds(WORDS - 1, peers, stride=WORDS), :]
    for r in range(4):
        pair = halves(arrived_ref[pl.ds(r, peers, stride=WORDS), :])
        for value, slot in zip(pair, (r, r + 4)):
            scale = unit(levels[:, free + slot : free + slot + 1])
            rows_ref[pl.ds(slot, peers, stride=8), :] = value * scale
    total = own_ref[...]
    for g in range(recv_ref.shape[0]):
        hot = one_hot(iota, recv_ref[g : g + 1, :])
        high, low = split_two(rows_ref[lane_block(g), :])
        total += jnp.dot(hot, high, preferred_element_type=F32)
        total += jnp.dot(hot, low, preferred_element_type=F32)
    out_ref[...] = total.astype(BF16)


def local(features, cotangent, relu_mask, weight, pair_in, pair_out, recv_index):
    x = features[0]
    own_rows, in_width = x.shape
    offsets, unused, out_width = weight.shape
    peers = lax.axis_size(SPACE)
    group = lax.axis_size(GROUP)
    scenes = lax.axis_size("scene")
    send_rows = recv_index.shape[2]
    slots = send_rows // peers
    targets = own_rows + send_rows
    columns = offsets * out_width // group
    recv = recv_index.reshape(send_rows // LANES, LANES)
    shape = jax.ShapeDtypeStruct

    hbm = pl.BlockSpec(memory_space=pltpu.HBM)
    vmem = pl.BlockSpec(memory_space=pltpu.VMEM)
    blocks = -(-columns // LANES)
    free = columns - (blocks - 1) * LANES

    lists = [pairs.reshape(offsets, 1, own_rows) for pairs in (pair_in, pair_out)]
    shared, outgoing = call(
        functools.partial(gather_kernel, targets=targets),
        (shape((out_width + 64, own_rows), BF16), shape((send_rows, out_width), BF16)),
        scratch=(
            pltpu.VMEM((own_rows, out_width), BF16),
            pltpu.VMEM((own_rows, out_width), I32),
            pltpu.VMEM(recv.shape, I32),
            pltpu.VMEM(lists[0].shape, I32),
            pltpu.VMEM(lists[1].shape, I32),
            pltpu.VMEM((64, own_rows), F32),
            pltpu.SemaphoreType.DMA((5,)),
        ),
        in_specs=[hbm] * 5,
        vmem=MOST_VMEM,
        flops=2 * send_rows * own_rows * out_width,
        moved=send_rows * out_width * 3,
    )(cotangent[0], relu_mask[0], recv, *lists)
    own_x, outgoing = lax.optimization_barrier((x, outgoing))
    returned = lax.all_to_all(outgoing.reshape(peers, slots, out_width), SPACE, 0, 0, tiled=True)

    swap = [(0, 1), (1, 0)]
    ring = [
        lax.ppermute(own_x, "scene", [(i, i ^ d) for i in range(scenes)]) for d in range(1, scenes)
    ]

    table, turned = call(
        table_kernel, (shape((32, own_rows), I32), shape((out_width, own_rows), BF16))
    )(shared)
    gathered = call(
        lookup_kernel,
        shape((offsets * out_width, own_rows), BF16),
        scratch=(
            pltpu.VMEM((out_width, targets), BF16),
            pltpu.VMEM((2, targets, STEP * LANES), BF16),
            pltpu.VMEM((offsets * out_width, own_rows), BF16),
            pltpu.SemaphoreType.DMA((-(-offsets // STEP),)),
        ),
        out_specs=hbm,
    )(turned, returned.reshape(send_rows, out_width), table)
    gathered, *ring = lax.optimization_barrier((gathered, *ring))
    group_g = lax.all_to_all(gathered.reshape(group, columns, own_rows), GROUP, 0, 0, tiled=True)

    near = jnp.stack([x] + ring)
    own, words, input_grad = call(
        functools.partial(forward_kernel, free=free),
        (
            shape((own_rows, out_width), F32),
            shape((5, peers, out_width), I32),
            shape((own_rows, in_width), BF16),
        ),
        scratch=(
            pltpu.VMEM(weight.shape, BF16),
            pltpu.VMEM((offsets * out_width, own_rows), BF16),
            pltpu.VMEM((offsets * own_rows, 2 * out_width), BF16),
            pltpu.VMEM((2, targets // 3, offsets * own_rows), BF16),
            pltpu.VMEM((targets, out_width), F32),
            pltpu.SemaphoreType.DMA((2, 3)),
            pltpu.SemaphoreType.DMA,
        ),
        in_specs=[vmem, hbm, vmem, hbm],
        out_specs=(hbm, vmem, vmem),
    )(near, weight, table, gathered)

    far = lax.ppermute(near, "core", swap)
    packed = call(
        pack_kernel,
        shape((peers * WORDS, LANES), I32),
        scratch=(pltpu.VMEM((blocks, in_width, LANES), F32),),
        flops=2 * columns * in_width * own_rows * group,
        moved=peers * WORDS * LANES * 8,
    )(group_g, near, far, words)
    arrived = lax.all_to_all(packed.reshape(peers, WORDS, LANES), SPACE, 0, 0, tiled=True)
    arrived = arrived.reshape(peers * WORDS, LANES)

    quarter = call(
        functools.partial(sum_kernel, free=free),
        shape((scenes, 16, LANES), F32),
        moved=peers * WORDS * LANES * 4,
    )(arrived)
    sums = lax.all_to_all(quarter, "scene", 0, 0, tiled=True)
    conv_out = call(
        functools.partial(receive_kernel, free=free),
        shape((own_rows, out_width), BF16),
        scratch=(pltpu.VMEM((send_rows, out_width), F32),),
        flops=4 * send_rows * own_rows * out_width,
        moved=send_rows * out_width * 4,
    )(own, arrived, recv)

    own_in = in_width // peers
    sums = sums.reshape(scenes, own_in, blocks, 2, LANES).transpose(1, 3, 0, 2, 4)
    sums = sums.reshape(own_in, group, blocks * LANES)[:, :, :columns]
    kernel_grad = sums.reshape(own_in, offsets, out_width)
    kernel_grad = kernel_grad.transpose(1, 0, 2).reshape(offsets, own_in * out_width)
    normalizer = 1.0 / math.sqrt(scenes * peers * own_rows)
    return (conv_out[None], input_grad[None], kernel_grad * normalizer)


def solution(mesh):
    scenes = mesh.devices.shape[1]
    fine = Mesh(mesh.devices.reshape(8, 8, 2, scenes), ("y", "z", "core", "scene"))
    voxels = P("scene", SPACE)
    return jax.shard_map(
        local,
        mesh=fine,
        in_specs=(voxels, voxels, voxels, P(), voxels, voxels, voxels),
        out_specs=(voxels, voxels, P(None, SPACE)),
        check_vma=False,
    )
```

```python
import functools
import math

import jax
import jax.numpy as jnp
from jax import lax
from jax.experimental import pallas as pl
from jax.experimental.pallas import tpu as pltpu
from jax.sharding import Mesh
from jax.sharding import PartitionSpec as P

F32 = jnp.float32
BF16 = jnp.bfloat16
I32 = jnp.int32
LANES = 128
STEP = 4
WORDS = 8
VMEM_BYTES = 24 * 1024 * 1024
MOST_VMEM = 64 * 1024 * 1024 - 128 * 1024
SPACE = ("y", "z", "core")
GROUP = ("core", "scene")


def call(kernel, outs, scratch=(), flops=0, moved=0, vmem=VMEM_BYTES, **specs):
    return pl.pallas_call(
        kernel,
        out_shape=outs,
        scratch_shapes=list(scratch),
        **specs,
        compiler_params=pltpu.CompilerParams(vmem_limit_bytes=vmem),
        cost_estimate=pl.CostEstimate(flops=flops, bytes_accessed=moved, transcendentals=0),
    )


def rows_iota(rows, start=0):
    return lax.broadcasted_iota(I32, (rows, LANES), 0) + start


def one_hot(iota, row):
    return jnp.where(iota == row, 1.0, 0.0).astype(BF16)


def one_hot_16(iota, row):
    rows = iota.shape[0]
    narrow = jnp.broadcast_to(row, (16, LANES)).astype(jnp.int16)
    narrow = jnp.concatenate([narrow] * (rows // 16), axis=0)
    return jnp.where(iota == narrow, jnp.ones((rows, LANES), BF16), jnp.zeros((rows, LANES), BF16))


def split_two(value):
    high = value.astype(BF16)
    low = (value - high.astype(F32)).astype(BF16)
    return high, low


def lane_block(k):
    return slice(k * LANES, (k + 1) * LANES)


def gather_kernel(
    cot_any, mask_any, recv_any, in_any, pair_any, shared_ref, out_ref, cot_ref, mask_ref, recv_ref, in_ref, pair_ref, digit_ref, sems, *, targets
):
    pairs = (
        (cot_any, cot_ref),
        (mask_any, mask_ref),
        (recv_any, recv_ref),
        (in_any, in_ref),
        (pair_any, pair_ref),
    )
    copies = [pltpu.make_async_copy(a, b, sems.at[i]) for i, (a, b) in enumerate(pairs)]
    for copy in copies:
        copy.start()
    digit_ref[...] = jnp.zeros_like(digit_ref)
    for copy in copies:
        copy.wait()
    up = (cot_ref[...].astype(F32) * mask_ref[...].astype(F32)).astype(BF16)
    shared_ref[0:LANES, :] = up.T
    iota = rows_iota(LANES)
    for g in range(recv_ref.shape[0]):
        hot = one_hot(iota, recv_ref[g : g + 1, :])
        rows = lax.dot_general(hot, up, (((0,), (0,)), ((), ())), preferred_element_type=F32)
        out_ref[lane_block(g), :] = rows.astype(BF16)
    picks = rows_iota(16)
    for k in range(in_ref.shape[0]):
        hot = one_hot(iota, in_ref[k])
        target = pair_ref[k]
        code = jnp.where(target < targets, target + 1, 0)
        digits = jnp.where(picks == 0, code >> 7, jnp.where(picks == 1, code & 127, 0))
        found = lax.dot_general(
            digits.astype(F32).astype(BF16), hot, (((1,), (1,)), ((), ())), preferred_element_type=F32
        )
        digit_ref[k : k + 1, :] = found[0:1]
        digit_ref[32 + k : 33 + k, :] = found[1:2]
    shared_ref[LANES : LANES + 64, :] = digit_ref[...].astype(BF16)


def table_kernel(shared_ref, table_ref, turned_ref):
    high = shared_ref[LANES : LANES + 32, :].astype(F32)
    low = shared_ref[LANES + 32 : LANES + 64, :].astype(F32)
    table_ref[...] = (high * 128.0 + low - 1.0).astype(I32)
    turned_ref[...] = shared_ref[0:LANES, :]


def lookup_kernel(turned_ref, back_ref, table_ref, gathered_any, ext_ref, hot_ref, gathered_ref, sems):
    blocks = back_ref.shape[0] // LANES
    offsets = gathered_ref.shape[0] // LANES
    ext_ref[:, 0:LANES] = turned_ref[...]
    for b in range(blocks):
        ext_ref[:, lane_block(b + 1)] = back_ref[lane_block(b), :].T
    iota = rows_iota((blocks + 1) * LANES).astype(jnp.int16)
    copies = []
    for first in range(0, offsets, STEP):
        count = min(STEP, offsets - first)
        slot = (first // STEP) % 2
        for k in range(count):
            hot_ref[slot, :, lane_block(k)] = one_hot_16(iota, table_ref[first + k : first + k + 1, :])
        rows = jnp.dot(
            ext_ref[...], hot_ref[slot, :, : count * LANES], preferred_element_type=F32
        ).astype(BF16)
        for k in range(count):
            gathered_ref[lane_block(first + k), :] = rows[:, lane_block(k)]
        part = pl.ds(first * LANES, count * LANES)
        copies.append(
            pltpu.make_async_copy(gathered_ref.at[part], gathered_any.at[part], sems.at[first // STEP])
        )
        copies[-1].start()
    for copy in copies:
        copy.wait()


def encode(value, top):
    level = jnp.ceil(jnp.log2(jnp.maximum(top, 1e-36)) * 8.0)
    code = jnp.round(value * jnp.exp2(level * -0.125) * 32767.0)
    return jnp.clip(code, -32767.0, 32767.0).astype(I32), level.astype(I32)


def unit(level):
    return jnp.exp2(level.astype(F32) * 0.125)


def join(first, second):
    return (first << 16) | (second & 0xFFFF)


def halves(word):
    scale = 1.0 / 32767.0
    return (word >> 16).astype(F32) * scale, ((word << 16) >> 16).astype(F32) * scale


def row_top(value):
    return jnp.max(jnp.abs(value), axis=1, keepdims=True)


def fetch(w_any, w_ref, gathered_any, gathered_ref, sems):
    offsets = w_ref.shape[0]
    parts = sems.shape[1]
    step = offsets // parts
    copies = []
    for i in range(parts):
        part = pl.ds(i * step, step)
        rows = pl.ds(i * step * LANES, step * LANES)
        copies.append(
            (
                pltpu.make_async_copy(w_any.at[part], w_ref.at[part], sems.at[0, i]),
                pltpu.make_async_copy(gathered_any.at[rows], gathered_ref.at[rows], sems.at[1, i]),
            )
        )
        for copy in copies[-1]:
            copy.start()
    return copies, step


def forward_kernel(
    near_ref,
    w_any,
    table_ref,
    gathered_any,
    own_any,
    word_ref,
    grad_ref,
    w_ref,
    gathered_ref,
    terms_ref,
    hot_ref,
    send_ref,
    sems,
    own_sem,
    *,
    free,
):
    offsets = w_ref.shape[0]
    copies, step = fetch(w_any, w_ref, gathered_any, gathered_ref, sems)
    total = jnp.zeros((w_ref.shape[1], LANES), F32)
    for k in range(offsets):
        if k % step == 0:
            for copy in copies[k // step]:
                copy.wait()
        high, low = split_two(jnp.dot(near_ref[0], w_ref[k], preferred_element_type=F32))
        terms_ref[lane_block(k), 0:LANES] = high
        terms_ref[lane_block(k), LANES : 2 * LANES] = low
        total += jnp.dot(w_ref[k], gathered_ref[lane_block(k), :], preferred_element_type=F32)
    grad_ref[...] = total.T.astype(BF16)
    iota = rows_iota(LANES).astype(jnp.int16)

    span = hot_ref.shape[1]
    own_rows = own_any.shape[0]
    own_copy = pltpu.make_async_copy(send_ref.at[pl.ds(0, own_rows)], own_any, own_sem)
    for i in range(send_ref.shape[0] // span):
        for j in range(span // LANES):
            for k in range(offsets):
                row = table_ref[k : k + 1, :] - (i * span + j * LANES)
                hot_ref[i % 2, lane_block(j), lane_block(k)] = one_hot_16(iota, row)
        both = jnp.dot(hot_ref[i % 2], terms_ref[...], preferred_element_type=F32)
        send_ref[pl.ds(i * span, span), :] = both[:, :LANES] + both[:, LANES:]
        if i == 0:
            own_copy.start()
    peers = word_ref.shape[1]
    lane = lax.broadcasted_iota(I32, (peers, LANES), 1)
    levels = jnp.zeros((peers, LANES), I32)
    for r in range(4):
        words = []
        for slot in (r, r + 4):
            value = send_ref[pl.ds(own_rows + slot, peers, stride=8), :]
            code, level = encode(value, row_top(value))
            words.append(code)
            levels = jnp.where(lane == free + slot, level, levels)
        word_ref[r] = join(*words)
    word_ref[4] = levels
    own_copy.wait()


def pack_kernel(g_ref, near_ref, far_ref, word_ref, out_ref, turn_ref):
    columns = g_ref.shape[1]
    peers = word_ref.shape[1]
    blocks = turn_ref.shape[0]
    scenes = near_ref.shape[0]
    core, scene = (lax.axis_index(axis) for axis in GROUP)
    total = jnp.zeros((columns, near_ref.shape[2]), F32)
    for s in range(0, g_ref.shape[0], 2):
        x_ref, holder = (near_ref, core) if s < scenes else (far_ref, 1 - core)
        senders = [holder * scenes + (scene ^ ((s + i) % scenes)) for i in range(2)]
        both = jnp.concatenate([g_ref[sender] for sender in senders], axis=1)
        first = s % scenes
        rows = x_ref[first : first + 2].reshape(both.shape[1], total.shape[1])
        total += jnp.dot(both, rows, preferred_element_type=F32)
    rest = blocks * LANES - columns
    total = jnp.concatenate([total, jnp.zeros((rest, total.shape[1]), F32)], axis=0)
    for h in range(blocks):
        turn_ref[h] = total[lane_block(h), :].T
    for r in range(4):
        out_ref[pl.ds(r, peers, stride=WORDS), :] = word_ref[r]
    parts = [[turn_ref[h, pl.ds(c, peers, stride=2), :] for c in range(2)] for h in range(blocks)]
    top = functools.reduce(jnp.maximum, [jnp.abs(part) for pair in parts for part in pair])
    top = jnp.max(top, axis=1, keepdims=True)
    free = LANES - rest
    lane = lax.broadcasted_iota(I32, (peers, LANES), 1)
    for h in range(blocks):
        codes = [encode(part, top) for part in parts[h]]
        word = join(codes[0][0], codes[1][0])
        if h == blocks - 1:
            levels = jnp.where(lane == free + 8, codes[0][1], word_ref[4])
            word = jnp.where(lane < free, word, levels)
        out_ref[pl.ds(4 + h, peers, stride=WORDS), :] = word


def sum_kernel(arrived_ref, out_ref, *, free):
    peers = arrived_ref.shape[0] // WORDS
    words = [arrived_ref[pl.ds(4 + h, peers, stride=WORDS), :] for h in range(4)]
    scale = unit(words[-1][:, free + 8 : free + 9])
    for h in range(4):
        for c, value in enumerate(halves(words[h])):
            total = (value * scale).reshape(peers // 8, 8, LANES).sum(axis=0)
            total = (total[0:2] + total[2:4]) + (total[4:6] + total[6:8])
            row = 2 * (4 * c + h)
            for s in range(out_ref.shape[0]):
                out_ref[s, row : row + 2, :] = total


def receive_kernel(own_ref, arrived_ref, recv_ref, out_ref, rows_ref, *, free):
    peers = arrived_ref.shape[0] // WORDS
    iota = rows_iota(LANES)
    levels = arrived_ref[pl.ds(WORDS - 1, peers, stride=WORDS), :]
    for r in range(4):
        pair = halves(arrived_ref[pl.ds(r, peers, stride=WORDS), :])
        for value, slot in zip(pair, (r, r + 4)):
            scale = unit(levels[:, free + slot : free + slot + 1])
            rows_ref[pl.ds(slot, peers, stride=8), :] = value * scale
    total = own_ref[...]
    for g in range(recv_ref.shape[0]):
        hot = one_hot(iota, recv_ref[g : g + 1, :])
        high, low = split_two(rows_ref[lane_block(g), :])
        total += jnp.dot(hot, high, preferred_element_type=F32)
        total += jnp.dot(hot, low, preferred_element_type=F32)
    out_ref[...] = total.astype(BF16)


def local(features, cotangent, relu_mask, weight, pair_in, pair_out, recv_index):
    x = features[0]
    own_rows, in_width = x.shape
    offsets, unused, out_width = weight.shape
    peers = lax.axis_size(SPACE)
    group = lax.axis_size(GROUP)
    scenes = lax.axis_size("scene")
    send_rows = recv_index.shape[2]
    slots = send_rows // peers
    targets = own_rows + send_rows
    columns = offsets * out_width // group
    recv = recv_index.reshape(send_rows // LANES, LANES)
    shape = jax.ShapeDtypeStruct

    hbm = pl.BlockSpec(memory_space=pltpu.HBM)
    vmem = pl.BlockSpec(memory_space=pltpu.VMEM)
    blocks = -(-columns // LANES)
    free = columns - (blocks - 1) * LANES

    lists = [pairs.reshape(offsets, 1, own_rows) for pairs in (pair_in, pair_out)]
    shared, outgoing = call(
        functools.partial(gather_kernel, targets=targets),
        (shape((out_width + 64, own_rows), BF16), shape((send_rows, out_width), BF16)),
        scratch=(
            pltpu.VMEM((own_rows, out_width), BF16),
            pltpu.VMEM((own_rows, out_width), I32),
            pltpu.VMEM(recv.shape, I32),
            pltpu.VMEM(lists[0].shape, I32),
            pltpu.VMEM(lists[1].shape, I32),
            pltpu.VMEM((64, own_rows), F32),
            pltpu.SemaphoreType.DMA((5,)),
        ),
        in_specs=[hbm] * 5,
        vmem=MOST_VMEM,
        flops=2 * send_rows * own_rows * out_width,
        moved=send_rows * out_width * 3,
    )(cotangent[0], relu_mask[0], recv, *lists)
    own_x, outgoing = lax.optimization_barrier((x, outgoing))
    returned = lax.all_to_all(outgoing.reshape(peers, slots, out_width), SPACE, 0, 0, tiled=True)

    swap = [(0, 1), (1, 0)]
    ring = [
        lax.ppermute(own_x, "scene", [(i, i ^ d) for i in range(scenes)]) for d in range(1, scenes)
    ]

    table, turned = call(
        table_kernel, (shape((32, own_rows), I32), shape((out_width, own_rows), BF16))
    )(shared)
    gathered = call(
        lookup_kernel,
        shape((offsets * out_width, own_rows), BF16),
        scratch=(
            pltpu.VMEM((out_width, targets), BF16),
            pltpu.VMEM((2, targets, STEP * LANES), BF16),
            pltpu.VMEM((offsets * out_width, own_rows), BF16),
            pltpu.SemaphoreType.DMA((-(-offsets // STEP),)),
        ),
        out_specs=hbm,
    )(turned, returned.reshape(send_rows, out_width), table)
    gathered, *ring = lax.optimization_barrier((gathered, *ring))
    group_g = lax.all_to_all(gathered.reshape(group, columns, own_rows), GROUP, 0, 0, tiled=True)

    near = jnp.stack([x] + ring)
    own, words, input_grad = call(
        functools.partial(forward_kernel, free=free),
        (
            shape((own_rows, out_width), F32),
            shape((5, peers, out_width), I32),
            shape((own_rows, in_width), BF16),
        ),
        scratch=(
            pltpu.VMEM(weight.shape, BF16),
            pltpu.VMEM((offsets * out_width, own_rows), BF16),
            pltpu.VMEM((offsets * own_rows, 2 * out_width), BF16),
            pltpu.VMEM((2, targets // 3, offsets * own_rows), BF16),
            pltpu.VMEM((targets, out_width), F32),
            pltpu.SemaphoreType.DMA((2, 3)),
            pltpu.SemaphoreType.DMA,
        ),
        in_specs=[vmem, hbm, vmem, hbm],
        out_specs=(hbm, vmem, vmem),
    )(near, weight, table, gathered)

    far = lax.ppermute(near, "core", swap)
    packed = call(
        pack_kernel,
        shape((peers * WORDS, LANES), I32),
        scratch=(pltpu.VMEM((blocks, in_width, LANES), F32),),
        flops=2 * columns * in_width * own_rows * group,
        moved=peers * WORDS * LANES * 8,
    )(group_g, near, far, words)
    arrived = lax.all_to_all(packed.reshape(peers, WORDS, LANES), SPACE, 0, 0, tiled=True)
    arrived = arrived.reshape(peers * WORDS, LANES)

    quarter = call(
        functools.partial(sum_kernel, free=free),
        shape((scenes, 16, LANES), F32),
        moved=peers * WORDS * LANES * 4,
    )(arrived)
    sums = lax.all_to_all(quarter, "scene", 0, 0, tiled=True)
    conv_out = call(
        functools.partial(receive_kernel, free=free),
        shape((own_rows, out_width), BF16),
        scratch=(pltpu.VMEM((send_rows, out_width), F32),),
        flops=4 * send_rows * own_rows * out_width,
        moved=send_rows * out_width * 4,
    )(own, arrived, recv)

    own_in = in_width // peers
    sums = sums.reshape(scenes, own_in, blocks, 2, LANES).transpose(1, 3, 0, 2, 4)
    sums = sums.reshape(own_in, group, blocks * LANES)[:, :, :columns]
    kernel_grad = sums.reshape(own_in, offsets, out_width)
    kernel_grad = kernel_grad.transpose(1, 0, 2).reshape(offsets, own_in * out_width)
    normalizer = 1.0 / math.sqrt(scenes * peers * own_rows)
    return (conv_out[None], input_grad[None], kernel_grad * normalizer)


def solution(mesh):
    scenes = mesh.devices.shape[1]
    fine = Mesh(mesh.devices.reshape(8, 8, 2, scenes), ("y", "z", "core", "scene"))
    voxels = P("scene", SPACE)
    return jax.shard_map(
        local,
        mesh=fine,
        in_specs=(voxels, voxels, voxels, P(), voxels, voxels, voxels),
        out_specs=(voxels, voxels, P(None, SPACE)),
        check_vma=False,
    )
```

```python
import functools
import math

import jax
import jax.numpy as jnp
from jax import lax
from jax.experimental import pallas as pl
from jax.experimental.pallas import tpu as pltpu
from jax.sharding import Mesh
from jax.sharding import PartitionSpec as P

F32 = jnp.float32
BF16 = jnp.bfloat16
I32 = jnp.int32
LANES = 128
STEP = 4
WORDS = 8
VMEM_BYTES = 24 * 1024 * 1024
MOST_VMEM = 64 * 1024 * 1024 - 128 * 1024
SPACE = ("y", "z", "core")
GROUP = ("core", "scene")


def call(kernel, outs, scratch=(), flops=0, moved=0, vmem=VMEM_BYTES, **specs):
    return pl.pallas_call(
        kernel,
        out_shape=outs,
        scratch_shapes=list(scratch),
        **specs,
        compiler_params=pltpu.CompilerParams(vmem_limit_bytes=vmem),
        cost_estimate=pl.CostEstimate(flops=flops, bytes_accessed=moved, transcendentals=0),
    )


def rows_iota(rows, start=0):
    return lax.broadcasted_iota(I32, (rows, LANES), 0) + start


def one_hot(iota, row):
    return jnp.where(iota == row, 1.0, 0.0).astype(BF16)


def one_hot_16(iota, row):
    rows = iota.shape[0]
    narrow = jnp.broadcast_to(row, (16, LANES)).astype(jnp.int16)
    narrow = jnp.concatenate([narrow] * (rows // 16), axis=0)
    return jnp.where(iota == narrow, jnp.ones((rows, LANES), BF16), jnp.zeros((rows, LANES), BF16))


def split_two(value):
    high = value.astype(BF16)
    low = (value - high.astype(F32)).astype(BF16)
    return high, low


def lane_block(k):
    return slice(k * LANES, (k + 1) * LANES)


def gather_kernel(
    cot_any, mask_any, recv_any, in_any, pair_any, shared_ref, out_ref, cot_ref, mask_ref, recv_ref, in_ref, pair_ref, digit_ref, sems, *, targets
):
    pairs = (
        (cot_any, cot_ref),
        (mask_any, mask_ref),
        (recv_any, recv_ref),
        (in_any, in_ref),
        (pair_any, pair_ref),
    )
    copies = [pltpu.make_async_copy(a, b, sems.at[i]) for i, (a, b) in enumerate(pairs)]
    for copy in copies:
        copy.start()
    digit_ref[...] = jnp.zeros_like(digit_ref)
    for copy in copies:
        copy.wait()
    up = (cot_ref[...].astype(F32) * mask_ref[...].astype(F32)).astype(BF16)
    shared_ref[0:LANES, :] = up.T
    iota = rows_iota(LANES)
    for g in range(recv_ref.shape[0]):
        hot = one_hot(iota, recv_ref[g : g + 1, :])
        rows = lax.dot_general(hot, up, (((0,), (0,)), ((), ())), preferred_element_type=F32)
        out_ref[lane_block(g), :] = rows.astype(BF16)
    picks = rows_iota(16)
    for k in range(in_ref.shape[0]):
        hot = one_hot(iota, in_ref[k])
        target = pair_ref[k]
        code = jnp.where(target < targets, target + 1, 0)
        digits = jnp.where(picks == 0, code >> 7, jnp.where(picks == 1, code & 127, 0))
        found = lax.dot_general(
            digits.astype(F32).astype(BF16), hot, (((1,), (1,)), ((), ())), preferred_element_type=F32
        )
        digit_ref[k : k + 1, :] = found[0:1]
        digit_ref[32 + k : 33 + k, :] = found[1:2]
    shared_ref[LANES : LANES + 64, :] = digit_ref[...].astype(BF16)


def table_kernel(shared_ref, table_ref, turned_ref):
    high = shared_ref[LANES : LANES + 32, :].astype(F32)
    low = shared_ref[LANES + 32 : LANES + 64, :].astype(F32)
    table_ref[...] = (high * 128.0 + low - 1.0).astype(I32)
    turned_ref[...] = shared_ref[0:LANES, :]


def lookup_kernel(turned_ref, back_ref, table_ref, gathered_any, ext_ref, hot_ref, gathered_ref, sems):
    blocks = back_ref.shape[0] // LANES
    offsets = gathered_ref.shape[0] // LANES
    ext_ref[:, 0:LANES] = turned_ref[...]
    for b in range(blocks):
        ext_ref[:, lane_block(b + 1)] = back_ref[lane_block(b), :].T
    iota = rows_iota((blocks + 1) * LANES).astype(jnp.int16)
    copies = []
    for first in range(0, offsets, STEP):
        count = min(STEP, offsets - first)
        slot = (first // STEP) % 2
        for k in range(count):
            hot_ref[slot, :, lane_block(k)] = one_hot_16(iota, table_ref[first + k : first + k + 1, :])
        rows = jnp.dot(
            ext_ref[...], hot_ref[slot, :, : count * LANES], preferred_element_type=F32
        ).astype(BF16)
        for k in range(count):
            gathered_ref[lane_block(first + k), :] = rows[:, lane_block(k)]
        part = pl.ds(first * LANES, count * LANES)
        copies.append(
            pltpu.make_async_copy(gathered_ref.at[part], gathered_any.at[part], sems.at[first // STEP])
        )
        copies[-1].start()
    for copy in copies:
        copy.wait()


def encode(value, top):
    level = jnp.ceil(jnp.log2(jnp.maximum(top, 1e-36)) * 8.0)
    code = jnp.round(value * jnp.exp2(level * -0.125) * 32767.0)
    return jnp.clip(code, -32767.0, 32767.0).astype(I32), level.astype(I32)


def unit(level):
    return jnp.exp2(level.astype(F32) * 0.125)


def join(first, second):
    return (first << 16) | (second & 0xFFFF)


def halves(word):
    scale = 1.0 / 32767.0
    return (word >> 16).astype(F32) * scale, ((word << 16) >> 16).astype(F32) * scale


def row_top(value):
    return jnp.max(jnp.abs(value), axis=1, keepdims=True)


def fetch(w_any, w_ref, gathered_any, gathered_ref, sems):
    offsets = w_ref.shape[0]
    parts = sems.shape[1]
    step = offsets // parts
    copies = []
    for i in range(parts):
        part = pl.ds(i * step, step)
        rows = pl.ds(i * step * LANES, step * LANES)
        copies.append(
            (
                pltpu.make_async_copy(w_any.at[part], w_ref.at[part], sems.at[0, i]),
                pltpu.make_async_copy(gathered_any.at[rows], gathered_ref.at[rows], sems.at[1, i]),
            )
        )
        for copy in copies[-1]:
            copy.start()
    return copies, step


def forward_kernel(
    near_ref,
    w_any,
    table_ref,
    gathered_any,
    own_any,
    word_ref,
    grad_ref,
    w_ref,
    gathered_ref,
    terms_ref,
    hot_ref,
    send_ref,
    sems,
    own_sem,
    *,
    free,
):
    offsets = w_ref.shape[0]
    copies, step = fetch(w_any, w_ref, gathered_any, gathered_ref, sems)
    total = jnp.zeros((w_ref.shape[1], LANES), F32)
    for k in range(offsets):
        if k % step == 0:
            for copy in copies[k // step]:
                copy.wait()
        high, low = split_two(jnp.dot(near_ref[0], w_ref[k], preferred_element_type=F32))
        terms_ref[lane_block(k), 0:LANES] = high
        terms_ref[lane_block(k), LANES : 2 * LANES] = low
        total += jnp.dot(w_ref[k], gathered_ref[lane_block(k), :], preferred_element_type=F32)
    grad_ref[...] = total.T.astype(BF16)
    iota = rows_iota(LANES).astype(jnp.int16)

    span = hot_ref.shape[1]
    own_rows = own_any.shape[0]
    own_copy = pltpu.make_async_copy(send_ref.at[pl.ds(0, own_rows)], own_any, own_sem)
    for i in range(send_ref.shape[0] // span):
        for j in range(span // LANES):
            for k in range(offsets):
                row = table_ref[k : k + 1, :] - (i * span + j * LANES)
                hot_ref[i % 2, lane_block(j), lane_block(k)] = one_hot_16(iota, row)
        both = jnp.dot(hot_ref[i % 2], terms_ref[...], preferred_element_type=F32)
        send_ref[pl.ds(i * span, span), :] = both[:, :LANES] + both[:, LANES:]
        if i == 0:
            own_copy.start()
    peers = word_ref.shape[1]
    lane = lax.broadcasted_iota(I32, (peers, LANES), 1)
    levels = jnp.zeros((peers, LANES), I32)
    for r in range(4):
        words = []
        for slot in (r, r + 4):
            value = send_ref[pl.ds(own_rows + slot, peers, stride=8), :]
            code, level = encode(value, row_top(value))
            words.append(code)
            levels = jnp.where(lane == free + slot, level, levels)
        word_ref[r] = join(*words)
    word_ref[4] = levels
    own_copy.wait()


def pack_kernel(g_ref, near_ref, far_ref, word_ref, out_ref, turn_ref):
    columns = g_ref.shape[1]
    peers = word_ref.shape[1]
    blocks = turn_ref.shape[0]
    scenes = near_ref.shape[0]
    core, scene = (lax.axis_index(axis) for axis in GROUP)
    total = jnp.zeros((columns, near_ref.shape[2]), F32)
    for s in range(0, g_ref.shape[0], 2):
        x_ref, holder = (near_ref, core) if s < scenes else (far_ref, 1 - core)
        senders = [holder * scenes + (scene ^ ((s + i) % scenes)) for i in range(2)]
        both = jnp.concatenate([g_ref[sender] for sender in senders], axis=1)
        first = s % scenes
        rows = x_ref[first : first + 2].reshape(both.shape[1], total.shape[1])
        total += jnp.dot(both, rows, preferred_element_type=F32)
    rest = blocks * LANES - columns
    total = jnp.concatenate([total, jnp.zeros((rest, total.shape[1]), F32)], axis=0)
    for h in range(blocks):
        turn_ref[h] = total[lane_block(h), :].T
    for r in range(4):
        out_ref[pl.ds(r, peers, stride=WORDS), :] = word_ref[r]
    parts = [[turn_ref[h, pl.ds(c, peers, stride=2), :] for c in range(2)] for h in range(blocks)]
    top = functools.reduce(jnp.maximum, [jnp.abs(part) for pair in parts for part in pair])
    top = jnp.max(top, axis=1, keepdims=True)
    free = LANES - rest
    lane = lax.broadcasted_iota(I32, (peers, LANES), 1)
    for h in range(blocks):
        codes = [encode(part, top) for part in parts[h]]
        word = join(codes[0][0], codes[1][0])
        if h == blocks - 1:
            levels = jnp.where(lane == free + 8, codes[0][1], word_ref[4])
            word = jnp.where(lane < free, word, levels)
        out_ref[pl.ds(4 + h, peers, stride=WORDS), :] = word


def sum_kernel(arrived_ref, out_ref, *, free):
    peers = arrived_ref.shape[0] // WORDS
    words = [arrived_ref[pl.ds(4 + h, peers, stride=WORDS), :] for h in range(4)]
    scale = unit(words[-1][:, free + 8 : free + 9])
    for h in range(4):
        for c, value in enumerate(halves(words[h])):
            total = (value * scale).reshape(peers // 8, 8, LANES).sum(axis=0)
            total = (total[0:2] + total[2:4]) + (total[4:6] + total[6:8])
            row = 2 * (4 * c + h)
            for s in range(out_ref.shape[0]):
                out_ref[s, row : row + 2, :] = total


def receive_kernel(own_ref, arrived_ref, recv_ref, out_ref, rows_ref, *, free):
    peers = arrived_ref.shape[0] // WORDS
    iota = rows_iota(LANES)
    levels = arrived_ref[pl.ds(WORDS - 1, peers, stride=WORDS), :]
    for r in range(4):
        pair = halves(arrived_ref[pl.ds(r, peers, stride=WORDS), :])
        for value, slot in zip(pair, (r, r + 4)):
            scale = unit(levels[:, free + slot : free + slot + 1])
            rows_ref[pl.ds(slot, peers, stride=8), :] = value * scale
    total = own_ref[...]
    for g in range(recv_ref.shape[0]):
        hot = one_hot(iota, recv_ref[g : g + 1, :])
        high, low = split_two(rows_ref[lane_block(g), :])
        total += jnp.dot(hot, high, preferred_element_type=F32)
        total += jnp.dot(hot, low, preferred_element_type=F32)
    out_ref[...] = total.astype(BF16)


def local(features, cotangent, relu_mask, weight, pair_in, pair_out, recv_index):
    x = features[0]
    own_rows, in_width = x.shape
    offsets, unused, out_width = weight.shape
    peers = lax.axis_size(SPACE)
    group = lax.axis_size(GROUP)
    scenes = lax.axis_size("scene")
    send_rows = recv_index.shape[2]
    slots = send_rows // peers
    targets = own_rows + send_rows
    columns = offsets * out_width // group
    recv = recv_index.reshape(send_rows // LANES, LANES)
    shape = jax.ShapeDtypeStruct

    hbm = pl.BlockSpec(memory_space=pltpu.HBM)
    vmem = pl.BlockSpec(memory_space=pltpu.VMEM)
    blocks = -(-columns // LANES)
    free = columns - (blocks - 1) * LANES

    lists = [pairs.reshape(offsets, 1, own_rows) for pairs in (pair_in, pair_out)]
    shared, outgoing = call(
        functools.partial(gather_kernel, targets=targets),
        (shape((out_width + 64, own_rows), BF16), shape((send_rows, out_width), BF16)),
        scratch=(
            pltpu.VMEM((own_rows, out_width), BF16),
            pltpu.VMEM((own_rows, out_width), I32),
            pltpu.VMEM(recv.shape, I32),
            pltpu.VMEM(lists[0].shape, I32),
            pltpu.VMEM(lists[1].shape, I32),
            pltpu.VMEM((64, own_rows), F32),
            pltpu.SemaphoreType.DMA((5,)),
        ),
        in_specs=[hbm] * 5,
        vmem=MOST_VMEM,
        flops=2 * send_rows * own_rows * out_width,
        moved=send_rows * out_width * 3,
    )(cotangent[0], relu_mask[0], recv, *lists)
    own_x, outgoing = lax.optimization_barrier((x, outgoing))
    returned = lax.all_to_all(outgoing.reshape(peers, slots, out_width), SPACE, 0, 0, tiled=True)

    swap = [(0, 1), (1, 0)]
    one, two = ([(i, i ^ d) for i in range(scenes)] for d in (1, 2))
    beside = lax.ppermute(own_x, "scene", one)
    table, turned = call(
        table_kernel, (shape((32, own_rows), I32), shape((out_width, own_rows), BF16))
    )(shared)
    beside, table, turned = lax.optimization_barrier((beside, table, turned))
    pair = jnp.stack([own_x, beside])
    other = lax.ppermute(pair, "scene", two)
    gathered = call(
        lookup_kernel,
        shape((offsets * out_width, own_rows), BF16),
        scratch=(
            pltpu.VMEM((out_width, targets), BF16),
            pltpu.VMEM((2, targets, STEP * LANES), BF16),
            pltpu.VMEM((offsets * out_width, own_rows), BF16),
            pltpu.SemaphoreType.DMA((-(-offsets // STEP),)),
        ),
        out_specs=hbm,
    )(turned, returned.reshape(send_rows, out_width), table)
    gathered, pair, other = lax.optimization_barrier((gathered, pair, other))
    group_g = lax.all_to_all(gathered.reshape(group, columns, own_rows), GROUP, 0, 0, tiled=True)

    near = jnp.concatenate([pair, other])
    own, words, input_grad = call(
        functools.partial(forward_kernel, free=free),
        (
            shape((own_rows, out_width), F32),
            shape((5, peers, out_width), I32),
            shape((own_rows, in_width), BF16),
        ),
        scratch=(
            pltpu.VMEM(weight.shape, BF16),
            pltpu.VMEM((offsets * out_width, own_rows), BF16),
            pltpu.VMEM((offsets * own_rows, 2 * out_width), BF16),
            pltpu.VMEM((2, targets // 3, offsets * own_rows), BF16),
            pltpu.VMEM((targets, out_width), F32),
            pltpu.SemaphoreType.DMA((2, 3)),
            pltpu.SemaphoreType.DMA,
        ),
        in_specs=[vmem, hbm, vmem, hbm],
        out_specs=(hbm, vmem, vmem),
    )(near, weight, table, gathered)

    far = lax.ppermute(near, "core", swap)
    packed = call(
        pack_kernel,
        shape((peers * WORDS, LANES), I32),
        scratch=(pltpu.VMEM((blocks, in_width, LANES), F32),),
        flops=2 * columns * in_width * own_rows * group,
        moved=peers * WORDS * LANES * 8,
    )(group_g, near, far, words)
    arrived = lax.all_to_all(packed.reshape(peers, WORDS, LANES), SPACE, 0, 0, tiled=True)
    arrived = arrived.reshape(peers * WORDS, LANES)

    quarter = call(
        functools.partial(sum_kernel, free=free),
        shape((scenes, 16, LANES), F32),
        moved=peers * WORDS * LANES * 4,
    )(arrived)
    sums = lax.all_to_all(quarter, "scene", 0, 0, tiled=True)
    conv_out = call(
        functools.partial(receive_kernel, free=free),
        shape((own_rows, out_width), BF16),
        scratch=(pltpu.VMEM((send_rows, out_width), F32),),
        flops=4 * send_rows * own_rows * out_width,
        moved=send_rows * out_width * 4,
    )(own, arrived, recv)

    own_in = in_width // peers
    sums = sums.reshape(scenes, own_in, blocks, 2, LANES).transpose(1, 3, 0, 2, 4)
    sums = sums.reshape(own_in, group, blocks * LANES)[:, :, :columns]
    kernel_grad = sums.reshape(own_in, offsets, out_width)
    kernel_grad = kernel_grad.transpose(1, 0, 2).reshape(offsets, own_in * out_width)
    normalizer = 1.0 / math.sqrt(scenes * peers * own_rows)
    return (conv_out[None], input_grad[None], kernel_grad * normalizer)


def solution(mesh):
    scenes = mesh.devices.shape[1]
    fine = Mesh(mesh.devices.reshape(8, 8, 2, scenes), ("y", "z", "core", "scene"))
    voxels = P("scene", SPACE)
    return jax.shard_map(
        local,
        mesh=fine,
        in_specs=(voxels, voxels, voxels, P(), voxels, voxels, voxels),
        out_specs=(voxels, voxels, P(None, SPACE)),
        check_vma=False,
    )
```

```python
import functools
import math

import jax
import jax.numpy as jnp
from jax import lax
from jax.experimental import pallas as pl
from jax.experimental.pallas import tpu as pltpu
from jax.sharding import Mesh
from jax.sharding import PartitionSpec as P

F32 = jnp.float32
BF16 = jnp.bfloat16
I32 = jnp.int32
LANES = 128
STEP = 4
WORDS = 8
VMEM_BYTES = 24 * 1024 * 1024
MOST_VMEM = 64 * 1024 * 1024 - 128 * 1024
SPACE = ("y", "z", "core")
GROUP = ("core", "scene")


def call(kernel, outs, scratch=(), flops=0, moved=0, vmem=VMEM_BYTES, **specs):
    return pl.pallas_call(
        kernel,
        out_shape=outs,
        scratch_shapes=list(scratch),
        **specs,
        compiler_params=pltpu.CompilerParams(vmem_limit_bytes=vmem),
        cost_estimate=pl.CostEstimate(flops=flops, bytes_accessed=moved, transcendentals=0),
    )


def rows_iota(rows, start=0):
    return lax.broadcasted_iota(I32, (rows, LANES), 0) + start


def one_hot(iota, row):
    return jnp.where(iota == row, 1.0, 0.0).astype(BF16)


def one_hot_16(iota, row):
    rows = iota.shape[0]
    narrow = jnp.broadcast_to(row, (16, LANES)).astype(jnp.int16)
    narrow = jnp.concatenate([narrow] * (rows // 16), axis=0)
    return jnp.where(iota == narrow, jnp.ones((rows, LANES), BF16), jnp.zeros((rows, LANES), BF16))


def split_two(value):
    high = value.astype(BF16)
    low = (value - high.astype(F32)).astype(BF16)
    return high, low


def lane_block(k):
    return slice(k * LANES, (k + 1) * LANES)


def gather_kernel(
    cot_any, mask_any, recv_any, in_any, pair_any, shared_ref, out_ref, cot_ref, mask_ref, recv_ref, in_ref, pair_ref, digit_ref, sems, *, targets
):
    pairs = (
        (cot_any, cot_ref),
        (mask_any, mask_ref),
        (recv_any, recv_ref),
        (in_any, in_ref),
        (pair_any, pair_ref),
    )
    copies = [pltpu.make_async_copy(a, b, sems.at[i]) for i, (a, b) in enumerate(pairs)]
    for copy in copies:
        copy.start()
    digit_ref[...] = jnp.zeros_like(digit_ref)
    for copy in copies:
        copy.wait()
    up = (cot_ref[...].astype(F32) * mask_ref[...].astype(F32)).astype(BF16)
    shared_ref[0:LANES, :] = up.T
    iota = rows_iota(LANES)
    for g in range(recv_ref.shape[0]):
        hot = one_hot(iota, recv_ref[g : g + 1, :])
        rows = lax.dot_general(hot, up, (((0,), (0,)), ((), ())), preferred_element_type=F32)
        out_ref[lane_block(g), :] = rows.astype(BF16)
    picks = rows_iota(16)
    for k in range(in_ref.shape[0]):
        hot = one_hot(iota, in_ref[k])
        target = pair_ref[k]
        code = jnp.where(target < targets, target + 1, 0)
        digits = jnp.where(picks == 0, code >> 7, jnp.where(picks == 1, code & 127, 0))
        found = lax.dot_general(
            digits.astype(F32).astype(BF16), hot, (((1,), (1,)), ((), ())), preferred_element_type=F32
        )
        digit_ref[k : k + 1, :] = found[0:1]
        digit_ref[32 + k : 33 + k, :] = found[1:2]
    shared_ref[LANES : LANES + 64, :] = digit_ref[...].astype(BF16)


def table_kernel(shared_ref, table_ref, turned_ref):
    high = shared_ref[LANES : LANES + 32, :].astype(F32)
    low = shared_ref[LANES + 32 : LANES + 64, :].astype(F32)
    table_ref[...] = (high * 128.0 + low - 1.0).astype(I32)
    turned_ref[...] = shared_ref[0:LANES, :]


def lookup_kernel(turned_ref, back_ref, table_ref, gathered_any, ext_ref, hot_ref, gathered_ref, sems):
    blocks = back_ref.shape[0] // LANES
    offsets = gathered_ref.shape[0] // LANES
    ext_ref[:, 0:LANES] = turned_ref[...]
    for b in range(blocks):
        ext_ref[:, lane_block(b + 1)] = back_ref[lane_block(b), :].T
    iota = rows_iota((blocks + 1) * LANES).astype(jnp.int16)
    copies = []
    for first in range(0, offsets, STEP):
        count = min(STEP, offsets - first)
        slot = (first // STEP) % 2
        for k in range(count):
            hot_ref[slot, :, lane_block(k)] = one_hot_16(iota, table_ref[first + k : first + k + 1, :])
        rows = jnp.dot(
            ext_ref[...], hot_ref[slot, :, : count * LANES], preferred_element_type=F32
        ).astype(BF16)
        for k in range(count):
            gathered_ref[lane_block(first + k), :] = rows[:, lane_block(k)]
        part = pl.ds(first * LANES, count * LANES)
        copies.append(
            pltpu.make_async_copy(gathered_ref.at[part], gathered_any.at[part], sems.at[first // STEP])
        )
        copies[-1].start()
    for copy in copies:
        copy.wait()


def encode(value, top):
    level = jnp.ceil(jnp.log2(jnp.maximum(top, 1e-36)) * 8.0)
    code = jnp.round(value * jnp.exp2(level * -0.125) * 32767.0)
    return jnp.clip(code, -32767.0, 32767.0).astype(I32), level.astype(I32)


def unit(level):
    return jnp.exp2(level.astype(F32) * 0.125)


def join(first, second):
    return (first << 16) | (second & 0xFFFF)


def halves(word):
    scale = 1.0 / 32767.0
    return (word >> 16).astype(F32) * scale, ((word << 16) >> 16).astype(F32) * scale


def row_top(value):
    return jnp.max(jnp.abs(value), axis=1, keepdims=True)


def fetch(w_any, w_ref, gathered_any, gathered_ref, sems):
    offsets = w_ref.shape[0]
    parts = sems.shape[1]
    step = offsets // parts
    copies = []
    for i in range(parts):
        part = pl.ds(i * step, step)
        rows = pl.ds(i * step * LANES, step * LANES)
        copies.append(
            (
                pltpu.make_async_copy(w_any.at[part], w_ref.at[part], sems.at[0, i]),
                pltpu.make_async_copy(gathered_any.at[rows], gathered_ref.at[rows], sems.at[1, i]),
            )
        )
        for copy in copies[-1]:
            copy.start()
    return copies, step


def forward_kernel(
    near_ref,
    w_any,
    table_ref,
    gathered_any,
    own_any,
    word_ref,
    grad_ref,
    w_ref,
    gathered_ref,
    terms_ref,
    hot_ref,
    send_ref,
    sems,
    own_sem,
    *,
    free,
):
    offsets = w_ref.shape[0]
    copies, step = fetch(w_any, w_ref, gathered_any, gathered_ref, sems)
    total = jnp.zeros((w_ref.shape[1], LANES), F32)
    for k in range(offsets):
        if k % step == 0:
            for copy in copies[k // step]:
                copy.wait()
        high, low = split_two(jnp.dot(near_ref[0], w_ref[k], preferred_element_type=F32))
        terms_ref[lane_block(k), 0:LANES] = high
        terms_ref[lane_block(k), LANES : 2 * LANES] = low
        total += jnp.dot(w_ref[k], gathered_ref[lane_block(k), :], preferred_element_type=F32)
    grad_ref[...] = total.T.astype(BF16)
    iota = rows_iota(LANES).astype(jnp.int16)

    span = hot_ref.shape[1]
    own_rows = own_any.shape[0]
    own_copy = pltpu.make_async_copy(send_ref.at[pl.ds(0, own_rows)], own_any, own_sem)
    for i in range(send_ref.shape[0] // span):
        for j in range(span // LANES):
            for k in range(offsets):
                row = table_ref[k : k + 1, :] - (i * span + j * LANES)
                hot_ref[i % 2, lane_block(j), lane_block(k)] = one_hot_16(iota, row)
        both = jnp.dot(hot_ref[i % 2], terms_ref[...], preferred_element_type=F32)
        send_ref[pl.ds(i * span, span), :] = both[:, :LANES] + both[:, LANES:]
        if i == 0:
            own_copy.start()
    peers = word_ref.shape[1]
    lane = lax.broadcasted_iota(I32, (peers, LANES), 1)
    levels = jnp.zeros((peers, LANES), I32)
    for r in range(4):
        words = []
        for slot in (r, r + 4):
            value = send_ref[pl.ds(own_rows + slot, peers, stride=8), :]
            code, level = encode(value, row_top(value))
            words.append(code)
            levels = jnp.where(lane == free + slot, level, levels)
        word_ref[r] = join(*words)
    word_ref[4] = levels
    own_copy.wait()


def pack_kernel(g_ref, near_ref, far_ref, word_ref, out_ref, turn_ref):
    columns = g_ref.shape[1]
    peers = word_ref.shape[1]
    blocks = turn_ref.shape[0]
    scenes = near_ref.shape[0]
    core, scene = (lax.axis_index(axis) for axis in GROUP)
    total = jnp.zeros((columns, near_ref.shape[2]), F32)
    for s in range(0, g_ref.shape[0], 2):
        x_ref, holder = (near_ref, core) if s < scenes else (far_ref, 1 - core)
        senders = [holder * scenes + (scene ^ ((s + i) % scenes)) for i in range(2)]
        both = jnp.concatenate([g_ref[sender] for sender in senders], axis=1)
        first = s % scenes
        rows = x_ref[first : first + 2].reshape(both.shape[1], total.shape[1])
        total += jnp.dot(both, rows, preferred_element_type=F32)
    rest = blocks * LANES - columns
    total = jnp.concatenate([total, jnp.zeros((rest, total.shape[1]), F32)], axis=0)
    for h in range(blocks):
        turn_ref[h] = total[lane_block(h), :].T
    for r in range(4):
        out_ref[pl.ds(r, peers, stride=WORDS), :] = word_ref[r]
    parts = [[turn_ref[h, pl.ds(c, peers, stride=2), :] for c in range(2)] for h in range(blocks)]
    top = functools.reduce(jnp.maximum, [jnp.abs(part) for pair in parts for part in pair])
    top = jnp.max(top, axis=1, keepdims=True)
    free = LANES - rest
    lane = lax.broadcasted_iota(I32, (peers, LANES), 1)
    for h in range(blocks):
        codes = [encode(part, top) for part in parts[h]]
        word = join(codes[0][0], codes[1][0])
        if h == blocks - 1:
            levels = jnp.where(lane == free + 8, codes[0][1], word_ref[4])
            word = jnp.where(lane < free, word, levels)
        out_ref[pl.ds(4 + h, peers, stride=WORDS), :] = word


def sum_kernel(arrived_ref, out_ref, *, free):
    peers = arrived_ref.shape[0] // WORDS
    words = [arrived_ref[pl.ds(4 + h, peers, stride=WORDS), :] for h in range(4)]
    scale = unit(words[-1][:, free + 8 : free + 9])
    for h in range(4):
        for c, value in enumerate(halves(words[h])):
            total = (value * scale).reshape(peers // 8, 8, LANES).sum(axis=0)
            total = (total[0:2] + total[2:4]) + (total[4:6] + total[6:8])
            for core in range(2):
                row = 4 * (2 * c + core) + h
                for s in range(out_ref.shape[0]):
                    out_ref[s, row : row + 1, :] = total[core : core + 1]


def receive_kernel(own_ref, arrived_ref, recv_ref, out_ref, rows_ref, *, free):
    peers = arrived_ref.shape[0] // WORDS
    iota = rows_iota(LANES)
    levels = arrived_ref[pl.ds(WORDS - 1, peers, stride=WORDS), :]
    for r in range(4):
        pair = halves(arrived_ref[pl.ds(r, peers, stride=WORDS), :])
        for value, slot in zip(pair, (r, r + 4)):
            scale = unit(levels[:, free + slot : free + slot + 1])
            rows_ref[pl.ds(slot, peers, stride=8), :] = value * scale
    total = own_ref[...]
    for g in range(recv_ref.shape[0]):
        hot = one_hot(iota, recv_ref[g : g + 1, :])
        high, low = split_two(rows_ref[lane_block(g), :])
        total += jnp.dot(hot, high, preferred_element_type=F32)
        total += jnp.dot(hot, low, preferred_element_type=F32)
    out_ref[...] = total.astype(BF16)


def local(features, cotangent, relu_mask, weight, pair_in, pair_out, recv_index):
    x = features[0]
    own_rows, in_width = x.shape
    offsets, unused, out_width = weight.shape
    peers = lax.axis_size(SPACE)
    group = lax.axis_size(GROUP)
    scenes = lax.axis_size("scene")
    send_rows = recv_index.shape[2]
    slots = send_rows // peers
    targets = own_rows + send_rows
    columns = offsets * out_width // group
    recv = recv_index.reshape(send_rows // LANES, LANES)
    shape = jax.ShapeDtypeStruct

    hbm = pl.BlockSpec(memory_space=pltpu.HBM)
    vmem = pl.BlockSpec(memory_space=pltpu.VMEM)
    blocks = -(-columns // LANES)
    free = columns - (blocks - 1) * LANES

    lists = [pairs.reshape(offsets, 1, own_rows) for pairs in (pair_in, pair_out)]
    shared, outgoing = call(
        functools.partial(gather_kernel, targets=targets),
        (shape((out_width + 64, own_rows), BF16), shape((send_rows, out_width), BF16)),
        scratch=(
            pltpu.VMEM((own_rows, out_width), BF16),
            pltpu.VMEM((own_rows, out_width), I32),
            pltpu.VMEM(recv.shape, I32),
            pltpu.VMEM(lists[0].shape, I32),
            pltpu.VMEM(lists[1].shape, I32),
            pltpu.VMEM((64, own_rows), F32),
            pltpu.SemaphoreType.DMA((5,)),
        ),
        in_specs=[hbm] * 5,
        vmem=MOST_VMEM,
        flops=2 * send_rows * own_rows * out_width,
        moved=send_rows * out_width * 3,
    )(cotangent[0], relu_mask[0], recv, *lists)
    own_x, outgoing = lax.optimization_barrier((x, outgoing))
    returned = lax.all_to_all(outgoing.reshape(peers, slots, out_width), SPACE, 0, 0, tiled=True)

    swap = [(0, 1), (1, 0)]
    ring = [
        lax.ppermute(own_x, "scene", [(i, i ^ d) for i in range(scenes)]) for d in range(1, scenes)
    ]

    table, turned = call(
        table_kernel, (shape((32, own_rows), I32), shape((out_width, own_rows), BF16))
    )(shared)
    gathered = call(
        lookup_kernel,
        shape((offsets * out_width, own_rows), BF16),
        scratch=(
            pltpu.VMEM((out_width, targets), BF16),
            pltpu.VMEM((2, targets, STEP * LANES), BF16),
            pltpu.VMEM((offsets * out_width, own_rows), BF16),
            pltpu.SemaphoreType.DMA((-(-offsets // STEP),)),
        ),
        out_specs=hbm,
    )(turned, returned.reshape(send_rows, out_width), table)
    gathered, *ring = lax.optimization_barrier((gathered, *ring))
    group_g = lax.all_to_all(gathered.reshape(group, columns, own_rows), GROUP, 0, 0, tiled=True)

    near = jnp.stack([x] + ring)
    own, words, input_grad = call(
        functools.partial(forward_kernel, free=free),
        (
            shape((own_rows, out_width), F32),
            shape((5, peers, out_width), I32),
            shape((own_rows, in_width), BF16),
        ),
        scratch=(
            pltpu.VMEM(weight.shape, BF16),
            pltpu.VMEM((offsets * out_width, own_rows), BF16),
            pltpu.VMEM((offsets * own_rows, 2 * out_width), BF16),
            pltpu.VMEM((2, targets // 3, offsets * own_rows), BF16),
            pltpu.VMEM((targets, out_width), F32),
            pltpu.SemaphoreType.DMA((2, 3)),
            pltpu.SemaphoreType.DMA,
        ),
        in_specs=[vmem, hbm, vmem, hbm],
        out_specs=(hbm, vmem, vmem),
    )(near, weight, table, gathered)

    far = lax.ppermute(near, "core", swap)
    packed = call(
        pack_kernel,
        shape((peers * WORDS, LANES), I32),
        scratch=(pltpu.VMEM((blocks, in_width, LANES), F32),),
        flops=2 * columns * in_width * own_rows * group,
        moved=peers * WORDS * LANES * 8,
    )(group_g, near, far, words)
    arrived = lax.all_to_all(packed.reshape(peers, WORDS, LANES), SPACE, 0, 0, tiled=True)
    arrived = arrived.reshape(peers * WORDS, LANES)

    quarter = call(
        functools.partial(sum_kernel, free=free),
        shape((scenes, 16, LANES), F32),
        moved=peers * WORDS * LANES * 4,
    )(arrived)
    sums = lax.all_to_all(quarter, "scene", 0, 0, tiled=True)
    conv_out = call(
        functools.partial(receive_kernel, free=free),
        shape((own_rows, out_width), BF16),
        scratch=(pltpu.VMEM((send_rows, out_width), F32),),
        flops=4 * send_rows * own_rows * out_width,
        moved=send_rows * out_width * 4,
    )(own, arrived, recv)

    own_in = in_width // peers
    sums = sums.reshape(scenes, own_in, 2, blocks, LANES).transpose(1, 2, 0, 3, 4)
    sums = sums.reshape(own_in, group, blocks * LANES)[:, :, :columns]
    kernel_grad = sums.reshape(own_in, offsets, out_width)
    kernel_grad = jnp.concatenate([kernel_grad[c] for c in range(own_in)], axis=1)
    normalizer = 1.0 / math.sqrt(scenes * peers * own_rows)
    return (conv_out[None], input_grad[None], kernel_grad * normalizer)


def solution(mesh):
    scenes = mesh.devices.shape[1]
    fine = Mesh(mesh.devices.reshape(8, 8, 2, scenes), ("y", "z", "core", "scene"))
    voxels = P("scene", SPACE)
    return jax.shard_map(
        local,
        mesh=fine,
        in_specs=(voxels, voxels, voxels, P(), voxels, voxels, voxels),
        out_specs=(voxels, voxels, P(None, SPACE)),
        check_vma=False,
    )
```

```python
import functools
import math

import jax
import jax.numpy as jnp
from jax import lax
from jax.experimental import pallas as pl
from jax.experimental.pallas import tpu as pltpu
from jax.sharding import Mesh
from jax.sharding import PartitionSpec as P

F32 = jnp.float32
BF16 = jnp.bfloat16
I32 = jnp.int32
LANES = 128
STEP = 2
WORDS = 8
VMEM_BYTES = 24 * 1024 * 1024
MOST_VMEM = 64 * 1024 * 1024 - 128 * 1024
SPACE = ("y", "z", "core")
GROUP = ("core", "scene")


def call(kernel, outs, scratch=(), flops=0, moved=0, vmem=VMEM_BYTES, **specs):
    return pl.pallas_call(
        kernel,
        out_shape=outs,
        scratch_shapes=list(scratch),
        **specs,
        compiler_params=pltpu.CompilerParams(vmem_limit_bytes=vmem),
        cost_estimate=pl.CostEstimate(flops=flops, bytes_accessed=moved, transcendentals=0),
    )


def rows_iota(rows, start=0):
    return lax.broadcasted_iota(I32, (rows, LANES), 0) + start


def one_hot(iota, row):
    return jnp.where(iota == row, 1.0, 0.0).astype(BF16)


def one_hot_16(iota, row):
    rows = iota.shape[0]
    narrow = jnp.broadcast_to(row, (16, LANES)).astype(jnp.int16)
    narrow = jnp.concatenate([narrow] * (rows // 16), axis=0)
    return jnp.where(iota == narrow, jnp.ones((rows, LANES), BF16), jnp.zeros((rows, LANES), BF16))


def split_two(value):
    high = value.astype(BF16)
    low = (value - high.astype(F32)).astype(BF16)
    return high, low


def lane_block(k):
    return slice(k * LANES, (k + 1) * LANES)


def gather_kernel(
    cot_any, mask_any, recv_any, in_any, pair_any, shared_ref, out_ref, cot_ref, mask_ref, recv_ref, in_ref, pair_ref, digit_ref, sems, *, targets
):
    pairs = (
        (cot_any, cot_ref),
        (mask_any, mask_ref),
        (recv_any, recv_ref),
        (in_any, in_ref),
        (pair_any, pair_ref),
    )
    copies = [pltpu.make_async_copy(a, b, sems.at[i]) for i, (a, b) in enumerate(pairs)]
    for copy in copies:
        copy.start()
    digit_ref[...] = jnp.zeros_like(digit_ref)
    for copy in copies:
        copy.wait()
    up = (cot_ref[...].astype(F32) * mask_ref[...].astype(F32)).astype(BF16)
    shared_ref[0:LANES, :] = up.T
    iota = rows_iota(LANES)
    for g in range(recv_ref.shape[0]):
        hot = one_hot(iota, recv_ref[g : g + 1, :])
        rows = lax.dot_general(hot, up, (((0,), (0,)), ((), ())), preferred_element_type=F32)
        out_ref[lane_block(g), :] = rows.astype(BF16)
    picks = rows_iota(16)
    for k in range(in_ref.shape[0]):
        hot = one_hot(iota, in_ref[k])
        target = pair_ref[k]
        code = jnp.where(target < targets, target + 1, 0)
        digits = jnp.where(picks == 0, code >> 7, jnp.where(picks == 1, code & 127, 0))
        found = lax.dot_general(
            digits.astype(F32).astype(BF16), hot, (((1,), (1,)), ((), ())), preferred_element_type=F32
        )
        digit_ref[k : k + 1, :] = found[0:1]
        digit_ref[32 + k : 33 + k, :] = found[1:2]
    shared_ref[LANES : LANES + 64, :] = digit_ref[...].astype(BF16)


def table_kernel(shared_ref, table_ref, turned_ref):
    high = shared_ref[LANES : LANES + 32, :].astype(F32)
    low = shared_ref[LANES + 32 : LANES + 64, :].astype(F32)
    table_ref[...] = (high * 128.0 + low - 1.0).astype(I32)
    turned_ref[...] = shared_ref[0:LANES, :]


def lookup_kernel(turned_ref, back_ref, table_ref, gathered_any, ext_ref, hot_ref, gathered_ref, sems):
    blocks = back_ref.shape[0] // LANES
    offsets = gathered_ref.shape[0] // LANES
    ext_ref[:, 0:LANES] = turned_ref[...]
    for b in range(blocks):
        ext_ref[:, lane_block(b + 1)] = back_ref[lane_block(b), :].T
    iota = rows_iota((blocks + 1) * LANES).astype(jnp.int16)
    copies = []
    for first in range(0, offsets, STEP):
        count = min(STEP, offsets - first)
        slot = (first // STEP) % 2
        for k in range(count):
            hot_ref[slot, :, lane_block(k)] = one_hot_16(iota, table_ref[first + k : first + k + 1, :])
        rows = jnp.dot(
            ext_ref[...], hot_ref[slot, :, : count * LANES], preferred_element_type=F32
        ).astype(BF16)
        for k in range(count):
            gathered_ref[lane_block(first + k), :] = rows[:, lane_block(k)]
        part = pl.ds(first * LANES, count * LANES)
        copies.append(
            pltpu.make_async_copy(gathered_ref.at[part], gathered_any.at[part], sems.at[first // STEP])
        )
        copies[-1].start()
    for copy in copies:
        copy.wait()


def encode(value, top):
    level = jnp.ceil(jnp.log2(jnp.maximum(top, 1e-36)) * 8.0)
    code = jnp.round(value * jnp.exp2(level * -0.125) * 32767.0)
    return jnp.clip(code, -32767.0, 32767.0).astype(I32), level.astype(I32)


def unit(level):
    return jnp.exp2(level.astype(F32) * 0.125)


def join(first, second):
    return (first << 16) | (second & 0xFFFF)


def halves(word):
    scale = 1.0 / 32767.0
    return (word >> 16).astype(F32) * scale, ((word << 16) >> 16).astype(F32) * scale


def row_top(value):
    return jnp.max(jnp.abs(value), axis=1, keepdims=True)


def fetch(w_any, w_ref, gathered_any, gathered_ref, sems):
    offsets = w_ref.shape[0]
    parts = sems.shape[1]
    step = offsets // parts
    copies = []
    for i in range(parts):
        part = pl.ds(i * step, step)
        rows = pl.ds(i * step * LANES, step * LANES)
        copies.append(
            (
                pltpu.make_async_copy(w_any.at[part], w_ref.at[part], sems.at[0, i]),
                pltpu.make_async_copy(gathered_any.at[rows], gathered_ref.at[rows], sems.at[1, i]),
            )
        )
        for copy in copies[-1]:
            copy.start()
    return copies, step


def forward_kernel(
    near_ref,
    w_any,
    table_ref,
    gathered_any,
    own_any,
    word_ref,
    grad_ref,
    w_ref,
    gathered_ref,
    terms_ref,
    hot_ref,
    send_ref,
    sems,
    own_sem,
    *,
    free,
):
    offsets = w_ref.shape[0]
    copies, step = fetch(w_any, w_ref, gathered_any, gathered_ref, sems)
    total = jnp.zeros((w_ref.shape[1], LANES), F32)
    for k in range(offsets):
        if k % step == 0:
            for copy in copies[k // step]:
                copy.wait()
        high, low = split_two(jnp.dot(near_ref[0], w_ref[k], preferred_element_type=F32))
        terms_ref[lane_block(k), 0:LANES] = high
        terms_ref[lane_block(k), LANES : 2 * LANES] = low
        total += jnp.dot(w_ref[k], gathered_ref[lane_block(k), :], preferred_element_type=F32)
    grad_ref[...] = total.T.astype(BF16)
    iota = rows_iota(LANES).astype(jnp.int16)

    span = hot_ref.shape[1]
    own_rows = own_any.shape[0]
    own_copy = pltpu.make_async_copy(send_ref.at[pl.ds(0, own_rows)], own_any, own_sem)
    for i in range(send_ref.shape[0] // span):
        for j in range(span // LANES):
            for k in range(offsets):
                row = table_ref[k : k + 1, :] - (i * span + j * LANES)
                hot_ref[i % 2, lane_block(j), lane_block(k)] = one_hot_16(iota, row)
        both = jnp.dot(hot_ref[i % 2], terms_ref[...], preferred_element_type=F32)
        send_ref[pl.ds(i * span, span), :] = both[:, :LANES] + both[:, LANES:]
        if i == 0:
            own_copy.start()
    peers = word_ref.shape[1]
    lane = lax.broadcasted_iota(I32, (peers, LANES), 1)
    levels = jnp.zeros((peers, LANES), I32)
    for r in range(4):
        words = []
        for slot in (r, r + 4):
            value = send_ref[pl.ds(own_rows + slot, peers, stride=8), :]
            code, level = encode(value, row_top(value))
            words.append(code)
            levels = jnp.where(lane == free + slot, level, levels)
        word_ref[r] = join(*words)
    word_ref[4] = levels
    own_copy.wait()


def pack_kernel(g_ref, near_ref, far_ref, word_ref, out_ref, turn_ref):
    columns = g_ref.shape[1]
    peers = word_ref.shape[1]
    blocks = turn_ref.shape[0]
    scenes = near_ref.shape[0]
    core, scene = (lax.axis_index(axis) for axis in GROUP)
    total = jnp.zeros((columns, near_ref.shape[2]), F32)
    for s in range(0, g_ref.shape[0], 2):
        x_ref, holder = (near_ref, core) if s < scenes else (far_ref, 1 - core)
        senders = [holder * scenes + (scene ^ ((s + i) % scenes)) for i in range(2)]
        both = jnp.concatenate([g_ref[sender] for sender in senders], axis=1)
        first = s % scenes
        rows = x_ref[first : first + 2].reshape(both.shape[1], total.shape[1])
        total += jnp.dot(both, rows, preferred_element_type=F32)
    rest = blocks * LANES - columns
    total = jnp.concatenate([total, jnp.zeros((rest, total.shape[1]), F32)], axis=0)
    for h in range(blocks):
        turn_ref[h] = total[lane_block(h), :].T
    for r in range(4):
        out_ref[pl.ds(r, peers, stride=WORDS), :] = word_ref[r]
    parts = [[turn_ref[h, pl.ds(c, peers, stride=2), :] for c in range(2)] for h in range(blocks)]
    top = functools.reduce(jnp.maximum, [jnp.abs(part) for pair in parts for part in pair])
    top = jnp.max(top, axis=1, keepdims=True)
    free = LANES - rest
    lane = lax.broadcasted_iota(I32, (peers, LANES), 1)
    for h in range(blocks):
        codes = [encode(part, top) for part in parts[h]]
        word = join(codes[0][0], codes[1][0])
        if h == blocks - 1:
            levels = jnp.where(lane == free + 8, codes[0][1], word_ref[4])
            word = jnp.where(lane < free, word, levels)
        out_ref[pl.ds(4 + h, peers, stride=WORDS), :] = word


def sum_kernel(arrived_ref, out_ref, *, free):
    peers = arrived_ref.shape[0] // WORDS
    words = [arrived_ref[pl.ds(4 + h, peers, stride=WORDS), :] for h in range(4)]
    scale = unit(words[-1][:, free + 8 : free + 9])
    for h in range(4):
        for c, value in enumerate(halves(words[h])):
            total = (value * scale).reshape(peers // 8, 8, LANES).sum(axis=0)
            total = (total[0:2] + total[2:4]) + (total[4:6] + total[6:8])
            row = 2 * (4 * c + h)
            for s in range(out_ref.shape[0]):
                out_ref[s, row : row + 2, :] = total


def receive_kernel(own_ref, arrived_ref, recv_ref, out_ref, rows_ref, *, free):
    peers = arrived_ref.shape[0] // WORDS
    iota = rows_iota(LANES)
    levels = arrived_ref[pl.ds(WORDS - 1, peers, stride=WORDS), :]
    for r in range(4):
        pair = halves(arrived_ref[pl.ds(r, peers, stride=WORDS), :])
        for value, slot in zip(pair, (r, r + 4)):
            scale = unit(levels[:, free + slot : free + slot + 1])
            rows_ref[pl.ds(slot, peers, stride=8), :] = value * scale
    total = own_ref[...]
    for g in range(recv_ref.shape[0]):
        hot = one_hot(iota, recv_ref[g : g + 1, :])
        high, low = split_two(rows_ref[lane_block(g), :])
        total += jnp.dot(hot, high, preferred_element_type=F32)
        total += jnp.dot(hot, low, preferred_element_type=F32)
    out_ref[...] = total.astype(BF16)


def local(features, cotangent, relu_mask, weight, pair_in, pair_out, recv_index):
    x = features[0]
    own_rows, in_width = x.shape
    offsets, unused, out_width = weight.shape
    peers = lax.axis_size(SPACE)
    group = lax.axis_size(GROUP)
    scenes = lax.axis_size("scene")
    send_rows = recv_index.shape[2]
    slots = send_rows // peers
    targets = own_rows + send_rows
    columns = offsets * out_width // group
    recv = recv_index.reshape(send_rows // LANES, LANES)
    shape = jax.ShapeDtypeStruct

    hbm = pl.BlockSpec(memory_space=pltpu.HBM)
    vmem = pl.BlockSpec(memory_space=pltpu.VMEM)
    blocks = -(-columns // LANES)
    free = columns - (blocks - 1) * LANES

    lists = [pairs.reshape(offsets, 1, own_rows) for pairs in (pair_in, pair_out)]
    shared, outgoing = call(
        functools.partial(gather_kernel, targets=targets),
        (shape((out_width + 64, own_rows), BF16), shape((send_rows, out_width), BF16)),
        scratch=(
            pltpu.VMEM((own_rows, out_width), BF16),
            pltpu.VMEM((own_rows, out_width), I32),
            pltpu.VMEM(recv.shape, I32),
            pltpu.VMEM(lists[0].shape, I32),
            pltpu.VMEM(lists[1].shape, I32),
            pltpu.VMEM((64, own_rows), F32),
            pltpu.SemaphoreType.DMA((5,)),
        ),
        in_specs=[hbm] * 5,
        vmem=MOST_VMEM,
        flops=2 * send_rows * own_rows * out_width,
        moved=send_rows * out_width * 3,
    )(cotangent[0], relu_mask[0], recv, *lists)
    own_x, outgoing = lax.optimization_barrier((x, outgoing))
    returned = lax.all_to_all(outgoing.reshape(peers, slots, out_width), SPACE, 0, 0, tiled=True)

    swap = [(0, 1), (1, 0)]
    ring = [
        lax.ppermute(own_x, "scene", [(i, i ^ d) for i in range(scenes)]) for d in range(1, scenes)
    ]

    table, turned = call(
        table_kernel, (shape((32, own_rows), I32), shape((out_width, own_rows), BF16))
    )(shared)
    gathered = call(
        lookup_kernel,
        shape((offsets * out_width, own_rows), BF16),
        scratch=(
            pltpu.VMEM((out_width, targets), BF16),
            pltpu.VMEM((2, targets, STEP * LANES), BF16),
            pltpu.VMEM((offsets * out_width, own_rows), BF16),
            pltpu.SemaphoreType.DMA((-(-offsets // STEP),)),
        ),
        out_specs=hbm,
    )(turned, returned.reshape(send_rows, out_width), table)
    gathered, *ring = lax.optimization_barrier((gathered, *ring))
    group_g = lax.all_to_all(gathered.reshape(group, columns, own_rows), GROUP, 0, 0, tiled=True)

    near = jnp.stack([x] + ring)
    own, words, input_grad = call(
        functools.partial(forward_kernel, free=free),
        (
            shape((own_rows, out_width), F32),
            shape((5, peers, out_width), I32),
            shape((own_rows, in_width), BF16),
        ),
        scratch=(
            pltpu.VMEM(weight.shape, BF16),
            pltpu.VMEM((offsets * out_width, own_rows), BF16),
            pltpu.VMEM((offsets * own_rows, 2 * out_width), BF16),
            pltpu.VMEM((2, targets // 3, offsets * own_rows), BF16),
            pltpu.VMEM((targets, out_width), F32),
            pltpu.SemaphoreType.DMA((2, 3)),
            pltpu.SemaphoreType.DMA,
        ),
        in_specs=[vmem, hbm, vmem, hbm],
        out_specs=(hbm, vmem, vmem),
    )(near, weight, table, gathered)

    far = lax.ppermute(near, "core", swap)
    packed = call(
        pack_kernel,
        shape((peers * WORDS, LANES), I32),
        scratch=(pltpu.VMEM((blocks, in_width, LANES), F32),),
        flops=2 * columns * in_width * own_rows * group,
        moved=peers * WORDS * LANES * 8,
    )(group_g, near, far, words)
    arrived = lax.all_to_all(packed.reshape(peers, WORDS, LANES), SPACE, 0, 0, tiled=True)
    arrived = arrived.reshape(peers * WORDS, LANES)

    quarter = call(
        functools.partial(sum_kernel, free=free),
        shape((scenes, 16, LANES), F32),
        moved=peers * WORDS * LANES * 4,
    )(arrived)
    sums = lax.all_to_all(quarter, "scene", 0, 0, tiled=True)
    conv_out = call(
        functools.partial(receive_kernel, free=free),
        shape((own_rows, out_width), BF16),
        scratch=(pltpu.VMEM((send_rows, out_width), F32),),
        flops=4 * send_rows * own_rows * out_width,
        moved=send_rows * out_width * 4,
    )(own, arrived, recv)

    own_in = in_width // peers
    sums = sums.reshape(scenes, own_in, blocks, 2, LANES).transpose(1, 3, 0, 2, 4)
    sums = sums.reshape(own_in, group, blocks * LANES)[:, :, :columns]
    kernel_grad = sums.reshape(own_in, offsets, out_width)
    kernel_grad = kernel_grad.transpose(1, 0, 2).reshape(offsets, own_in * out_width)
    normalizer = 1.0 / math.sqrt(scenes * peers * own_rows)
    return (conv_out[None], input_grad[None], kernel_grad * normalizer)


def solution(mesh):
    scenes = mesh.devices.shape[1]
    fine = Mesh(mesh.devices.reshape(8, 8, 2, scenes), ("y", "z", "core", "scene"))
    voxels = P("scene", SPACE)
    return jax.shard_map(
        local,
        mesh=fine,
        in_specs=(voxels, voxels, voxels, P(), voxels, voxels, voxels),
        out_specs=(voxels, voxels, P(None, SPACE)),
        check_vma=False,
    )
```

```python
import functools
import math

import jax
import jax.numpy as jnp
from jax import lax
from jax.experimental import pallas as pl
from jax.experimental.pallas import tpu as pltpu
from jax.sharding import Mesh
from jax.sharding import PartitionSpec as P

F32 = jnp.float32
BF16 = jnp.bfloat16
I32 = jnp.int32
LANES = 128
STEP = 2
WORDS = 8
VMEM_BYTES = 24 * 1024 * 1024
MOST_VMEM = 64 * 1024 * 1024 - 128 * 1024
SPACE = ("y", "z", "core")
GROUP = ("core", "scene")


def call(kernel, outs, scratch=(), flops=0, moved=0, vmem=VMEM_BYTES, **specs):
    return pl.pallas_call(
        kernel,
        out_shape=outs,
        scratch_shapes=list(scratch),
        **specs,
        compiler_params=pltpu.CompilerParams(vmem_limit_bytes=vmem),
        cost_estimate=pl.CostEstimate(flops=flops, bytes_accessed=moved, transcendentals=0),
    )


def rows_iota(rows, start=0):
    return lax.broadcasted_iota(I32, (rows, LANES), 0) + start


def one_hot(iota, row):
    return jnp.where(iota == row, 1.0, 0.0).astype(BF16)


def one_hot_16(iota, row):
    rows = iota.shape[0]
    narrow = jnp.broadcast_to(row, (16, LANES)).astype(jnp.int16)
    narrow = jnp.concatenate([narrow] * (rows // 16), axis=0)
    return jnp.where(iota == narrow, jnp.ones((rows, LANES), BF16), jnp.zeros((rows, LANES), BF16))


def split_two(value):
    high = value.astype(BF16)
    low = (value - high.astype(F32)).astype(BF16)
    return high, low


def lane_block(k):
    return slice(k * LANES, (k + 1) * LANES)


def gather_kernel(
    cot_any, mask_any, recv_any, in_any, pair_any, shared_ref, out_ref, cot_ref, mask_ref, recv_ref, in_ref, pair_ref, digit_ref, sems, *, targets
):
    pairs = (
        (cot_any, cot_ref),
        (mask_any, mask_ref),
        (recv_any, recv_ref),
        (in_any, in_ref),
        (pair_any, pair_ref),
    )
    copies = [pltpu.make_async_copy(a, b, sems.at[i]) for i, (a, b) in enumerate(pairs)]
    for copy in copies:
        copy.start()
    digit_ref[...] = jnp.zeros_like(digit_ref)
    for copy in copies:
        copy.wait()
    up = (cot_ref[...].astype(F32) * mask_ref[...].astype(F32)).astype(BF16)
    shared_ref[0:LANES, :] = up.T
    iota = rows_iota(LANES)
    for g in range(recv_ref.shape[0]):
        hot = one_hot(iota, recv_ref[g : g + 1, :])
        rows = lax.dot_general(hot, up, (((0,), (0,)), ((), ())), preferred_element_type=F32)
        out_ref[lane_block(g), :] = rows.astype(BF16)
    picks = rows_iota(16)
    for k in range(in_ref.shape[0]):
        hot = one_hot(iota, in_ref[k])
        target = pair_ref[k]
        code = jnp.where(target < targets, target + 1, 0)
        digits = jnp.where(picks == 0, code >> 7, jnp.where(picks == 1, code & 127, 0))
        found = lax.dot_general(
            digits.astype(F32).astype(BF16), hot, (((1,), (1,)), ((), ())), preferred_element_type=F32
        )
        digit_ref[k : k + 1, :] = found[0:1]
        digit_ref[32 + k : 33 + k, :] = found[1:2]
    shared_ref[LANES : LANES + 64, :] = digit_ref[...].astype(BF16)


def table_kernel(shared_ref, table_ref, turned_ref):
    high = shared_ref[LANES : LANES + 32, :].astype(F32)
    low = shared_ref[LANES + 32 : LANES + 64, :].astype(F32)
    table_ref[...] = (high * 128.0 + low - 1.0).astype(I32)
    turned_ref[...] = shared_ref[0:LANES, :]


def lookup_kernel(turned_ref, back_ref, table_ref, gathered_any, ext_ref, hot_ref, gathered_ref, sems):
    blocks = back_ref.shape[0] // LANES
    offsets = gathered_ref.shape[0] // LANES
    ext_ref[:, 0:LANES] = turned_ref[...]
    for b in range(blocks):
        ext_ref[:, lane_block(b + 1)] = back_ref[lane_block(b), :].T
    iota = rows_iota((blocks + 1) * LANES).astype(jnp.int16)
    copies = []
    for first in range(0, offsets, STEP):
        count = min(STEP, offsets - first)
        slot = (first // STEP) % 2
        for k in range(count):
            hot_ref[slot, :, lane_block(k)] = one_hot_16(iota, table_ref[first + k : first + k + 1, :])
        rows = jnp.dot(
            ext_ref[...], hot_ref[slot, :, : count * LANES], preferred_element_type=F32
        ).astype(BF16)
        for k in range(count):
            gathered_ref[lane_block(first + k), :] = rows[:, lane_block(k)]
        part = pl.ds(first * LANES, count * LANES)
        copies.append(
            pltpu.make_async_copy(gathered_ref.at[part], gathered_any.at[part], sems.at[first // STEP])
        )
        copies[-1].start()
    for copy in copies:
        copy.wait()


def encode(value, top):
    level = jnp.ceil(jnp.log2(jnp.maximum(top, 1e-36)) * 8.0)
    code = jnp.round(value * jnp.exp2(level * -0.125) * 32767.0)
    return jnp.clip(code, -32767.0, 32767.0).astype(I32), level.astype(I32)


def unit(level):
    return jnp.exp2(level.astype(F32) * 0.125)


def join(first, second):
    return (first << 16) | (second & 0xFFFF)


def halves(word):
    scale = 1.0 / 32767.0
    return (word >> 16).astype(F32) * scale, ((word << 16) >> 16).astype(F32) * scale


def row_top(value):
    return jnp.max(jnp.abs(value), axis=1, keepdims=True)


def fetch(w_any, w_ref, gathered_any, gathered_ref, sems):
    offsets = w_ref.shape[0]
    parts = sems.shape[1]
    step = offsets // parts
    copies = []
    for i in range(parts):
        part = pl.ds(i * step, step)
        rows = pl.ds(i * step * LANES, step * LANES)
        copies.append(
            (
                pltpu.make_async_copy(w_any.at[part], w_ref.at[part], sems.at[0, i]),
                pltpu.make_async_copy(gathered_any.at[rows], gathered_ref.at[rows], sems.at[1, i]),
            )
        )
        for copy in copies[-1]:
            copy.start()
    return copies, step


def forward_kernel(
    near_ref,
    w_any,
    table_ref,
    gathered_any,
    own_any,
    word_ref,
    grad_ref,
    w_ref,
    gathered_ref,
    terms_ref,
    hot_ref,
    send_ref,
    sems,
    own_sem,
    *,
    free,
):
    offsets = w_ref.shape[0]
    copies, step = fetch(w_any, w_ref, gathered_any, gathered_ref, sems)
    total = jnp.zeros((w_ref.shape[1], LANES), F32)
    for k in range(offsets):
        if k % step == 0:
            for copy in copies[k // step]:
                copy.wait()
        high, low = split_two(jnp.dot(near_ref[0], w_ref[k], preferred_element_type=F32))
        terms_ref[lane_block(k), 0:LANES] = high
        terms_ref[lane_block(k), LANES : 2 * LANES] = low
        total += jnp.dot(w_ref[k], gathered_ref[lane_block(k), :], preferred_element_type=F32)
    grad_ref[...] = total.T.astype(BF16)
    iota = rows_iota(LANES).astype(jnp.int16)

    span = hot_ref.shape[1]
    own_rows = own_any.shape[0]
    own_copy = pltpu.make_async_copy(send_ref.at[pl.ds(0, own_rows)], own_any, own_sem)
    for i in range(send_ref.shape[0] // span):
        for j in range(span // LANES):
            for k in range(offsets):
                row = table_ref[k : k + 1, :] - (i * span + j * LANES)
                hot_ref[i % 2, lane_block(j), lane_block(k)] = one_hot_16(iota, row)
        both = jnp.dot(hot_ref[i % 2], terms_ref[...], preferred_element_type=F32)
        send_ref[pl.ds(i * span, span), :] = both[:, :LANES] + both[:, LANES:]
        if i == 0:
            own_copy.start()
    peers = word_ref.shape[1]
    lane = lax.broadcasted_iota(I32, (peers, LANES), 1)
    levels = jnp.zeros((peers, LANES), I32)
    for r in range(4):
        words = []
        for slot in (r, r + 4):
            value = send_ref[pl.ds(own_rows + slot, peers, stride=8), :]
            code, level = encode(value, row_top(value))
            words.append(code)
            levels = jnp.where(lane == free + slot, level, levels)
        word_ref[r] = join(*words)
    word_ref[4] = levels
    own_copy.wait()


def pack_kernel(g_ref, near_ref, far_ref, word_ref, out_ref, turn_ref):
    columns = g_ref.shape[1]
    peers = word_ref.shape[1]
    blocks = turn_ref.shape[0]
    scenes = near_ref.shape[0]
    core, scene = (lax.axis_index(axis) for axis in GROUP)
    total = jnp.zeros((columns, near_ref.shape[2]), F32)
    for s in range(0, g_ref.shape[0], 2):
        x_ref, holder = (near_ref, core) if s < scenes else (far_ref, 1 - core)
        senders = [holder * scenes + (scene ^ ((s + i) % scenes)) for i in range(2)]
        both = jnp.concatenate([g_ref[sender] for sender in senders], axis=1)
        first = s % scenes
        rows = x_ref[first : first + 2].reshape(both.shape[1], total.shape[1])
        total += jnp.dot(both, rows, preferred_element_type=F32)
    rest = blocks * LANES - columns
    total = jnp.concatenate([total, jnp.zeros((rest, total.shape[1]), F32)], axis=0)
    for h in range(blocks):
        turn_ref[h] = total[lane_block(h), :].T
    for r in range(4):
        out_ref[pl.ds(r, peers, stride=WORDS), :] = word_ref[r]
    parts = [[turn_ref[h, pl.ds(c, peers, stride=2), :] for c in range(2)] for h in range(blocks)]
    top = functools.reduce(jnp.maximum, [jnp.abs(part) for pair in parts for part in pair])
    top = jnp.max(top, axis=1, keepdims=True)
    free = LANES - rest
    lane = lax.broadcasted_iota(I32, (peers, LANES), 1)
    for h in range(blocks):
        codes = [encode(part, top) for part in parts[h]]
        word = join(codes[0][0], codes[1][0])
        if h == blocks - 1:
            levels = jnp.where(lane == free + 8, codes[0][1], word_ref[4])
            word = jnp.where(lane < free, word, levels)
        out_ref[pl.ds(4 + h, peers, stride=WORDS), :] = word


def sum_kernel(arrived_ref, out_ref, *, free):
    peers = arrived_ref.shape[0] // WORDS
    words = [arrived_ref[pl.ds(4 + h, peers, stride=WORDS), :] for h in range(4)]
    scale = unit(words[-1][:, free + 8 : free + 9])
    for h in range(4):
        for c, value in enumerate(halves(words[h])):
            total = (value * scale).reshape(peers // 8, 8, LANES).sum(axis=0)
            total = (total[0:2] + total[2:4]) + (total[4:6] + total[6:8])
            for core in range(2):
                row = 4 * (2 * c + core) + h
                for s in range(out_ref.shape[0]):
                    out_ref[s, row : row + 1, :] = total[core : core + 1]


def receive_kernel(own_ref, arrived_ref, recv_ref, out_ref, rows_ref, *, free):
    peers = arrived_ref.shape[0] // WORDS
    iota = rows_iota(LANES)
    levels = arrived_ref[pl.ds(WORDS - 1, peers, stride=WORDS), :]
    for r in range(4):
        pair = halves(arrived_ref[pl.ds(r, peers, stride=WORDS), :])
        for value, slot in zip(pair, (r, r + 4)):
            scale = unit(levels[:, free + slot : free + slot + 1])
            rows_ref[pl.ds(slot, peers, stride=8), :] = value * scale
    total = own_ref[...]
    for g in range(recv_ref.shape[0]):
        hot = one_hot(iota, recv_ref[g : g + 1, :])
        high, low = split_two(rows_ref[lane_block(g), :])
        total += jnp.dot(hot, high, preferred_element_type=F32)
        total += jnp.dot(hot, low, preferred_element_type=F32)
    out_ref[...] = total.astype(BF16)


def local(features, cotangent, relu_mask, weight, pair_in, pair_out, recv_index):
    x = features[0]
    own_rows, in_width = x.shape
    offsets, unused, out_width = weight.shape
    peers = lax.axis_size(SPACE)
    group = lax.axis_size(GROUP)
    scenes = lax.axis_size("scene")
    send_rows = recv_index.shape[2]
    slots = send_rows // peers
    targets = own_rows + send_rows
    columns = offsets * out_width // group
    recv = recv_index.reshape(send_rows // LANES, LANES)
    shape = jax.ShapeDtypeStruct

    hbm = pl.BlockSpec(memory_space=pltpu.HBM)
    vmem = pl.BlockSpec(memory_space=pltpu.VMEM)
    blocks = -(-columns // LANES)
    free = columns - (blocks - 1) * LANES

    lists = [pairs.reshape(offsets, 1, own_rows) for pairs in (pair_in, pair_out)]
    shared, outgoing = call(
        functools.partial(gather_kernel, targets=targets),
        (shape((out_width + 64, own_rows), BF16), shape((send_rows, out_width), BF16)),
        scratch=(
            pltpu.VMEM((own_rows, out_width), BF16),
            pltpu.VMEM((own_rows, out_width), I32),
            pltpu.VMEM(recv.shape, I32),
            pltpu.VMEM(lists[0].shape, I32),
            pltpu.VMEM(lists[1].shape, I32),
            pltpu.VMEM((64, own_rows), F32),
            pltpu.SemaphoreType.DMA((5,)),
        ),
        in_specs=[hbm] * 5,
        vmem=MOST_VMEM,
        flops=2 * send_rows * own_rows * out_width,
        moved=send_rows * out_width * 3,
    )(cotangent[0], relu_mask[0], recv, *lists)
    own_x, outgoing = lax.optimization_barrier((x, outgoing))
    returned = lax.all_to_all(outgoing.reshape(peers, slots, out_width), SPACE, 0, 0, tiled=True)

    swap = [(0, 1), (1, 0)]
    ring = [
        lax.ppermute(own_x, "scene", [(i, i ^ d) for i in range(scenes)]) for d in range(1, scenes)
    ]

    table, turned = call(
        table_kernel, (shape((32, own_rows), I32), shape((out_width, own_rows), BF16))
    )(shared)
    gathered = call(
        lookup_kernel,
        shape((offsets * out_width, own_rows), BF16),
        scratch=(
            pltpu.VMEM((out_width, targets), BF16),
            pltpu.VMEM((2, targets, STEP * LANES), BF16),
            pltpu.VMEM((offsets * out_width, own_rows), BF16),
            pltpu.SemaphoreType.DMA((-(-offsets // STEP),)),
        ),
        out_specs=hbm,
    )(turned, returned.reshape(send_rows, out_width), table)
    gathered, *ring = lax.optimization_barrier((gathered, *ring))
    group_g = lax.all_to_all(gathered.reshape(group, columns, own_rows), GROUP, 0, 0, tiled=True)

    near = jnp.stack([x] + ring)
    own, words, input_grad = call(
        functools.partial(forward_kernel, free=free),
        (
            shape((own_rows, out_width), F32),
            shape((5, peers, out_width), I32),
            shape((own_rows, in_width), BF16),
        ),
        scratch=(
            pltpu.VMEM(weight.shape, BF16),
            pltpu.VMEM((offsets * out_width, own_rows), BF16),
            pltpu.VMEM((offsets * own_rows, 2 * out_width), BF16),
            pltpu.VMEM((2, targets // 3, offsets * own_rows), BF16),
            pltpu.VMEM((targets, out_width), F32),
            pltpu.SemaphoreType.DMA((2, 3)),
            pltpu.SemaphoreType.DMA,
        ),
        in_specs=[vmem, hbm, vmem, hbm],
        out_specs=(hbm, vmem, vmem),
    )(near, weight, table, gathered)

    far = lax.ppermute(near, "core", swap)
    packed = call(
        pack_kernel,
        shape((peers * WORDS, LANES), I32),
        scratch=(pltpu.VMEM((blocks, in_width, LANES), F32),),
        flops=2 * columns * in_width * own_rows * group,
        moved=peers * WORDS * LANES * 8,
    )(group_g, near, far, words)
    arrived = lax.all_to_all(packed.reshape(peers, WORDS, LANES), SPACE, 0, 0, tiled=True)
    arrived = arrived.reshape(peers * WORDS, LANES)

    quarter = call(
        functools.partial(sum_kernel, free=free),
        shape((scenes, 16, LANES), F32),
        moved=peers * WORDS * LANES * 4,
    )(arrived)
    sums = lax.all_to_all(quarter, "scene", 0, 0, tiled=True)
    conv_out = call(
        functools.partial(receive_kernel, free=free),
        shape((own_rows, out_width), BF16),
        scratch=(pltpu.VMEM((send_rows, out_width), F32),),
        flops=4 * send_rows * own_rows * out_width,
        moved=send_rows * out_width * 4,
    )(own, arrived, recv)

    own_in = in_width // peers
    sums = sums.reshape(scenes, own_in, 2, blocks, LANES).transpose(1, 2, 0, 3, 4)
    sums = sums.reshape(own_in, group, blocks * LANES)[:, :, :columns]
    kernel_grad = sums.reshape(own_in, offsets, out_width)
    kernel_grad = jnp.concatenate([kernel_grad[c] for c in range(own_in)], axis=1)
    normalizer = 1.0 / math.sqrt(scenes * peers * own_rows)
    return (conv_out[None], input_grad[None], kernel_grad * normalizer)


def solution(mesh):
    scenes = mesh.devices.shape[1]
    fine = Mesh(mesh.devices.reshape(8, 8, 2, scenes), ("y", "z", "core", "scene"))
    voxels = P("scene", SPACE)
    return jax.shard_map(
        local,
        mesh=fine,
        in_specs=(voxels, voxels, voxels, P(), voxels, voxels, voxels),
        out_specs=(voxels, voxels, P(None, SPACE)),
        check_vma=False,
    )
```
